32 devices in a mesh: ctx: 16 (over z, x, core), fsdp: 2 (over y).
Axes of the slice: x: 2, y: 2, z: 4, core: 2. Of those that a mesh axis runs over, the one named last changes fastest.
Arguments:
- inputs: bfloat16 [2, 4096, 1024], P('fsdp', 'ctx'), may hold values from -6 to 6
- cotangent: bfloat16 [2, 4096, 1024], P('fsdp', 'ctx'), may hold values from -6 to 6
- lengths: int32 [2, 8], P('fsdp'), may hold values from 1 to 2048, 4096 in all within a row
- gain_one: float32 [1024], replicated, may hold values from 0.25 to 1.75
- gain_two: float32 [1024], replicated, may hold values from 0.25 to 1.75
- query_gain: float32 [64], replicated, may hold values from 0.25 to 1.75
- key_norm_gain: float32 [64], replicated, may hold values from 0.25 to 1.75
- w_query: float32 [1024, 1024], P(None, 'fsdp'), may hold values from -0.1875 to 0.1875
- key_projection: float32 [1024, 512], P(None, 'fsdp'), may hold values from -0.1875 to 0.1875
- value_projection: float32 [1024, 512], P(None, 'fsdp'), may hold values from -0.1875 to 0.1875
- w_out: float32 [1024, 1024], P(None, 'fsdp'), may hold values from -3 to 3
- w_gate: float32 [1024, 4608], P(None, 'fsdp'), may hold values from -0.1875 to 0.1875
- w_up: float32 [1024, 4608], P(None, 'fsdp'), may hold values from -0.1875 to 0.1875
- w_down: float32 [1024, 4608], P(None, 'fsdp'), may hold values from -0.09375 to 0.09375
Outputs:
- block_out: bfloat16 [2, 4096, 1024], P('fsdp', 'ctx')
- grad_inputs: bfloat16 [2, 4096, 1024], P('fsdp', 'ctx')
- grad_gain_one: float32 [1024], replicated
- grad_gain_two: float32 [1024], replicated
- grad_query_gain: float32 [64], replicated
- grad_key_gain: float32 [64], replicated
- grad_w_query: float32 [1024, 1024], P('ctx', 'fsdp')
- grad_w_key: float32 [1024, 512], P('ctx', 'fsdp')
- grad_w_value: float32 [1024, 512], P('ctx', 'fsdp')
- grad_w_out: float32 [1024, 1024], P('ctx', 'fsdp')
- grad_w_gate: float32 [1024, 4608], P('ctx', 'fsdp')
- grad_w_up: float32 [1024, 4608], P('ctx', 'fsdp')
- grad_w_down: float32 [1024, 4608], P('ctx', 'fsdp')
The draws below stay inside these ranges and needn't reach their ends.
Inputs may be any that keep to these rules, and one draw needn't show every extreme that they name: `lengths`: each row sums to 4096; its longest sequence has exactly 2048 tokens.
All inputs are finite; a program needn't handle non-finite values.
Results may differ from the reference program's by a relative error of at most 0.02.
Values may be sent and summed in bfloat16 or wider, within the bound.
A program may use at most 256 MiB of HBM per device.

```python
import math
import jax
import jax.numpy as jnp
import numpy as np
from jax import lax

MODEL_WIDTH = 1024
QUERY_HEADS = 16
KEY_VALUE_HEADS = 8
HEAD_SIZE = 64
FF = 4608
NSEQ = 8
GROUP = 4096
SEQ_MAX = 2048
N_FSDP = 2


def block_levels(key, shape, shards, smallest, largest):
    level = 1.0
    for position, shards_of in shards:
        steps = jax.random.uniform(jax.random.fold_in(jax.random.fold_in(key, 6), position), (shards_of,), jnp.float32, smallest / len(shards), largest / len(shards))
        level = level * jnp.repeat(jnp.exp(steps), shape[position] // shards_of).reshape((-1,) + (1,) * (len(shape) - 1 - position))
    return level


def split_up(number_of, total, limit, lean):
    loads = [(1 << 20) // math.isqrt(rank ** lean) + 1 for rank in range(2, number_of + 1)]
    rest, holding = total - limit - (number_of - 1), [1] * (number_of - 1)
    while rest > 0:
        free = [i for i in range(number_of - 1) if holding[i] < limit]
        whole, left = sum([loads[i] for i in free]), rest
        for i in free:
            addition = min(limit - holding[i], max(1, left * loads[i] // whole), rest)
            holding[i] = holding[i] + addition
            rest = rest - addition
    return np.array([limit] + holding)


def uneven(rng, amount, total, bound, lean):
    if amount == 2:
        one = jax.random.randint(rng, (), max(1, total - bound), min(bound, total - 1) + 1)
        return jnp.stack([one, total - one])
    sizes = jnp.asarray(split_up(amount, total, bound, lean), jnp.int32)
    couples = (amount - 1) // 2
    source_of, taker = sizes[1:1 + 2 * couples:2], sizes[2:2 + 2 * couples:2]
    slack = jnp.minimum(source_of - 1, bound - taker)
    shifted = jax.random.randint(jax.random.fold_in(rng, 1), (couples,), 0, 1 << 20) % (slack + 1)
    sizes = sizes.at[1:1 + 2 * couples:2].set(source_of - shifted).at[2:2 + 2 * couples:2].set(taker + shifted)
    return sizes[jax.random.permutation(jax.random.fold_in(rng, 2), amount)]


def normal_values(own_key, shape, scale, most, cuts=(), kind=jnp.bfloat16):
    level = block_levels(own_key, shape, cuts, -0.22, 0.18) if cuts else 1.0
    values = jax.random.normal(own_key, shape, jnp.float32) * scale * level
    return jnp.minimum(jnp.maximum(values, -most), most).astype(kind)


def setup_inputs(seed: int = 0) -> dict:
    keys = jax.random.split(jax.random.key(seed), 15)
    return {
        "inputs": normal_values(keys[0], (N_FSDP, GROUP, MODEL_WIDTH), 1.0, 6.0, ((0, 2), (1, 16))),
        "cotangent": normal_values(keys[1], (N_FSDP, GROUP, MODEL_WIDTH), 1.0, 6.0, ((0, 2), (1, 16))),
        "lengths": jax.vmap(lambda own: uneven(own, NSEQ, GROUP, SEQ_MAX, 2))(jax.random.split(keys[2], N_FSDP)).reshape((N_FSDP, NSEQ)).astype(jnp.int32),
        "gain_one": jnp.clip(1.0 + 0.15 * jax.random.normal(keys[3], (MODEL_WIDTH,), jnp.float32), 0.25, 1.75),
        "gain_two": jnp.clip(1.0 + 0.15 * jax.random.normal(keys[4], (MODEL_WIDTH,), jnp.float32), 0.25, 1.75),
        "query_gain": jnp.clip(1.0 + 0.15 * jax.random.normal(keys[5], (HEAD_SIZE,), jnp.float32), 0.25, 1.75),
        "key_norm_gain": jnp.clip(1.0 + 0.15 * jax.random.normal(keys[6], (HEAD_SIZE,), jnp.float32), 0.25, 1.75),
        "w_query": normal_values(keys[7], (MODEL_WIDTH, QUERY_HEADS * HEAD_SIZE), MODEL_WIDTH ** -0.5, 0.1875, ((1, 2),), jnp.float32),
        "key_projection": normal_values(keys[8], (MODEL_WIDTH, KEY_VALUE_HEADS * HEAD_SIZE), MODEL_WIDTH ** -0.5, 0.1875, ((1, 2),), jnp.float32),
        "value_projection": normal_values(keys[9], (MODEL_WIDTH, KEY_VALUE_HEADS * HEAD_SIZE), MODEL_WIDTH ** -0.5, 0.1875, ((1, 2),), jnp.float32),
        "w_out": normal_values(keys[10], (MODEL_WIDTH, QUERY_HEADS * HEAD_SIZE), (max(QUERY_HEADS * HEAD_SIZE // 256, 1)) ** -0.5, 3.0, ((1, 2),), jnp.float32),
        "w_gate": normal_values(keys[11], (MODEL_WIDTH, FF), MODEL_WIDTH ** -0.5, 0.1875, ((1, 2),), jnp.float32),
        "w_up": normal_values(keys[12], (MODEL_WIDTH, FF), MODEL_WIDTH ** -0.5, 0.1875, ((1, 2),), jnp.float32),
        "w_down": normal_values(keys[13], (MODEL_WIDTH, FF), FF ** -0.5, 0.09375, ((1, 2),), jnp.float32),
    }


@jax.custom_vjp
def lower_precision(v):
    return lax.optimization_barrier(v.astype(jnp.bfloat16)).astype(jnp.float32)

@jax.custom_vjp
def lower_precision_backward(v):
    return v

def low_keep(v):
    return (lower_precision(v), None)

def low_pass(kept, grad):
    return (grad,)

def back_keep(v):
    return (v, None)

def back_low(kept, grad):
    return (lower_precision(grad),)
lower_precision.defvjp(low_keep, low_pass)
lower_precision_backward.defvjp(back_keep, back_low)
EPS = 1e-05
THETA = 1000000.0
MASKED_FILL = -1e+30
HIGH = lax.Precision.HIGHEST

def matrix_product(left, right):
    return jnp.dot(left, right, precision=HIGH)

def root_mean_norm(values, gain):
    return values * lax.rsqrt(lax.optimization_barrier(jnp.mean(values * values, axis=-1, keepdims=True)) + EPS) * gain

def apply_rotary(values, cosine_table, sine_table):
    half_width = values.shape[-1] // 2
    turned = jnp.concatenate([-values[..., half_width:], values[..., :half_width]], axis=-1)
    return values * cosine_table + turned * sine_table

def places(lengths, where):
    ends = jnp.cumsum(lengths).astype(jnp.int32)
    before = (ends[None, :] <= where[:, None]).astype(jnp.int32)
    segment = lax.optimization_barrier(jnp.sum(before, axis=1)).astype(jnp.int32)
    offset = where - lax.optimization_barrier(jnp.sum(before * lengths[None, :], axis=1)).astype(jnp.int32)
    return (segment, offset)

def attention(query_rows, key, value_rows, segment):
    token_count = query_rows.shape[0]
    input_rows = min(512, token_count)
    shared_heads = QUERY_HEADS // KEY_VALUE_HEADS
    where = jnp.arange(token_count, dtype=jnp.int32)
    scale = 1.0 / math.sqrt(HEAD_SIZE)
    blocked_queries = query_rows.reshape(token_count // input_rows, input_rows, KEY_VALUE_HEADS, shared_heads, HEAD_SIZE)
    segment_blocks = segment.reshape(token_count // input_rows, input_rows)
    where_blocks = where.reshape(token_count // input_rows, input_rows)

    def block(pieces):
        query_block, segment_block, where_block = pieces
        scores = jnp.einsum('qhgd,khd->hgqk', query_block, key, precision=HIGH) * scale
        scores = lower_precision_backward(scores)
        allowed = (segment_block[:, None] == segment[None, :]) & (where_block[:, None] >= where[None, :])
        scores = jnp.where(allowed[None, None], scores, MASKED_FILL)
        weights = lower_precision(jax.nn.softmax(scores, axis=-1))
        result = jnp.einsum('hgqk,khd->qhgd', weights, value_rows, precision=HIGH)
        return result.reshape(input_rows, QUERY_HEADS * HEAD_SIZE)
    results = lax.map(jax.checkpoint(block), (blocked_queries, segment_blocks, where_blocks))
    return results.reshape(token_count, QUERY_HEADS * HEAD_SIZE)

def group_forward(inputs, lengths, params):
    gain_one, gain_two, query_gain, key_norm_gain, w_query, key_projection, value_projection, w_out, w_gate, w_up, w_down = params
    token_count = inputs.shape[0]
    where = jnp.arange(token_count, dtype=jnp.int32)
    segment, offset = places(lengths, where)
    freq = jnp.exp(jnp.arange(HEAD_SIZE // 2, dtype=jnp.float32) * (-2.0 * math.log(THETA) / HEAD_SIZE))
    angle = offset.astype(jnp.float32)[:, None] * freq[None, :]
    cosine_table = jnp.concatenate([jnp.cos(angle), jnp.cos(angle)], axis=-1)[:, None, :]
    sine_table = jnp.concatenate([jnp.sin(angle), jnp.sin(angle)], axis=-1)[:, None, :]
    normed_input = lower_precision(root_mean_norm(inputs, gain_one))
    query_raw = lower_precision_backward(matrix_product(normed_input, w_query)).reshape(token_count, QUERY_HEADS, HEAD_SIZE)
    unrotated_key = lower_precision_backward(matrix_product(normed_input, key_projection)).reshape(token_count, KEY_VALUE_HEADS, HEAD_SIZE)
    value_rows = lower_precision(lower_precision_backward(matrix_product(normed_input, value_projection))).reshape(token_count, KEY_VALUE_HEADS, HEAD_SIZE)
    query_rows = lower_precision(lower_precision_backward(apply_rotary(root_mean_norm(query_raw, query_gain), cosine_table, sine_table)))
    key = lower_precision(lower_precision_backward(apply_rotary(root_mean_norm(unrotated_key, key_norm_gain), cosine_table, sine_table)))
    heads = attention(query_rows, key, value_rows, segment)
    mixed = lower_precision(lower_precision_backward(heads))
    branch = lower_precision_backward(matrix_product(mixed, w_out.T))
    middle = inputs + branch
    normed_two = lower_precision(root_mean_norm(middle, gain_two))
    gate = lower_precision_backward(matrix_product(normed_two, w_gate))
    upward = lower_precision_backward(matrix_product(normed_two, w_up))
    hidden = lower_precision(jax.nn.silu(gate) * upward)
    return middle + matrix_product(hidden, w_down.T)

def reference(inputs, cotangent, lengths, gain_one, gain_two, query_gain, key_norm_gain, w_query, key_projection, value_projection, w_out, w_gate, w_up, w_down):
    params = tuple((value_rows.astype(jnp.float32) for value_rows in (gain_one, gain_two, query_gain, key_norm_gain, w_query, key_projection, value_projection, w_out, w_gate, w_up, w_down)))

    def forward(all_inputs, all_params):
        rounded = tuple((lower_precision(weight) for weight in all_params[4:]))
        full_result = tuple(all_params[:4]) + rounded
        results = []
        for group_index in range(N_FSDP):
            results.append(group_forward(all_inputs[group_index], lengths[group_index], full_result))
        return jnp.stack(results)
    floats = inputs.astype(jnp.float32)
    result, pullback = jax.vjp(forward, floats, params)
    grad_floats, grad_params = pullback(cotangent.astype(jnp.float32))
    return (result.astype(jnp.bfloat16), grad_floats.astype(jnp.bfloat16), grad_params[0], grad_params[1], grad_params[2], grad_params[3], grad_params[4], grad_params[5], grad_params[6], grad_params[7], grad_params[8], grad_params[9], grad_params[10])
```

```python
import functools
import math

import jax
import jax.numpy as jnp
import numpy as np
from jax import lax
from jax.experimental import pallas as pl
from jax.experimental.pallas import tpu as pltpu
from jax.sharding import PartitionSpec as P

MESH = pl.DeviceIdType.MESH
BF16, F32 = jnp.bfloat16, jnp.float32
HEAD = 64
TILE = 256
EPS = 1e-05
THETA = 1000000.0
PLANES = 4
WINDOW = 3
EXP2_SCALE = math.log2(math.e) / math.sqrt(HEAD)


def nt_dot(left, right):
    return lax.dot_general(left, right, (((1,), (1,)), ((), ())), preferred_element_type=F32)


def dot(left, right):
    return jnp.dot(left, right, preferred_element_type=F32)


class Plan:
    def __init__(self, ctx, groups, rows, width, kv_heads, ff):
        self.A, self.B, self.G = PLANES, ctx // (2 * PLANES), groups
        self.R, self.D, self.KV, self.FL = rows, width, kv_heads, ff
        self.S = width // ctx
        self.nt = ff // TILE
        self.HQ = 128 * kv_heads
        self.no = self.HQ // TILE
        self.tiles = 3 * self.nt + self.no + kv_heads
        self.gate, self.up, self.down, self.out = 0, self.nt, 2 * self.nt, 3 * self.nt
        self.qkv = self.out + self.no
        self.batches = []
        for first, count, step in ((0, 3 * self.nt, 3), (self.out, self.no, 2), (self.qkv, kv_heads, 2)):
            self.batches += [(t, min(step, first + count - t)) for t in range(first, first + count, step)]
        self.ff_batches = -(-3 * self.nt // 3)

    def fits(self):
        rows = self.G * self.R
        weights = 2 * self.tiles * self.D * TILE
        keys = 2 * WINDOW * 2 * self.B * self.G * self.KV * self.R * 128
        activations = 2 * rows * (13 * self.D + 3 * self.FL)
        even = self.FL % TILE == 0 and self.HQ % TILE == 0 and self.R % 128 == 0
        return even and weights + keys + activations < 45 << 20


def rotate(u, cos, sin):
    low, high = u[:, :32], u[:, 32:]
    return jnp.concatenate([low * cos - high * sin, high * cos + low * sin], axis=1)


def rotate_back(u, cos, sin):
    low, high = u[:, :32], u[:, 32:]
    return jnp.concatenate([low * cos + high * sin, high * cos - low * sin], axis=1)


AG_X, AG_AUX, AG_DY, AG_N2, AG_GB, RS_P, RS_FO, RS_GN2, RS_GN = range(9)


def kernel(p, names, *refs):
    r = dict(zip(names, refs))
    A, B, G, R, D, KV, S = p.A, p.B, p.G, p.R, p.D, p.KV, p.S
    i, f = lax.axis_index("ctx"), lax.axis_index("fsdp")
    c = lax.rem(i, 2)
    b = lax.rem(i // 2, B)
    a = i // (2 * B)
    place = 2 * b + c
    others = range(1, G)

    def at(aa, bb, cc):
        return ((aa * B + bb) * 2 + cc, f)

    def group_device(k):
        return (i, lax.rem(f + k, G))

    def remote(src, dst, send, recv, device):
        return pltpu.make_async_remote_copy(
            src_ref=src, dst_ref=dst, send_sem=send, recv_sem=recv, device_id=device, device_id_type=MESH
        )

    sibling = at(a, b, 1 - c)

    peers = [sibling]
    peers += [at(a, lax.rem(b + k, B), c) for k in range(1, B)]
    peers += [at(lax.rem(a + k, A), b, c) for k in range(1, A)]
    peers += [group_device(k) for k in others]
    barrier = pltpu.get_barrier_semaphore()
    for peer in peers:
        pl.semaphore_signal(barrier, inc=1, device_id=peer, device_id_type=MESH)

    y_sems = r["y_sems"]

    def gather(kind, buffer, k):
        return remote(buffer.at[0], buffer.at[G - k], y_sems.at[kind, 0, k], y_sems.at[kind, 1, G - k], group_device(k))

    def gathered(kind, buffer, k):
        return remote(buffer.at[k], buffer.at[k], y_sems.at[kind, 0, k], y_sems.at[kind, 1, k], group_device(k))

    def scatter(kind, send, recv, k):
        return remote(send.at[k], recv.at[G - k], y_sems.at[kind, 0, k], y_sems.at[kind, 1, G - k], group_device(k))

    def scattered(kind, send, recv, k):
        return remote(send.at[k], recv.at[k], y_sems.at[kind, 0, k], y_sems.at[kind, 1, k], group_device(k))

    x_all, aux, dy_all = r["x_all"], r["aux"], r["dy_all"]
    local_sems = r["local_sems"]
    own_x = pltpu.make_async_copy(r["x"].at[0], x_all.at[0], local_sems.at[0])
    own_dy = pltpu.make_async_copy(r["dy"].at[0], dy_all.at[0], local_sems.at[1])
    own_x.start()
    own_dy.start()

    where = i * R + lax.broadcasted_iota(jnp.int32, (8, R), 1)
    start = jnp.zeros((8, R), jnp.int32)
    end = jnp.int32(0)
    for j in range(p.nseq):
        end = end + r["lengths"][0, j]
        start = jnp.where(where >= end, end, start)
    offset = (where - start).astype(F32)
    angle = offset[0:1] * r["freq"][...]
    aux[0, 0:32] = jnp.cos(angle)
    aux[0, 32:64] = jnp.sin(angle)
    aux[0, 64:72] = start.astype(F32)
    gains = r["head_gains"][...]
    gain_columns = jnp.transpose(jnp.broadcast_to(gains, (128, 128)))
    r["gain_columns"][...] = gain_columns

    pl.semaphore_wait(barrier, len(peers))
    own_x.wait()
    for k in others:
        gather(AG_X, x_all, k).start()
        gather(AG_AUX, aux, k).start()
    own_dy.wait()
    for k in others:
        gather(AG_DY, dy_all, k).start()

    kvw = r["kvw"]
    z_sems, x_sems, c_sems = r["z_sems"], r["x_sems"], r["c_sems"]
    wall = r["wall"]

    def weight(t):
        return wall[t].reshape(D, TILE)

    def weight_rows(t, aa):
        return wall[t, aa].reshape(D // A, TILE)

    n_t = r["n_t"]
    raws, q_t, o_acc = r["raws"], r["q_t"], r["o_acc"]

    def z_copy(d, k):
        return remote(kvw.at[d - 1, place, k], kvw.at[d, place, k], z_sems.at[0, d - 1, k], z_sems.at[1, d - 1, k], at(lax.rem(a + 1, A), b, c))

    def x_copy(d, shift, k):
        return remote(kvw.at[d, place, k], kvw.at[d, place, k], x_sems.at[0, d, shift, k], x_sems.at[1, d, shift, k], at(a, lax.rem(b + shift, B), c))

    def x_arrival(d, shift, k):
        other = lax.rem(b + B - shift, B)
        slot = kvw.at[d, 2 * other + c, k]
        return remote(slot, slot, x_sems.at[0, d, shift, k], x_sems.at[1, d, shift, k], at(a, other, c))

    def c_copy(d, column, k):
        slot = kvw.at[d, 2 * column + c, k]
        return remote(slot, slot, c_sems.at[0, d, column, k], c_sems.at[1, d, column, k], sibling)

    def c_arrival(d, column, k):
        slot = kvw.at[d, 2 * column + 1 - c, k]
        return remote(slot, slot, c_sems.at[0, d, column, k], c_sems.at[1, d, column, k], sibling)

    def x_needed(d, source, target):
        if d == 0:
            return target > source
        if d == 1:
            return target >= 0
        return target < source

    def c_needed(d, column, core):
        if d == 0:
            return jnp.logical_or(column < b, jnp.logical_and(column == b, core == 0))
        if d == 1:
            return column >= 0
        return jnp.logical_or(column > b, jnp.logical_and(column == b, core == 1))

    def when_all(*conditions):
        whole = conditions[0]
        for condition in conditions[1:]:
            whole = jnp.logical_and(whole, condition)
        return pl.when(whole)

    def spread(d, k):
        if d + 1 < WINDOW:
            @when_all(a + 1 < A, a >= d)
            def _():
                z_copy(d + 1, k).start()
        for shift in range(1, B):
            @when_all(a >= d, x_needed(d, b, lax.rem(b + shift, B)))
            def _():
                x_copy(d, shift, k).start()
        @when_all(a >= d, c_needed(d, b, c))
        def _():
            c_copy(d, b, k).start()

    def from_plane(d, k):
        @pl.when(a >= d)
        def _():
            z_arrival(d, k).wait_recv()
        spread(d, k)

    def z_arrival(d, k):
        slot = kvw.at[d, place, k]
        return remote(slot, slot, z_sems.at[0, d - 1, k], z_sems.at[1, d - 1, k], at(lax.rem(a + A - 1, A), b, c))

    def from_columns(d, k):
        for shift in range(1, B):
            other = lax.rem(b + B - shift, B)
            @when_all(a >= d, x_needed(d, other, b))
            def _():
                x_arrival(d, shift, k).wait_recv()
                c_copy(d, other, k).start()

    def from_sibling(d, k):
        def step(column, _):
            @when_all(a >= d, c_needed(d, column, 1 - c))
            def _():
                c_arrival(d, column, k).wait_recv()
            return 0
        lax.fori_loop(0, B, step, 0)

    def all_sent(k):
        for d in range(WINDOW):
            if d + 1 < WINDOW:
                @when_all(a + 1 < A, a >= d)
                def _():
                    z_copy(d + 1, k).wait_send()
            for shift in range(1, B):
                @when_all(a >= d, x_needed(d, b, lax.rem(b + shift, B)))
                def _():
                    x_copy(d, shift, k).wait_send()
            def step(column, _):
                @when_all(a >= d, c_needed(d, column, c))
                def _():
                    c_copy(d, column, k).wait_send()
                return 0
            lax.fori_loop(0, B, step, 0)

    def project(k):
        for piece in range(R // 128):
            rows = pl.ds(piece * 128, 128)
            x = x_all[k, rows].astype(F32)
            n = x * lax.rsqrt(jnp.mean(x * x, axis=1, keepdims=True) + EPS) * r["gain_one"][...]
            r["n_rows"][rows] = n.astype(BF16)
            n_t[:, k * R + piece * 128:k * R + (piece + 1) * 128] = jnp.transpose(n).astype(BF16)
        cos, sin = aux[k, 0:32], aux[k, 32:64]
        q_gain, k_gain = r["gain_columns"][0:64, 0:1], r["gain_columns"][64:128, 0:1]
        for h in range(KV):
            raw = jnp.transpose(dot(r["n_rows"][...], weight(p.qkv + h)))
            raws[k, h] = raw[0:192]
            q = raw[0:128].reshape(2, HEAD, R)
            q = q * lax.rsqrt(jnp.mean(q * q, axis=1, keepdims=True) + EPS) * q_gain
            q = rotate(q, cos, sin).astype(BF16)
            q_t[k, h, 0:64, 0:R] = q[0]
            q_t[k, h, 0:64, R:2 * R] = q[1]
            q_t[k, h, 64:128] = jnp.zeros((64, 2 * R), BF16)
            key = raw[128:192].reshape(1, HEAD, R)
            key = key * lax.rsqrt(jnp.mean(key * key, axis=1, keepdims=True) + EPS) * k_gain
            key = rotate(key, cos, sin).reshape(HEAD, R)
            kv = jnp.concatenate([key, raw[192:256]], axis=0)
            kvw[0, place, k, h] = jnp.transpose(kv).astype(BF16)

    def mask_of(k, key_start, diagonal):
        keys = lax.broadcasted_iota(jnp.int32, (R, 2 * R), 0)
        start = jnp.concatenate([aux[k, 64:65], aux[k, 64:65]], axis=1)
        allowed = (keys + key_start).astype(F32) >= start
        if diagonal:
            query = lax.broadcasted_iota(jnp.int32, (R, 2 * R), 1)
            query = jnp.where(query >= R, query - R, query)
            allowed = jnp.logical_and(allowed, keys <= query)
        return allowed

    def attend(d, other, k, diagonal=False):
        key_start = ((a - d) * 2 * B + other) * R
        allowed = mask_of(k, key_start, diagonal)
        for h in range(KV):
            kv = kvw[d, other, k, h]
            scores = dot(kv, q_t[k, h])
            weights = jnp.where(allowed, jnp.exp2(scores * EXP2_SCALE), 0.0).astype(BF16)
            values = jnp.concatenate([jnp.transpose(kv)[64:128], jnp.ones((16, R), BF16)], axis=0)
            added = dot(values, weights)
            if diagonal:
                o_acc[k, h] = added
            else:
                o_acc[k, h] += added

    def attended(d):
        if d == 0:
            return 0, place
        if d == 1:
            return 0, jnp.where(a >= 1, 2 * B, 0)
        return place, jnp.where(a >= 2, 2 * B, 0)

    def attend_plane(d, k):
        low, high = attended(d)
        def step(other, _):
            attend(d, other, k)
            return 0
        lax.fori_loop(low, high, step, 0)

    def forward_scope(s_q, s_k, s_v, s_o, stage, stage_sems):
        loads = [
            pltpu.make_async_copy(r[name], s, local_sems.at[2 + j])
            for j, (name, s) in enumerate((("w_query", s_q), ("w_key", s_k), ("w_value", s_v), ("w_out", s_o)))
        ]
        for load in loads:
            load.start()
        def ff_load(name, step):
            rows = pl.ds(step * 2 * S, 2 * S)
            return pltpu.make_async_copy(r[name].at[rows], stage.at[lax.rem(step, 2)], stage_sems.at[lax.rem(step, 2)])

        def cast_ff(name, first):
            ff_load(name, 0).start()
            def step(n, _):
                @pl.when(n + 1 < A * B)
                def _():
                    ff_load(name, n + 1).start()
                ff_load(name, n).wait()
                for t in range(p.nt):
                    part = stage[lax.rem(n, 2), :, t * TILE:(t + 1) * TILE]
                    wall[first + t, n // B, lax.rem(n, B)] = part.astype(BF16).reshape(2, S, TILE)
                return 0
            lax.fori_loop(0, A * B, step, 0)

        for load in loads[:3]:
            load.wait()
        def cast_qkv(aa, _):
            rows = pl.ds(aa * (D // A), D // A)
            for h in range(KV):
                whole = jnp.concatenate(
                    [s_q[rows, 128 * h:128 * h + 128], s_k[rows, 64 * h:64 * h + 64], s_v[rows, 64 * h:64 * h + 64]], axis=1
                ).astype(BF16)
                wall[p.qkv + h, aa] = whole.reshape(B, 2, S, TILE)
            return 0
        lax.fori_loop(0, A, cast_qkv, 0)
        project(0)
        spread(0, 0)
        attend(0, place, 0, True)
        loads[3].wait()
        def cast_out(aa, _):
            rows = pl.ds(aa * (D // A), D // A)
            for t in range(p.no):
                wall[p.out + t, aa] = s_o[rows, TILE * t:TILE * (t + 1)].astype(BF16).reshape(B, 2, S, TILE)
            return 0
        lax.fori_loop(0, A, cast_out, 0)
        cast_ff("w_gate", p.gate)
        for k in others:
            gathered(AG_X, x_all, k).wait_recv()
            gathered(AG_AUX, aux, k).wait_recv()
            project(k)
            spread(0, k)
        from_columns(0, 0)
        from_plane(1, 0)
        for k in others:
            attend(0, place, k, True)
        cast_ff("w_up", p.up)
        from_columns(1, 0)
        from_sibling(0, 0)
        attend_plane(0, 0)
        for k in others:
            from_columns(0, k)
            from_plane(1, k)
        from_plane(2, 0)
        cast_ff("w_down", p.down)
        from_sibling(1, 0)
        attend_plane(1, 0)
        for k in others:
            from_columns(1, k)
        from_columns(2, 0)
        from_sibling(2, 0)
        attend_plane(2, 0)
        for k in others:
            from_sibling(0, k)
            attend_plane(0, k)
            from_plane(2, k)
            from_sibling(1, k)
            attend_plane(1, k)
            from_columns(2, k)
            from_sibling(2, k)
            attend_plane(2, k)
        for k in range(G):
            all_sent(k)

    pl.run_scoped(
        forward_scope,
        pltpu.VMEM((D, 128 * KV), F32),
        pltpu.VMEM((D, 64 * KV), F32),
        pltpu.VMEM((D, 64 * KV), F32),
        pltpu.VMEM((D, 128 * KV), F32),
        pltpu.VMEM((2, 2 * S, p.FL), F32),
        pltpu.SemaphoreType.DMA((2,)),
    )
    for k in others:
        gather(AG_X, x_all, k).wait_send()
        gather(AG_AUX, aux, k).wait_send()

    mixed = r["mixed"]
    for k in range(G):
        for h in range(KV):
            o = o_acc[k, h]
            o_n = o[0:64] / o[64:65]
            o_acc[k, h, 0:64] = o_n
            both = jnp.concatenate([o_n[:, 0:R], o_n[:, R:2 * R]], axis=0)
            mixed[k, :, 128 * h:128 * h + 128] = jnp.transpose(both).astype(BF16)

    y_send, y_recv, fo_send, fo_recv = r["y_send"], r["y_recv"], r["fo_send"], r["fo_recv"]
    part, out_acc, middle = r["part"], r["out_acc"], r["middle"]
    n2_all, gb_all = r["n2_all"], r["gb_all"]
    gains = r["gains"]

    def store_part(k, send, own, aa, value):
        columns = slice(aa * (D // A), (aa + 1) * (D // A))
        if k == 0:
            own[:, columns] = value
        else:
            send[k, :, columns] = value.astype(BF16)

    def project_out(k):
        for aa in range(A):
            total = nt_dot(mixed[k, :, 0:TILE], weight_rows(p.out, aa))
            for t in range(1, p.no):
                total += nt_dot(mixed[k, :, t * TILE:(t + 1) * TILE], weight_rows(p.out + t, aa))
            store_part(k, y_send, part, aa, total)

    for k in others:
        project_out(k)
        scatter(RS_P, y_send, y_recv, k).start()
    project_out(0)

    rc, rx, rz = r["rc"], r["rx"], r["rz"]
    w_sems = r["w_sems"]
    stage_c, stage_x, stage_z = r["stage_c"], r["stage_x"], r["stage_z"]
    fetch_sems = r["fetch_sems"]

    def sum_core(n):
        t, m = p.batches[n]
        return remote(wall.at[pl.ds(t, m), :, :, 1 - c], rc.at[pl.ds(t, m)], w_sems.at[0, 0, n], w_sems.at[1, 0, n], sibling)

    def sum_columns(n, shift):
        t, m = p.batches[n]
        target = lax.rem(b + shift, B)
        return remote(wall.at[pl.ds(t, m), :, target, c], rx.at[shift - 1, pl.ds(t, m)], w_sems.at[0, shift, n], w_sems.at[1, shift, n], at(a, target, c))

    def sum_planes(n, shift):
        t, m = p.batches[n]
        target = lax.rem(a + shift, A)
        j = B - 1 + shift
        return remote(wall.at[pl.ds(t, m), target, b, c], rz.at[shift - 1, pl.ds(t, m)], w_sems.at[0, j, n], w_sems.at[1, j, n], at(target, b, c))

    def fetch_core(n):
        t, m = p.batches[n]
        return pltpu.make_async_copy(rc.at[pl.ds(t, m)], stage_c.at[n % 2, pl.ds(0, m)], fetch_sems.at[0, n % 2])

    def fetch_columns(n):
        t, m = p.batches[n]
        return pltpu.make_async_copy(rx.at[:, pl.ds(t, m)], stage_x.at[:, pl.ds(0, m)], fetch_sems.at[1, 0])

    def fetch_planes(n):
        t, m = p.batches[n]
        return pltpu.make_async_copy(rz.at[:, pl.ds(t, m)], stage_z.at[:, pl.ds(0, m)], fetch_sems.at[2, 0])

    def step_core(n):
        sum_core(n).start()

    def step_core_fetch(n):
        sum_core(n).wait_recv()
        fetch_core(n).start()

    def step_columns(n):
        t, m = p.batches[n]
        fetch_core(n).wait()
        def add(j, _):
            tile, aa = j // A, lax.rem(j, A)
            mine = wall[t + tile, aa, :, c].astype(F32) + stage_c[n % 2, tile, aa].astype(F32)
            wall[t + tile, aa, :, c] = mine.astype(BF16)
            return 0
        lax.fori_loop(0, m * A, add, 0)
        for shift in range(1, B):
            sum_columns(n, shift).start()

    def step_columns_fetch(n):
        for shift in range(1, B):
            sum_columns(n, shift).wait_recv()
        fetch_columns(n).start()

    def step_planes(n):
        t, m = p.batches[n]
        fetch_columns(n).wait()
        def add(tile, _):
            mine = wall[t + tile, :, b, c].astype(F32)
            for shift in range(1, B):
                mine += stage_x[shift - 1, tile].astype(F32)
            wall[t + tile, :, b, c] = mine.astype(BF16)
            return 0
        lax.fori_loop(0, m, add, 0)
        for shift in range(1, A):
            sum_planes(n, shift).start()

    def step_planes_fetch(n):
        for shift in range(1, A):
            sum_planes(n, shift).wait_recv()
        fetch_planes(n).start()

    def step_out(n):
        t, m = p.batches[n]
        fetch_planes(n).wait()
        for tile in range(m):
            mine = wall[t + tile, a, b, c].astype(F32)
            for shift in range(1, A):
                mine += stage_z[shift - 1, tile].astype(F32)
            u = t + tile
            for name, first in (("d_gate", p.gate), ("d_up", p.up), ("d_down", p.down), ("d_out", p.out)):
                count = p.no if name == "d_out" else p.nt
                if first <= u < first + count:
                    r[name][:, (u - first) * TILE:(u - first + 1) * TILE] = mine
            if u >= p.qkv:
                h = u - p.qkv
                r["d_query"][:, 128 * h:128 * h + 128] = mine[:, 0:128]
                r["d_key"][:, 64 * h:64 * h + 64] = mine[:, 128:192]
                r["d_value"][:, 64 * h:64 * h + 64] = mine[:, 192:256]

    def steps_planes(n):
        step_columns_fetch(n)
        step_planes(n)

    def steps_out(n):
        step_planes_fetch(n)
        step_out(n)

    def feed_forward(hs, n2_t, dy_t):
        def turned(source, k, target):
            for piece in range(R // 128):
                rows = pl.ds(piece * 128, 128)
                target[:, k * R + piece * 128:k * R + (piece + 1) * 128] = jnp.transpose(source[k, rows].astype(F32)).astype(BF16)

        turned(dy_all, 0, dy_t)
        for k in others:
            gathered(AG_DY, dy_all, k).wait_recv()
            turned(dy_all, k, dy_t)
        for k in others:
            scattered(RS_P, y_send, y_recv, k).wait_recv()
        for piece in range(R // 128):
            rows = pl.ds(piece * 128, 128)
            v = x_all[0, rows].astype(F32) + part[rows]
            for k in others:
                v += y_recv[k, rows].astype(F32)
            middle[rows] = v
            n2_all[0, rows] = (v * lax.rsqrt(jnp.mean(v * v, axis=1, keepdims=True) + EPS) * r["gain_two"][...]).astype(BF16)
        for k in others:
            gather(AG_N2, n2_all, k).start()
        turned(n2_all, 0, n2_t)

        def hidden(k):
            rows = slice(k * R, (k + 1) * R)
            def step(t, _):
                gate = dot(n2_all[k], weight(p.gate + t))
                up = dot(n2_all[k], weight(p.up + t))
                grad = dot(dy_all[k], weight(p.down + t))
                sig = 1.0 / (1.0 + jnp.exp(-gate))
                silu = gate * sig
                hs[2, t, rows] = (silu * up).astype(BF16)
                hs[0, t, rows] = (grad * up * (sig * (1.0 + gate * (1.0 - sig)))).astype(BF16)
                hs[1, t, rows] = (grad * silu).astype(BF16)
                return 0
            lax.fori_loop(0, p.nt, step, 0)

        def back_normed(k):
            rows = slice(k * R, (k + 1) * R)
            for aa in range(A):
                total = jnp.zeros((R, D // A), F32)
                for t in range(p.nt):
                    total += nt_dot(hs[0, t, rows], weight_rows(p.gate + t, aa))
                    total += nt_dot(hs[1, t, rows], weight_rows(p.up + t, aa))
                store_part(k, y_send, part, aa, total)

        def down(k):
            rows = slice(k * R, (k + 1) * R)
            for aa in range(A):
                total = jnp.zeros((R, D // A), F32)
                for t in range(p.nt):
                    total += nt_dot(hs[2, t, rows], weight_rows(p.down + t, aa))
                if k == 0:
                    columns = slice(aa * (D // A), (aa + 1) * (D // A))
                    out_acc[:, columns] = middle[:, columns] + total
                else:
                    store_part(k, fo_send, None, aa, total)

        hidden(0)
        back_normed(0)
        down(0)
        for k in others:
            scatter(RS_P, y_send, y_recv, k).wait_send()
            gathered(AG_N2, n2_all, k).wait_recv()
            hidden(k)
            back_normed(k)
            scatter(RS_GN2, y_send, y_recv, k).start()
        for k in others:
            turned(n2_all, k, n2_t)
            down(k)

        def weight_gradients(n):
            t, m = p.batches[n]
            for tile in range(t, t + m):
                kind, u = tile // p.nt, tile % p.nt
                left = dy_t if kind == 2 else n2_t
                for aa in range(A):
                    rows = slice(aa * (D // A), (aa + 1) * (D // A))
                    wall[tile, aa] = dot(left[rows], hs[kind, u]).astype(BF16).reshape(B, 2, S, TILE)

        for n in range(p.ff_batches):
            weight_gradients(n)
            step_core(n)
            if n >= 1:
                step_core_fetch(n - 1)
            if n >= 2:
                step_columns(n - 2)

    pl.run_scoped(
        feed_forward,
        pltpu.VMEM((3, p.nt, G * R, TILE), BF16),
        pltpu.VMEM((D, G * R), BF16),
        pltpu.VMEM((D, G * R), BF16),
    )
    last = p.ff_batches
    step_core_fetch(last - 1)
    step_columns(last - 2)

    gb_t = r["gb_t"]
    for k in others:
        scattered(RS_GN2, y_send, y_recv, k).wait_recv()
    gain_grad = jnp.zeros((1, D), F32)
    for piece in range(R // 128):
        rows = pl.ds(piece * 128, 128)
        e = part[rows]
        for k in others:
            e += y_recv[k, rows].astype(F32)
        v = middle[rows]
        rr = lax.rsqrt(jnp.mean(v * v, axis=1, keepdims=True) + EPS)
        vh = v * rr
        gain_grad += jnp.sum(e * vh, axis=0, keepdims=True)
        ge = e * r["gain_two"][...]
        gm = dy_all[0, rows].astype(F32) + rr * (ge - vh * jnp.mean(vh * ge, axis=1, keepdims=True))
        middle[rows] = gm
        gb_all[0, rows] = gm.astype(BF16)
        gb_t[:, piece * 128:(piece + 1) * 128] = jnp.transpose(gm).astype(BF16)
    gains[...] = jnp.zeros((8, D), F32)
    gains[0:1] = gain_grad
    for k in others:
        gather(AG_GB, gb_all, k).start()
        scatter(RS_FO, fo_send, fo_recv, k).start()
    step_columns(last - 1)

    dm = r["dm"]
    graw = r["graw"]
    kvr, xr, zr = r["kvr"], r["xr"], r["zr"]
    kc_sems, kx_sems, kz_sems = r["kc_sems"], r["kx_sems"], r["kz_sems"]
    head_sums = r["head_sums"]
    head_sums[...] = jnp.zeros((128, R), F32)

    def mixed_gradient(k):
        for t in range(p.no):
            dm[:, t * TILE:(t + 1) * TILE] = dot(gb_all[k], weight(p.out + t)).astype(BF16)

    def k_core(d, column, k):
        return remote(kvw.at[d, 2 * column + 1 - c, k], kvr.at[d, column, k], kc_sems.at[0, d, column, k], kc_sems.at[1, d, column, k], sibling)

    def k_column(d, shift, k):
        target = lax.rem(b + shift, B)
        return remote(kvw.at[d, 2 * target + c, k], xr.at[d, shift - 1, k], kx_sems.at[0, d, shift, k], kx_sems.at[1, d, shift, k], at(a, target, c))

    def k_plane(d, k):
        return remote(kvw.at[d, place, k], zr.at[d - 1, k], kz_sems.at[0, d - 1, k], kz_sems.at[1, d - 1, k], at(lax.rem(a + A - 1, A), b, c))

    def in_window(d, column, core, from_core):
        if d == 0:
            return jnp.logical_or(column < b, jnp.logical_and(column == b, core <= from_core))
        if d == 1:
            return column >= 0
        return jnp.logical_or(column > b, jnp.logical_and(column == b, core >= from_core))

    def column_reached(d, target, source):
        if d == 0:
            return target < source
        if d == 1:
            return target >= 0
        return target > source

    def keys_core(d, k):
        for column in range(B):
            @when_all(a >= d, in_window(d, column, 1 - c, c))
            def _():
                k_core(d, column, k).start()

    def keys_scope(k, kv_stage, kv_sems):
        def fetch(d, column):
            return pltpu.make_async_copy(kvr.at[d, column, k], kv_stage.at[d, column], kv_sems.at[d, column])

        for d in (2, 1, 0):
            for column in range(B):
                @when_all(a >= d, in_window(d, column, c, 1 - c))
                def _():
                    k_core(d, column, k).wait_recv()
                    fetch(d, column).start()
        for d in (2, 1, 0):
            for column in range(B):
                @when_all(a >= d, in_window(d, column, c, 1 - c))
                def _():
                    fetch(d, column).wait()
                    for h in range(KV):
                        slot = 2 * column + c
                        kvw[d, slot, k, h] = (kvw[d, slot, k, h].astype(F32) + kv_stage[d, column, h].astype(F32)).astype(BF16)
            for shift in range(1, B):
                @when_all(a >= d, column_reached(d, lax.rem(b + shift, B), b))
                def _():
                    k_column(d, shift, k).start()

    def keys_columns(d, k):
        for shift in range(1, B):
            @when_all(a >= d, column_reached(d, b, lax.rem(b + B - shift, B)))
            def _():
                k_column(d, shift, k).wait_recv()
                for h in range(KV):
                    kvw[d, place, k, h] = (kvw[d, place, k, h].astype(F32) + xr[d, shift - 1, k, h].astype(F32)).astype(BF16)

    def keys_plane(d, k):
        @pl.when(a >= d)
        def _():
            k_plane(d, k).start()

    def keys_from_plane(d, k):
        @when_all(a + 1 < A, a + 1 >= d)
        def _():
            k_plane(d, k).wait_recv()
            for h in range(KV):
                kvw[d - 1, place, k, h] = (kvw[d - 1, place, k, h].astype(F32) + zr[d - 1, k, h].astype(F32)).astype(BF16)

    def keys_sent(k):
        for d in range(WINDOW):
            for column in range(B):
                @when_all(a >= d, in_window(d, column, 1 - c, c))
                def _():
                    k_core(d, column, k).wait_send()
            for shift in range(1, B):
                @when_all(a >= d, column_reached(d, lax.rem(b + shift, B), b))
                def _():
                    k_column(d, shift, k).wait_send()
            if d:
                @pl.when(a >= d)
                def _():
                    k_plane(d, k).wait_send()

    def rms_back(raw, e, gain):
        rr = lax.rsqrt(jnp.mean(raw * raw, axis=1, keepdims=True) + EPS)
        vh = raw * rr
        ge = e * gain
        return jnp.sum(e * vh, axis=0), rr * (ge - vh * jnp.mean(vh * ge, axis=1, keepdims=True))

    def attention_back(k, do_t, do_rows, q_rows, dq, rows_of, between):
        mixed_gradient(k)
        for h in range(KV):
            turned = jnp.transpose(dm[:, 128 * h:128 * h + 128].astype(F32))
            grad = jnp.concatenate([turned[0:64], turned[64:128]], axis=1)
            rows_of[h, 0:1] = jnp.log2(o_acc[k, h, 64:65])
            rows_of[h, 1:2] = jnp.sum(grad * o_acc[k, h, 0:64], axis=0, keepdims=True)
            padded = jnp.concatenate([jnp.zeros((64, 2 * R), F32), grad], axis=0)
            do_t[h] = padded.astype(BF16)
            do_rows[h] = jnp.transpose(padded).astype(BF16)
            q_rows[h] = (jnp.transpose(q_t[k, h].astype(F32)) * (1.0 / math.sqrt(HEAD))).astype(BF16)

        def block(d, other, diagonal=False):
            key_start = ((a - d) * 2 * B + other) * R
            allowed = mask_of(k, key_start, diagonal)
            for h in range(KV):
                kv = kvw[d, other, k, h]
                scores = dot(kv, q_t[k, h])
                probs = jnp.where(allowed, jnp.exp2(scores * EXP2_SCALE - rows_of[h, 0:1]), 0.0)
                grad = dot(kv, do_t[h])
                grad_scores = (probs * (grad - rows_of[h, 1:2])).astype(BF16)
                kvw[d, other, k, h] = (dot(grad_scores, q_rows[h]) + dot(probs.astype(BF16), do_rows[h])).astype(BF16)
                keys = jnp.transpose(kv)[0:64]
                if diagonal:
                    dq[h] = dot(keys, grad_scores)
                else:
                    dq[h] += dot(keys, grad_scores)

        def plane(d):
            low, high = attended(d)
            def step(other, _):
                block(d, other)
                return 0
            lax.fori_loop(low, high, step, 0)

        block(0, place, True)
        plane(2)
        keys_core(2, k)
        between(0)
        plane(1)
        keys_core(1, k)
        between(1)
        plane(0)
        keys_core(0, k)
        cos, sin = aux[k, 0:32], aux[k, 32:64]
        for h in range(KV):
            e = (dq[h] * (1.0 / math.sqrt(HEAD))).astype(BF16).astype(F32)
            e = rotate_back(jnp.stack([e[:, 0:R], e[:, R:2 * R]]), cos, sin)
            gain_part, grad = rms_back(raws[k, h, 0:128].reshape(2, HEAD, R), e, r["gain_columns"][0:64, 0:1])
            head_sums[0:64] += gain_part
            graw[h, k * R:(k + 1) * R, 0:128] = jnp.transpose(grad.reshape(128, R)).astype(BF16)

    def keys_back(k):
        cos, sin = aux[k, 0:32], aux[k, 32:64]
        for h in range(KV):
            final = jnp.transpose(kvw[0, place, k, h].astype(F32))
            e = rotate_back(final[0:64].reshape(1, HEAD, R), cos, sin)
            gain_part, grad = rms_back(raws[k, h, 128:192].reshape(1, HEAD, R), e, r["gain_columns"][64:128, 0:1])
            head_sums[64:128] += gain_part
            both = jnp.concatenate([grad.reshape(HEAD, R), final[64:128]], axis=0)
            graw[h, k * R:(k + 1) * R, 128:256] = jnp.transpose(both).astype(BF16)

    xg = r["xg"]

    def input_gradient(k):
        for aa in range(A):
            columns = slice(aa * (D // A), (aa + 1) * (D // A))
            total = jnp.zeros((R, D // A), F32)
            for h in range(KV):
                total += nt_dot(graw[h, k * R:(k + 1) * R], weight_rows(p.qkv + h, aa))
            store_part(k, y_send, part, aa, total)
            x = x_all[k, :, columns].astype(F32)
            xg[:, columns] += jnp.sum(total * x * x_scale(k), axis=0, keepdims=True)

    def x_scale(k):
        return r["x_scale"][k, :, 0:1]

    def backward_scope(do_t, do_rows, q_rows, dq, rows_of, kv_stage, kv_sems):
        pending = [lambda n=n, s=s: s(n) for n in range(last) for s in (steps_planes,)]
        done = []

        def advance(count):
            for _ in range(count):
                if pending:
                    pending.pop(0)()

        advance(1)
        attention_back(0, do_t, do_rows, q_rows, dq, rows_of, lambda n: advance(1))
        for k in others:
            gathered(AG_GB, gb_all, k).wait_recv()
            for piece in range(R // 128):
                rows = pl.ds(piece * 128, 128)
                gb_t[:, k * R + piece * 128:k * R + (piece + 1) * 128] = jnp.transpose(gb_all[k, rows].astype(F32)).astype(BF16)
            if k == 1:
                keys_scope(0, kv_stage, kv_sems)
            attention_back(k, do_t, do_rows, q_rows, dq, rows_of, lambda n: advance(1))
        keys_columns(2, 0)
        keys_plane(2, 0)
        for t in range(p.no):
            for aa in range(A):
                rows = slice(aa * (D // A), (aa + 1) * (D // A))
                total = jnp.zeros((D // A, TILE), F32)
                for k in range(G):
                    total += dot(gb_t[rows, k * R:(k + 1) * R], mixed[k, :, t * TILE:(t + 1) * TILE])
                wall[p.out + t, aa] = total.astype(BF16).reshape(B, 2, S, TILE)
        step_core(last)
        for k in others:
            keys_scope(k, kv_stage, kv_sems)
        step_core_fetch(last)
        keys_columns(1, 0)
        keys_from_plane(2, 0)
        keys_plane(1, 0)
        step_columns(last)
        for k in others:
            keys_columns(2, k)
            keys_plane(2, k)
        advance(1)
        keys_columns(0, 0)
        for k in others:
            keys_columns(1, k)
            keys_from_plane(2, k)
            keys_plane(1, k)
        advance(1)
        keys_from_plane(1, 0)
        keys_back(0)
        for k in others:
            keys_columns(0, k)
        advance(1)
        for k in others:
            keys_from_plane(1, k)
            keys_back(k)
        while pending:
            advance(1)

    pl.run_scoped(
        backward_scope,
        pltpu.VMEM((KV, 128, 2 * R), BF16),
        pltpu.VMEM((KV, 2 * R, 128), BF16),
        pltpu.VMEM((KV, 2 * R, 128), BF16),
        pltpu.VMEM((KV, 64, 2 * R), F32),
        pltpu.VMEM((KV, 8, 2 * R), F32),
        pltpu.VMEM((WINDOW, B, KV, R, 128), BF16),
        pltpu.SemaphoreType.DMA((WINDOW, B)),
    )

    xg[...] = jnp.zeros((1, D), F32)
    for k in range(G):
        x = x_all[k].astype(F32)
        r["x_scale"][k] = jnp.broadcast_to(lax.rsqrt(jnp.mean(x * x, axis=1, keepdims=True) + EPS), (R, 128))
    for k in others:
        scatter(RS_GN2, y_send, y_recv, k).wait_send()
        input_gradient(k)
        scatter(RS_GN, y_send, y_recv, k).start()
    input_gradient(0)
    for n in (last + 1, last + 2):
        t, m = p.batches[n]
        for tile in range(t, t + m):
            for aa in range(A):
                rows = slice(aa * (D // A), (aa + 1) * (D // A))
                wall[tile, aa] = dot(n_t[rows], graw[tile - p.qkv]).astype(BF16).reshape(B, 2, S, TILE)
        step_core(n)

    gains[1:2] = xg[...]
    sums = jnp.sum(jnp.transpose(head_sums[...]), axis=0, keepdims=True)
    gains[2:3, 0:128] = sums
    g_land, g_sems = r["g_land"], r["g_sems"]
    stages = [
        (2, c, lambda j: at(a, b, j)),
        (B, b, lambda j: at(a, j, c)),
        (A, a, lambda j: at(j, b, c)),
        (G, f, lambda j: (i, j)),
    ]

    def gain_send(s, shift):
        size, mine, device = stages[s]
        return remote(gains, g_land.at[s, mine], g_sems.at[0, s, shift], g_sems.at[1, s, shift], device(lax.rem(mine + shift, size)))

    def gain_arrival(s, shift):
        size, mine, device = stages[s]
        slot = lax.rem(mine + size - shift, size)
        return remote(gains, g_land.at[s, slot], g_sems.at[0, s, shift], g_sems.at[1, s, shift], device(slot))

    def gain_start(s):
        size, mine, _ = stages[s]
        for shift in range(1, size):
            gain_send(s, shift).start()
        g_land[s, mine] = gains[...]

    def gain_finish(s):
        size, mine, _ = stages[s]
        for shift in range(1, size):
            gain_arrival(s, shift).wait_recv()
            gain_send(s, shift).wait_send()
        total = g_land[s, 0]
        for j in range(1, size):
            total += g_land[s, j]
        gains[...] = total

    gain_start(0)
    step_core_fetch(last + 1)
    step_columns(last + 1)
    gain_finish(0)
    gain_start(1)
    step_core_fetch(last + 2)
    step_columns(last + 2)
    gain_finish(1)
    gain_start(2)
    for n in range(last):
        steps_out(n)
    for n in (last, last + 1, last + 2):
        steps_planes(n)
    gain_finish(2)
    gain_start(3)
    for k in others:
        scattered(RS_FO, fo_send, fo_recv, k).wait_recv()
    for piece in range(R // 128):
        rows = pl.ds(piece * 128, 128)
        v = out_acc[rows]
        for k in others:
            v += fo_recv[k, rows].astype(F32)
        r["block_out"][0, rows] = v.astype(BF16)
    for k in others:
        scattered(RS_GN, y_send, y_recv, k).wait_recv()
    for piece in range(R // 128):
        rows = pl.ds(piece * 128, 128)
        e = part[rows]
        for k in others:
            e += y_recv[k, rows].astype(F32)
        v = x_all[0, rows].astype(F32)
        rr = r["x_scale"][0, rows, 0:1]
        vh = v * rr
        ge = e * r["gain_one"][...]
        back = rr * (ge - vh * jnp.mean(vh * ge, axis=1, keepdims=True))
        r["grad_inputs"][0, rows] = (middle[rows] + back).astype(BF16)
    gain_finish(3)
    r["d_gains"][...] = gains[...]
    for n in (last, last + 1, last + 2):
        steps_out(n)

    for k in range(G):
        keys_sent(k)
    for k in others:
        gather(AG_DY, dy_all, k).wait_send()
        gather(AG_N2, n2_all, k).wait_send()
        gather(AG_GB, gb_all, k).wait_send()
        scatter(RS_FO, fo_send, fo_recv, k).wait_send()
        scatter(RS_GN, y_send, y_recv, k).wait_send()
    for n in range(len(p.batches)):
        sum_core(n).wait_send()
        for shift in range(1, B):
            sum_columns(n, shift).wait_send()
        for shift in range(1, A):
            sum_planes(n, shift).wait_send()


def local(p, x, dy, lengths, gain_one, gain_two, query_gain, key_gain, wq, wk, wv, wo, wg, wu, wd):
    A, B, G, R, D, KV, S = p.A, p.B, p.G, p.R, p.D, p.KV, p.S
    freq = np.exp(np.arange(32, dtype=np.float32) * np.float32(-2.0 * math.log(THETA) / HEAD)).astype(np.float32)
    freq = jnp.broadcast_to(jnp.asarray(freq)[:, None], (32, R))
    head_gains = jnp.concatenate([query_gain, key_gain])[None]
    any_spec, vmem, smem = (pl.BlockSpec(memory_space=m) for m in (pl.ANY, pltpu.VMEM, pltpu.SMEM))
    ins = dict(
        x=(x, any_spec), dy=(dy, any_spec), lengths=(lengths, smem), gain_one=(gain_one[None], vmem),
        gain_two=(gain_two[None], vmem), head_gains=(head_gains, vmem), freq=(freq, vmem),
        w_query=(wq, any_spec), w_key=(wk, any_spec), w_value=(wv, any_spec), w_out=(wo, any_spec),
        w_gate=(wg, any_spec), w_up=(wu, any_spec), w_down=(wd, any_spec),
    )
    rows_out = ((1, R, D), BF16)
    outs = dict(
        block_out=rows_out, grad_inputs=rows_out, d_gains=((8, D), F32),
        d_query=((S, 128 * KV), F32), d_key=((S, 64 * KV), F32), d_value=((S, 64 * KV), F32), d_out=((S, 128 * KV), F32),
        d_gate=((S, p.FL), F32), d_up=((S, p.FL), F32), d_down=((S, p.FL), F32),
    )
    landing = dict(
        rc=((p.tiles, A, B, S, TILE), BF16), rx=((B - 1, p.tiles, A, S, TILE), BF16), rz=((A - 1, p.tiles, S, TILE), BF16),
        kvr=((WINDOW, B, G, KV, R, 128), BF16),
    )
    DMA = pltpu.SemaphoreType.DMA
    n_batches, widest = len(p.batches), max(m for _, m in p.batches)
    scratch = dict(
        x_all=pltpu.VMEM((G, R, D), BF16), aux=pltpu.VMEM((G, 72, R), F32), dy_all=pltpu.VMEM((G, R, D), BF16),
        y_sems=DMA((9, 2, G)), local_sems=DMA((8,)),
        gain_columns=pltpu.VMEM((128, 128), F32),
        kvw=pltpu.VMEM((WINDOW, 2 * B, G, KV, R, 128), BF16),
        z_sems=DMA((2, 2, G)), x_sems=DMA((2, WINDOW, B, G)), c_sems=DMA((2, WINDOW, B, G)),
        wall=pltpu.VMEM((p.tiles, A, B, 2, S, TILE), BF16),
        n_t=pltpu.VMEM((D, G * R), BF16), n_rows=pltpu.VMEM((R, D), BF16),
        raws=pltpu.VMEM((G, KV, 192, R), F32), q_t=pltpu.VMEM((G, KV, 128, 2 * R), BF16),
        o_acc=pltpu.VMEM((G, KV, 80, 2 * R), F32), mixed=pltpu.VMEM((G, R, p.HQ), BF16),
        y_send=pltpu.VMEM((G, R, D), BF16), y_recv=pltpu.VMEM((G, R, D), BF16),
        fo_send=pltpu.VMEM((G, R, D), BF16), fo_recv=pltpu.VMEM((G, R, D), BF16),
        part=pltpu.VMEM((R, D), F32), out_acc=pltpu.VMEM((R, D), F32), middle=pltpu.VMEM((R, D), F32),
        n2_all=pltpu.VMEM((G, R, D), BF16), gb_all=pltpu.VMEM((G, R, D), BF16), gb_t=pltpu.VMEM((D, G * R), BF16),
        gains=pltpu.VMEM((8, D), F32), xg=pltpu.VMEM((1, D), F32), x_scale=pltpu.VMEM((G, R, 128), F32),
        w_sems=DMA((2, A + B - 1, n_batches)), fetch_sems=DMA((3, 2)),
        stage_c=pltpu.VMEM((2, widest, A, B, S, TILE), BF16), stage_x=pltpu.VMEM((B - 1, widest, A, S, TILE), BF16),
        stage_z=pltpu.VMEM((A - 1, widest, S, TILE), BF16),
        dm=pltpu.VMEM((R, p.HQ), BF16), graw=pltpu.VMEM((KV, G * R, TILE), BF16),
        xr=pltpu.VMEM((WINDOW, B - 1, G, KV, R, 128), BF16), zr=pltpu.VMEM((2, G, KV, R, 128), BF16),
        kc_sems=DMA((2, WINDOW, B, G)), kx_sems=DMA((2, WINDOW, B, G)), kz_sems=DMA((2, 2, G)),
        head_sums=pltpu.VMEM((128, R), F32),
        g_land=pltpu.VMEM((4, max(A, B, G, 2), 8, D), F32), g_sems=DMA((2, 4, max(A, B, G, 2))),
    )
    outs_all = dict(outs, **landing)
    out_specs = [vmem for _ in outs] + [any_spec for _ in landing]
    names = list(ins) + list(outs_all) + list(scratch)
    results = pl.pallas_call(
        functools.partial(kernel, p, names),
        out_shape=[jax.ShapeDtypeStruct(*o) for o in outs_all.values()],
        in_specs=[s for _, s in ins.values()],
        out_specs=out_specs,
        scratch_shapes=list(scratch.values()),
        compiler_params=pltpu.CompilerParams(collective_id=0, has_side_effects=True, vmem_limit_bytes=64 << 20),
        name="block",
    )(*[v for v, _ in ins.values()])
    o = dict(zip(outs_all, results))
    g = o["d_gains"]
    return (
        o["block_out"], o["grad_inputs"], g[1], g[0], g[2, 0:64], g[2, 64:128],
        o["d_query"], o["d_key"], o["d_value"], o["d_out"], o["d_gate"], o["d_up"], o["d_down"],
    )


QUERY_HEADS = 16
KEY_VALUE_HEADS = 8
HEAD_SIZE = HEAD


MASKED_FILL = -1e30


def swapped(value, axis, bit):
    mask = 2**bit
    pairs = [(source, source ^ mask) for source in range(lax.axis_size(axis))]
    return lax.ppermute(value, axis, pairs)


def root_mean_norm(values, gain):
    return values * lax.rsqrt(jnp.mean(values * values, axis=-1, keepdims=True) + EPS) * gain


def apply_rotary(values, cosine_table, sine_table):
    half_width = values.shape[-1] // 2
    turned = jnp.concatenate([-values[..., half_width:], values[..., :half_width]], axis=-1)
    return values * cosine_table + turned * sine_table


def places(lengths, where):
    ends = jnp.cumsum(lengths)
    before = (ends[None, :] <= where[:, None]).astype(jnp.int32)
    segment = jnp.sum(before, axis=1)
    offset = where - jnp.sum(before * lengths[None, :], axis=1)
    return (segment, offset)


def head_post(query_raw, unrotated_key, query_gain, key_norm_gain, cosine_table, sine_table):
    token_count = query_raw.shape[0]
    query_rot = apply_rotary(
        root_mean_norm(query_raw.reshape(token_count, QUERY_HEADS, HEAD_SIZE), query_gain),
        cosine_table,
        sine_table,
    )
    rotated_key = apply_rotary(
        root_mean_norm(
            unrotated_key.reshape(token_count, KEY_VALUE_HEADS, HEAD_SIZE), key_norm_gain
        ),
        cosine_table,
        sine_table,
    )
    return (query_rot, rotated_key)


def swiglu(gate, upward):
    return jax.nn.silu(gate) * upward


def matmul(left, right):
    return jnp.dot(left, right, preferred_element_type=jnp.float32)


def project_back(left, right):
    return lax.dot_general(
        left, right, (((1,), (1,)), ((), ())), preferred_element_type=jnp.float32
    )


def outer_sum(left, right):
    return lax.dot_general(
        left, right, (((0,), (0,)), ((), ())), preferred_element_type=jnp.float32
    )


def mirror_out(payload, steps):
    for bit in range(steps):
        payload = swapped(payload, "ctx", bit)
    return payload


def mirror_back(payload, steps):
    for bit in range(steps):
        payload = swapped(payload, "ctx", bit)
    return payload


def halves_order(array, parts):
    shaped = array.reshape((parts, 2, array.shape[0] // (2 * parts)) + array.shape[1:])
    return jnp.stack([shaped[:, 0], shaped[::-1, 1]], axis=1).reshape(array.shape)


def general(
    inputs,
    cotangent,
    lengths,
    gain_one,
    gain_two,
    query_gain,
    key_norm_gain,
    w_query,
    key_projection,
    value_projection,
    w_out,
    w_gate,
    w_up,
    w_down,
):
    brain_float = jnp.bfloat16
    parts = lax.axis_size("ctx")
    steps = parts.bit_length() - 1
    device_index = lax.axis_index("ctx")
    row_count = inputs.shape[1]
    head_group = row_count * parts
    half_width = row_count // 2
    own_lengths = lengths[0]
    offsets_half = jnp.arange(half_width, dtype=jnp.int32)
    arrived = mirror_out(jnp.stack([inputs[0][half_width:], cotangent[0][half_width:]]), steps)
    x_rows = jnp.concatenate([inputs[0][:half_width], arrived[0]], axis=0)
    dy_rows = jnp.concatenate([cotangent[0][:half_width], arrived[1]], axis=0)
    query_place = jnp.concatenate(
        [
            device_index * row_count + offsets_half,
            (parts - 1 - device_index) * row_count + half_width + offsets_half,
        ]
    )
    key_place = jnp.arange(head_group, dtype=jnp.int32)
    query_segment, query_offset = places(own_lengths, query_place)
    key_segment, key_offset = places(own_lengths, key_place)
    weight_query, weight_key, weight_value, weight_out = (
        lax.all_gather(w_query.astype(brain_float), "fsdp", axis=1, tiled=True),
        lax.all_gather(key_projection.astype(brain_float), "fsdp", axis=1, tiled=True),
        lax.all_gather(value_projection.astype(brain_float), "fsdp", axis=1, tiled=True),
        lax.all_gather(w_out.astype(brain_float), "fsdp", axis=1, tiled=True),
    )
    x_float = x_rows.astype(jnp.float32)
    normed_f, norm_one_back = jax.vjp(root_mean_norm, x_float, gain_one)
    normed_input = normed_f.astype(brain_float)
    query_raw = matmul(normed_input, weight_query)
    unrotated_key = matmul(normed_input, weight_key)
    value_b = matmul(normed_input, weight_value).astype(brain_float)
    freq = jnp.exp(
        jnp.arange(HEAD_SIZE // 2, dtype=jnp.float32) * (-2.0 * math.log(THETA) / HEAD_SIZE)
    )
    angle = query_offset.astype(jnp.float32)[:, None] * freq[None, :]
    cosine_table = jnp.concatenate([jnp.cos(angle), jnp.cos(angle)], axis=-1)[:, None, :]
    sine_table = jnp.concatenate([jnp.sin(angle), jnp.sin(angle)], axis=-1)[:, None, :]

    def post_local(query_in, key_in, gain_q, gain_k):
        return head_post(query_in, key_in, gain_q, gain_k, cosine_table, sine_table)

    (query_rot, rotated_key), post_back = jax.vjp(
        post_local, query_raw, unrotated_key, query_gain, key_norm_gain
    )
    query_batch = query_rot.astype(brain_float)
    key_batch = rotated_key.astype(brain_float).reshape(row_count, KEY_VALUE_HEADS * HEAD_SIZE)
    gathered_keys, gathered_values = (
        lax.all_gather(key_batch, "ctx", axis=0, tiled=True),
        lax.all_gather(value_b, "ctx", axis=0, tiled=True),
    )
    gathered_keys = halves_order(gathered_keys, parts)
    gathered_values = halves_order(gathered_values, parts)
    shared_heads = QUERY_HEADS // KEY_VALUE_HEADS
    score_scale = 1.0 / math.sqrt(HEAD_SIZE)
    keys_per_block = min(1024, head_group)
    block_count = head_group // keys_per_block
    query_quad = query_batch.reshape(row_count, KEY_VALUE_HEADS, shared_heads, HEAD_SIZE)
    blocked_keys = gathered_keys.reshape(block_count, keys_per_block, KEY_VALUE_HEADS, HEAD_SIZE)
    blocked_values = gathered_values.reshape(
        block_count, keys_per_block, KEY_VALUE_HEADS, HEAD_SIZE
    )
    segment_blocks = key_segment.reshape(block_count, keys_per_block)
    place_blocks = key_place.reshape(block_count, keys_per_block)

    def tile_backward(query_tile, tile_segment, tile_place, tile_log, grad_tile, tile_delta):

        def allowed_of(segment_block, place_block):
            return (tile_segment[:, None] == segment_block[None, :]) & (
                tile_place[:, None] >= place_block[None, :]
            )

        def back_step(carry, block):
            key_block, value_block, segment_block, place_block = block
            allowed = allowed_of(segment_block, place_block)

            def back_active(grad_query):
                raw_scores = (
                    jnp.einsum(
                        "qhgd,khd->hgqk", query_tile, key_block, preferred_element_type=jnp.float32
                    )
                    * score_scale
                )
                probs = jnp.exp(
                    jnp.where(allowed[None, None], raw_scores, MASKED_FILL) - tile_log[..., None]
                )
                grad_probs = jnp.einsum(
                    "qhgd,khd->hgqk", grad_tile, value_block, preferred_element_type=jnp.float32
                )
                grad_scores = (probs * (grad_probs - tile_delta[..., None])).astype(brain_float)
                grad_query = grad_query + jnp.einsum(
                    "hgqk,khd->qhgd", grad_scores, key_block, preferred_element_type=jnp.float32
                )
                grad_key_block = jnp.einsum(
                    "hgqk,qhgd->khd", grad_scores, query_tile, preferred_element_type=jnp.float32
                )
                grad_value_block = jnp.einsum(
                    "hgqk,qhgd->khd",
                    probs.astype(brain_float),
                    grad_tile,
                    preferred_element_type=jnp.float32,
                )
                return (grad_query, (grad_key_block, grad_value_block))

            def skipped(grad_query):
                empty_result = jnp.zeros((keys_per_block, KEY_VALUE_HEADS, HEAD_SIZE), jnp.float32)
                return (grad_query, (empty_result, empty_result))

            return lax.cond(jnp.any(allowed), back_active, skipped, carry)

        initial_gradient = jnp.zeros(
            (half_width, KEY_VALUE_HEADS, shared_heads, HEAD_SIZE), jnp.float32
        )
        return lax.scan(
            back_step,
            initial_gradient,
            (blocked_keys, blocked_values, segment_blocks, place_blocks),
        )

    heads_list = []
    extra_list = []
    log_list = []
    for tile in range(2):
        rows_tile = slice(tile * half_width, (tile + 1) * half_width)
        tile_query_tile = query_quad[rows_tile]
        tile_tile_segment = query_segment[rows_tile]
        tile_tile_place = query_place[rows_tile]

        def tile_allowed_of(segment_block, place_block):
            return (tile_tile_segment[:, None] == segment_block[None, :]) & (
                tile_tile_place[:, None] >= place_block[None, :]
            )

        def scores_of(key_block, allowed):
            raw_scores = (
                jnp.einsum(
                    "qhgd,khd->hgqk", tile_query_tile, key_block, preferred_element_type=jnp.float32
                )
                * score_scale
            )
            return jnp.where(allowed[None, None], raw_scores, MASKED_FILL)

        def stats_step(carry, block):
            key_block, segment_block, place_block = block
            allowed = tile_allowed_of(segment_block, place_block)

            def stats_active(state):
                peak, total = state
                scores = scores_of(key_block, allowed)
                newest = jnp.maximum(peak, jnp.max(scores, axis=-1))
                total = total * jnp.exp(peak - newest) + jnp.sum(
                    jnp.exp(scores - newest[..., None]), axis=-1
                )
                return (newest, total)

            return (lax.cond(jnp.any(allowed), stats_active, lambda state: state, carry), None)

        initial_peak = jnp.full(
            (KEY_VALUE_HEADS, shared_heads, half_width), MASKED_FILL, jnp.float32
        )
        initial_total = jnp.zeros((KEY_VALUE_HEADS, shared_heads, half_width), jnp.float32)
        (peak, total), unused = lax.scan(
            stats_step, (initial_peak, initial_total), (blocked_keys, segment_blocks, place_blocks)
        )
        tile_tile_log = peak + jnp.log(total)

        def output_step(carry, block):
            key_block, value_block, segment_block, place_block = block
            allowed = tile_allowed_of(segment_block, place_block)

            def output_active(state):
                upper, lower = state
                probs = jnp.exp(scores_of(key_block, allowed) - tile_tile_log[..., None])
                probs_high = probs.astype(brain_float)
                probs_low = (probs - probs_high.astype(jnp.float32)).astype(brain_float)
                upper = upper + jnp.einsum(
                    "hgqk,khd->qhgd", probs_high, value_block, preferred_element_type=jnp.float32
                )
                lower = lower + jnp.einsum(
                    "hgqk,khd->qhgd", probs_low, value_block, preferred_element_type=jnp.float32
                )
                return (upper, lower)

            return (lax.cond(jnp.any(allowed), output_active, lambda state: state, carry), None)

        initial_accumulator = jnp.zeros(
            (half_width, KEY_VALUE_HEADS, shared_heads, HEAD_SIZE), jnp.float32
        )
        (tile_heads, tile_extra), unused = lax.scan(
            output_step,
            (initial_accumulator, initial_accumulator),
            (blocked_keys, blocked_values, segment_blocks, place_blocks),
        )
        tile_heads, tile_extra, tile_log = (tile_heads, tile_extra, tile_tile_log)
        heads_list.append(tile_heads)
        extra_list.append(tile_extra)
        log_list.append(tile_log)
    heads_four = jnp.concatenate(heads_list, axis=0)
    heads_extra = jnp.concatenate(extra_list, axis=0)
    mixed = heads_four.reshape(row_count, QUERY_HEADS * HEAD_SIZE).astype(brain_float)
    middle = x_float + project_back(mixed, weight_out)
    normed_two_f, norm_two_back = jax.vjp(root_mean_norm, middle, gain_two)
    normed_two = normed_two_f.astype(brain_float)
    weight_gate, weight_up, weight_down = (
        lax.all_gather(w_gate.astype(brain_float), "fsdp", axis=1, tiled=True),
        lax.all_gather(w_up.astype(brain_float), "fsdp", axis=1, tiled=True),
        lax.all_gather(w_down.astype(brain_float), "fsdp", axis=1, tiled=True),
    )
    gate = matmul(normed_two, weight_gate)
    upward = matmul(normed_two, weight_up)
    hidden_f, swiglu_back = jax.vjp(swiglu, gate, upward)
    hidden = hidden_f.astype(brain_float)
    ffn_out = project_back(hidden, weight_down)
    grad_gate_f, grad_up_f = swiglu_back(matmul(dy_rows, weight_down))
    grad_gate = grad_gate_f.astype(brain_float)
    grad_up = grad_up_f.astype(brain_float)
    grad_normed_two = project_back(grad_gate, weight_gate) + project_back(grad_up, weight_up)
    grad_gate_weight = outer_sum(normed_two, grad_gate)
    grad_up_weight = outer_sum(normed_two, grad_up)
    grad_down_weight = outer_sum(dy_rows, hidden)
    grad_middle_norm, grad_gain_two = norm_two_back(grad_normed_two)
    grad_middle = dy_rows.astype(jnp.float32) + grad_middle_norm
    grad_branch = grad_middle.astype(brain_float)
    grad_out_weight = outer_sum(grad_branch, mixed)
    mixed_gradient = matmul(grad_branch, weight_out).astype(brain_float)
    mixed_gradient_quad = mixed_gradient.reshape(
        row_count, KEY_VALUE_HEADS, shared_heads, HEAD_SIZE
    )
    exact_heads = heads_four + heads_extra
    delta = jnp.sum(mixed_gradient_quad.astype(jnp.float32) * exact_heads, axis=-1).transpose(
        1, 2, 0
    )
    grad_query_list = []
    all_key_gradients = jnp.zeros((head_group, KEY_VALUE_HEADS * HEAD_SIZE), jnp.float32)
    all_value_gradients = jnp.zeros((head_group, KEY_VALUE_HEADS * HEAD_SIZE), jnp.float32)
    for tile in range(2):
        rows_tile = slice(tile * half_width, (tile + 1) * half_width)
        tile_grad_query, (key_block_gradients, value_block_gradients) = tile_backward(
            query_quad[rows_tile],
            query_segment[rows_tile],
            query_place[rows_tile],
            log_list[tile],
            mixed_gradient_quad[rows_tile],
            delta[:, :, rows_tile],
        )
        grad_query_list.append(tile_grad_query)
        all_key_gradients = all_key_gradients + key_block_gradients.reshape(
            head_group, KEY_VALUE_HEADS * HEAD_SIZE
        )
        all_value_gradients = all_value_gradients + value_block_gradients.reshape(
            head_group, KEY_VALUE_HEADS * HEAD_SIZE
        )
    grad_query_four = jnp.concatenate(grad_query_list, axis=0)
    all_key_gradients = all_key_gradients * score_scale
    all_key_gradients = halves_order(all_key_gradients, parts)
    all_value_gradients = halves_order(all_value_gradients, parts)
    own_key_gradient, grad_value_own = (
        lax.psum_scatter(
            all_key_gradients.astype(jnp.bfloat16), "ctx", scatter_dimension=0, tiled=True
        ).astype(jnp.float32),
        lax.psum_scatter(
            all_value_gradients.astype(jnp.bfloat16), "ctx", scatter_dimension=0, tiled=True
        ).astype(jnp.float32),
    )
    rotated_key_gradient = (
        own_key_gradient.astype(brain_float)
        .astype(jnp.float32)
        .reshape(row_count, KEY_VALUE_HEADS, HEAD_SIZE)
    )
    grad_value = grad_value_own.astype(brain_float)
    grad_query_rot = (
        (grad_query_four * score_scale)
        .astype(brain_float)
        .astype(jnp.float32)
        .reshape(row_count, QUERY_HEADS, HEAD_SIZE)
    )
    grad_query_raw_f, grad_key_raw_f, grad_query_gain, grad_key_gain = post_back(
        (grad_query_rot, rotated_key_gradient)
    )
    grad_query_raw = grad_query_raw_f.astype(brain_float)
    grad_key_raw = grad_key_raw_f.astype(brain_float)
    grad_normed = (
        project_back(grad_query_raw, weight_query)
        + project_back(grad_key_raw, weight_key)
        + project_back(grad_value, weight_value)
    )
    grad_query_weight = outer_sum(normed_input, grad_query_raw)
    grad_key_weight = outer_sum(normed_input, grad_key_raw)
    grad_value_weight = outer_sum(normed_input, grad_value)
    grad_x_norm, grad_gain_one = norm_one_back(grad_normed)
    out_rows = (middle + ffn_out).astype(brain_float)
    grad_rows = (grad_middle + grad_x_norm).astype(brain_float)
    returned = mirror_back(jnp.stack([out_rows[half_width:], grad_rows[half_width:]]), steps)
    out_rows = jnp.concatenate([out_rows[:half_width], returned[0]], axis=0)
    grad_rows = jnp.concatenate([grad_rows[:half_width], returned[1]], axis=0)
    summed = (
        lax.psum_scatter(
            grad_query_weight.astype(jnp.bfloat16), "fsdp", scatter_dimension=1, tiled=True
        ).astype(jnp.float32),
        lax.psum_scatter(
            grad_key_weight.astype(jnp.bfloat16), "fsdp", scatter_dimension=1, tiled=True
        ).astype(jnp.float32),
        lax.psum_scatter(
            grad_value_weight.astype(jnp.bfloat16), "fsdp", scatter_dimension=1, tiled=True
        ).astype(jnp.float32),
        lax.psum_scatter(
            grad_out_weight.astype(jnp.bfloat16), "fsdp", scatter_dimension=1, tiled=True
        ).astype(jnp.float32),
        lax.psum_scatter(
            grad_gate_weight.astype(jnp.bfloat16), "fsdp", scatter_dimension=1, tiled=True
        ).astype(jnp.float32),
        lax.psum_scatter(
            grad_up_weight.astype(jnp.bfloat16), "fsdp", scatter_dimension=1, tiled=True
        ).astype(jnp.float32),
        lax.psum_scatter(
            grad_down_weight.astype(jnp.bfloat16), "fsdp", scatter_dimension=1, tiled=True
        ).astype(jnp.float32),
    )
    final_grads = (
        lax.psum_scatter(
            summed[0].astype(jnp.bfloat16), "ctx", scatter_dimension=0, tiled=True
        ).astype(jnp.float32),
        lax.psum_scatter(
            summed[1].astype(jnp.bfloat16), "ctx", scatter_dimension=0, tiled=True
        ).astype(jnp.float32),
        lax.psum_scatter(
            summed[2].astype(jnp.bfloat16), "ctx", scatter_dimension=0, tiled=True
        ).astype(jnp.float32),
        lax.psum_scatter(
            summed[3].astype(jnp.bfloat16), "ctx", scatter_dimension=0, tiled=True
        ).astype(jnp.float32),
        lax.psum_scatter(
            summed[4].astype(jnp.bfloat16), "ctx", scatter_dimension=0, tiled=True
        ).astype(jnp.float32),
        lax.psum_scatter(
            summed[5].astype(jnp.bfloat16), "ctx", scatter_dimension=0, tiled=True
        ).astype(jnp.float32),
        lax.psum_scatter(
            summed[6].astype(jnp.bfloat16), "ctx", scatter_dimension=0, tiled=True
        ).astype(jnp.float32),
    )
    gains_total = lax.psum(
        (grad_gain_one, grad_gain_two, grad_query_gain, grad_key_gain), ("ctx", "fsdp")
    )
    return (
        out_rows[None],
        grad_rows[None],
        gains_total[0],
        gains_total[1],
        gains_total[2],
        gains_total[3],
        final_grads[0],
        final_grads[1],
        final_grads[2],
        final_grads[3],
        final_grads[4],
        final_grads[5],
        final_grads[6],
    )


def solution(mesh):
    row, whole, split = P("fsdp", "ctx", None), P(), P(None, "fsdp")
    out_split = P("ctx", "fsdp")

    def step(x, dy, lengths, *rest):
        p = Plan(mesh.shape["ctx"], mesh.shape["fsdp"], x.shape[1], x.shape[2], rest[5].shape[1] // HEAD, rest[8].shape[1])
        p.nseq = lengths.shape[1]
        if not p.fits():
            return general(x, dy, lengths, *rest)
        return local(p, x, dy, lengths, *rest)

    return jax.shard_map(
        step, mesh=mesh,
        in_specs=(row, row, P("fsdp", None), whole, whole, whole, whole) + (split,) * 7,
        out_specs=(row, row, whole, whole, whole, whole) + (out_split,) * 7,
        check_vma=False,
    )
```

```python
import functools
import math

import jax
import jax.numpy as jnp
import numpy as np
from jax import lax
from jax.experimental import pallas as pl
from jax.experimental.pallas import tpu as pltpu
from jax.sharding import PartitionSpec as P

MESH = pl.DeviceIdType.MESH
BF16, F32 = jnp.bfloat16, jnp.float32
HEAD = 64
TILE = 256
EPS = 1e-05
THETA = 1000000.0
PLANES = 4
WINDOW = 3
FF_SLOTS = 12
EXP2_SCALE = math.log2(math.e) / math.sqrt(HEAD)


def nt_dot(left, right):
    return lax.dot_general(left, right, (((1,), (1,)), ((), ())), preferred_element_type=F32)


def dot(left, right):
    return jnp.dot(left, right, preferred_element_type=F32)


class Plan:
    def __init__(self, ctx, groups, rows, width, kv_heads, ff):
        self.A, self.B, self.G = PLANES, ctx // (2 * PLANES), groups
        self.R, self.D, self.KV, self.FL = rows, width, kv_heads, ff
        self.S = width // ctx
        self.nt = ff // TILE
        self.HQ = 128 * kv_heads
        self.no = self.HQ // TILE
        self.tiles = 3 * self.nt + self.no + kv_heads
        self.gate, self.up, self.down, self.out = 0, self.nt, 2 * self.nt, 3 * self.nt
        self.qkv = self.out + self.no
        self.batches = []
        for first, count, step in ((0, 3 * self.nt, 3), (self.out, self.no, 2), (self.qkv, kv_heads, 2)):
            self.batches += [(t, min(step, first + count - t)) for t in range(first, first + count, step)]
        self.ff_batches = -(-3 * self.nt // 3)
        self.pair_first = (1, 3, 5)

    def fits(self):
        rows = self.G * self.R
        weights = 2 * self.tiles * self.D * TILE
        keys = 2 * WINDOW * 2 * self.B * self.G * self.KV * self.R * 128
        activations = 2 * rows * (13 * self.D + 3 * self.FL)
        even = self.B == 2 and self.FL % TILE == 0 and self.HQ % TILE == 0 and self.R % 128 == 0
        return even and weights + keys + activations < 45 << 20


def rotate(u, cos, sin):
    low, high = u[:, :32], u[:, 32:]
    return jnp.concatenate([low * cos - high * sin, high * cos + low * sin], axis=1)


def rotate_back(u, cos, sin):
    low, high = u[:, :32], u[:, 32:]
    return jnp.concatenate([low * cos + high * sin, high * cos - low * sin], axis=1)


AG_X, AG_AUX, AG_DY, AG_N2, AG_GB, RS_P, RS_FO, RS_GN2, RS_GN = range(9)


def kernel(p, names, *refs):
    r = dict(zip(names, refs))
    A, B, G, R, D, KV, S = p.A, p.B, p.G, p.R, p.D, p.KV, p.S
    i, f = lax.axis_index("ctx"), lax.axis_index("fsdp")
    c = lax.rem(i, 2)
    b = lax.rem(i // 2, B)
    a = i // (2 * B)
    place = 2 * b + c
    others = range(1, G)

    def at(aa, bb, cc):
        return ((aa * B + bb) * 2 + cc, f)

    def group_device(k):
        return (i, lax.rem(f + k, G))

    def remote(src, dst, send, recv, device):
        return pltpu.make_async_remote_copy(
            src_ref=src, dst_ref=dst, send_sem=send, recv_sem=recv, device_id=device, device_id_type=MESH
        )

    sibling = at(a, b, 1 - c)

    peers = [sibling]
    peers += [at(a, lax.rem(b + k, B), c) for k in range(1, B)]
    peers += [at(lax.rem(a + k, A), b, c) for k in range(1, A)]
    peers += [group_device(k) for k in others]
    barrier = pltpu.get_barrier_semaphore()
    for peer in peers:
        pl.semaphore_signal(barrier, inc=1, device_id=peer, device_id_type=MESH)

    y_sems = r["y_sems"]

    def gather(kind, buffer, k):
        return remote(buffer.at[0], buffer.at[G - k], y_sems.at[kind, 0, k], y_sems.at[kind, 1, G - k], group_device(k))

    def gathered(kind, buffer, k):
        return remote(buffer.at[k], buffer.at[k], y_sems.at[kind, 0, k], y_sems.at[kind, 1, k], group_device(k))

    def scatter(kind, send, recv, k):
        return remote(send.at[k - 1], recv.at[G - k - 1], y_sems.at[kind, 0, k], y_sems.at[kind, 1, G - k], group_device(k))

    def scattered(kind, send, recv, k):
        return remote(send.at[k - 1], recv.at[k - 1], y_sems.at[kind, 0, k], y_sems.at[kind, 1, k], group_device(k))

    x_all, aux, dy_all = r["x_all"], r["aux"], r["dy_all"]
    local_sems = r["local_sems"]

    def tables():
        where = i * R + lax.broadcasted_iota(jnp.int32, (8, R), 1)
        start = jnp.zeros((8, R), jnp.int32)
        end = jnp.int32(0)
        for j in range(p.nseq):
            end = end + r["lengths"][0, j]
            start = jnp.where(where >= end, end, start)
        offset = (where - start).astype(F32)
        steps = lax.broadcasted_iota(jnp.int32, (32, R), 0).astype(F32)
        angle = offset[0:1] * jnp.exp(steps * (-2.0 * math.log(THETA) / HEAD))
        aux[0, 0:32] = jnp.cos(angle)
        aux[0, 32:64] = jnp.sin(angle)
        aux[0, 64:72] = start.astype(F32)
        for j, name in enumerate(("query_gain", "key_gain")):
            wide = jnp.concatenate([jnp.broadcast_to(r[name][...], (128, HEAD))] * 2, axis=1)
            r["gain_columns"][j * HEAD:(j + 1) * HEAD] = jnp.transpose(wide)[0:HEAD]

    kvw = r["kvw"]
    z_sems, x_sems, c_sems = r["z_sems"], r["x_sems"], r["c_sems"]
    wall = r["wall"]

    def weight(t):
        return wall[t].reshape(D, TILE)

    def weight_rows(t, aa):
        return wall[t, aa // 2, aa % 2].reshape(D // A, TILE)

    n_t = r["n_t"]
    raws, q_t, o_acc = r["raws"], r["q_t"], r["o_acc"]

    def z_copy(d, k):
        return remote(kvw.at[d - 1, place, k], kvw.at[d, place, k], z_sems.at[0, d - 1, k], z_sems.at[1, d - 1, k], at(lax.rem(a + 1, A), b, c))

    def x_copy(d, shift, k):
        return remote(kvw.at[d, place, k], kvw.at[d, place, k], x_sems.at[0, d, shift, k], x_sems.at[1, d, shift, k], at(a, lax.rem(b + shift, B), c))

    def x_arrival(d, shift, k):
        other = lax.rem(b + B - shift, B)
        slot = kvw.at[d, 2 * other + c, k]
        return remote(slot, slot, x_sems.at[0, d, shift, k], x_sems.at[1, d, shift, k], at(a, other, c))

    def c_copy(d, column, k):
        slot = kvw.at[d, 2 * column + c, k]
        return remote(slot, slot, c_sems.at[0, d, column, k], c_sems.at[1, d, column, k], sibling)

    def c_arrival(d, column, k):
        slot = kvw.at[d, 2 * column + 1 - c, k]
        return remote(slot, slot, c_sems.at[0, d, column, k], c_sems.at[1, d, column, k], sibling)

    def x_needed(d, source, target):
        if d == 0:
            return target > source
        if d == 1:
            return target >= 0
        return target < source

    def c_needed(d, column, core):
        if d == 0:
            return jnp.logical_or(column < b, jnp.logical_and(column == b, core == 0))
        if d == 1:
            return column >= 0
        return jnp.logical_or(column > b, jnp.logical_and(column == b, core == 1))

    def when_all(*conditions):
        whole = conditions[0]
        for condition in conditions[1:]:
            whole = jnp.logical_and(whole, condition)
        return pl.when(whole)

    def spread(d, k):
        if d + 1 < WINDOW:
            @when_all(a + 1 < A, a >= d)
            def _():
                z_copy(d + 1, k).start()
        for shift in range(1, B):
            @when_all(a >= d, x_needed(d, b, lax.rem(b + shift, B)))
            def _():
                x_copy(d, shift, k).start()
        @when_all(a >= d, c_needed(d, b, c))
        def _():
            c_copy(d, b, k).start()

    def from_plane(d, k):
        @pl.when(a >= d)
        def _():
            z_arrival(d, k).wait_recv()
        spread(d, k)

    def z_arrival(d, k):
        slot = kvw.at[d, place, k]
        return remote(slot, slot, z_sems.at[0, d - 1, k], z_sems.at[1, d - 1, k], at(lax.rem(a + A - 1, A), b, c))

    def from_columns(d, k):
        for shift in range(1, B):
            other = lax.rem(b + B - shift, B)
            @when_all(a >= d, x_needed(d, other, b))
            def _():
                x_arrival(d, shift, k).wait_recv()
                c_copy(d, other, k).start()

    def from_sibling(d, k):
        def step(column, _):
            @when_all(a >= d, c_needed(d, column, 1 - c))
            def _():
                c_arrival(d, column, k).wait_recv()
            return 0
        lax.fori_loop(0, B, step, 0)

    def all_sent(k):
        for d in range(WINDOW):
            if d + 1 < WINDOW:
                @when_all(a + 1 < A, a >= d)
                def _():
                    z_copy(d + 1, k).wait_send()
            for shift in range(1, B):
                @when_all(a >= d, x_needed(d, b, lax.rem(b + shift, B)))
                def _():
                    x_copy(d, shift, k).wait_send()
            def step(column, _):
                @when_all(a >= d, c_needed(d, column, c))
                def _():
                    c_copy(d, column, k).wait_send()
                return 0
            lax.fori_loop(0, B, step, 0)

    def project(k):
        for piece in range(R // 128):
            rows = pl.ds(piece * 128, 128)
            x = x_all[k, rows].astype(F32)
            n = x * lax.rsqrt(jnp.mean(x * x, axis=1, keepdims=True) + EPS) * r["gain_one"][...]
            r["n_rows"][rows] = n.astype(BF16)
            n_t[:, k * R + piece * 128:k * R + (piece + 1) * 128] = jnp.transpose(n).astype(BF16)
        cos, sin = aux[k, 0:32], aux[k, 32:64]
        q_gain, k_gain = r["gain_columns"][0:64, 0:1], r["gain_columns"][64:128, 0:1]
        for h in range(KV):
            raw = jnp.transpose(dot(r["n_rows"][...], weight(p.qkv + h)))
            raws[k, h] = raw[0:192]
            q = raw[0:128].reshape(2, HEAD, R)
            q = q * lax.rsqrt(jnp.mean(q * q, axis=1, keepdims=True) + EPS) * q_gain
            q = rotate(q, cos, sin).astype(BF16)
            q_t[k, h, 0:64, 0:R] = q[0]
            q_t[k, h, 0:64, R:2 * R] = q[1]
            q_t[k, h, 64:128] = jnp.zeros((64, 2 * R), BF16)
            key = raw[128:192].reshape(1, HEAD, R)
            key = key * lax.rsqrt(jnp.mean(key * key, axis=1, keepdims=True) + EPS) * k_gain
            key = rotate(key, cos, sin).reshape(HEAD, R)
            kv = jnp.concatenate([key, raw[192:256]], axis=0)
            kvw[0, place, k, h] = jnp.transpose(kv).astype(BF16)

    def mask_of(k, key_start, diagonal):
        keys = lax.broadcasted_iota(jnp.int32, (R, 2 * R), 0)
        start = jnp.concatenate([aux[k, 64:65], aux[k, 64:65]], axis=1)
        allowed = (keys + key_start).astype(F32) >= start
        if diagonal:
            query = lax.broadcasted_iota(jnp.int32, (R, 2 * R), 1)
            query = jnp.where(query >= R, query - R, query)
            allowed = jnp.logical_and(allowed, keys <= query)
        return allowed

    def attend(d, other, k, diagonal=False):
        key_start = ((a - d) * 2 * B + other) * R
        allowed = mask_of(k, key_start, diagonal)
        for h in range(KV):
            kv = kvw[d, other, k, h]
            scores = dot(kv, q_t[k, h])
            weights = jnp.where(allowed, jnp.exp2(scores * EXP2_SCALE), 0.0).astype(BF16)
            values = jnp.concatenate([jnp.transpose(kv)[64:128], jnp.ones((16, R), BF16)], axis=0)
            added = dot(values, weights)
            if diagonal:
                o_acc[k, h] = added
            else:
                o_acc[k, h] += added

    def attended(d):
        if d == 0:
            return 0, place
        if d == 1:
            return 0, jnp.where(a >= 1, 2 * B, 0)
        return place, jnp.where(a >= 2, 2 * B, 0)

    def attend_plane(d, k):
        low, high = attended(d)
        def step(other, _):
            attend(d, other, k)
            return 0
        lax.fori_loop(low, high, step, 0)

    mixed = r["mixed"]
    y_send, y_recv, fo_send, fo_recv = r["y_send"], r["y_recv"], r["fo_send"], r["fo_recv"]
    part, out_acc, middle = r["part"], r["out_acc"], r["middle"]
    gains = r["gains"]

    def store_part(k, send, own, aa, value):
        columns = slice(aa * (D // A), (aa + 1) * (D // A))
        if k == 0:
            own[:, columns] = value
        else:
            send[k - 1, :, columns] = value.astype(BF16)

    def finish_heads(k):
        for h in range(KV):
            o = o_acc[k, h]
            o_n = o[0:64] / o[64:65]
            o_acc[k, h, 0:64] = o_n
            both = jnp.concatenate([o_n[:, 0:R], o_n[:, R:2 * R]], axis=0)
            mixed[k, :, 128 * h:128 * h + 128] = jnp.transpose(both).astype(BF16)

    def project_out(k):
        finish_heads(k)
        for aa in range(A):
            total = nt_dot(mixed[k, :, 0:TILE], weight_rows(p.out, aa))
            for t in range(1, p.no):
                total += nt_dot(mixed[k, :, t * TILE:(t + 1) * TILE], weight_rows(p.out + t, aa))
            store_part(k, y_send, part, aa, total)

    def load_scope(s_q, s_k, s_v, s_o):
        own_x = pltpu.make_async_copy(r["x"].at[0], x_all.at[0], local_sems.at[0])
        loads = [
            pltpu.make_async_copy(r[name], s, local_sems.at[2 + j])
            for j, (name, s) in enumerate((("w_query", s_q), ("w_key", s_k), ("w_value", s_v), ("w_out", s_o)))
        ]
        own_x.start()
        for load in loads:
            load.start()

        def cast_qkv(aa, _):
            rows = pl.ds(aa * (D // A), D // A)
            for h in range(KV):
                whole = jnp.concatenate(
                    [s_q[rows, 128 * h:128 * h + 128], s_k[rows, 64 * h:64 * h + 64], s_v[rows, 64 * h:64 * h + 64]], axis=1
                ).astype(BF16)
                wall[p.qkv + h, aa // 2, lax.rem(aa, 2)] = whole.reshape(B, 2, S, TILE)
            return 0

        def cast_out(aa, _):
            rows = pl.ds(aa * (D // A), D // A)
            for t in range(p.no):
                wall[p.out + t, aa // 2, lax.rem(aa, 2)] = s_o[rows, TILE * t:TILE * (t + 1)].astype(BF16).reshape(B, 2, S, TILE)
            return 0

        tables()
        own_x.wait()
        pl.semaphore_wait(barrier, len(peers))
        for k in others:
            gather(AG_AUX, aux, k).start()
            gather(AG_X, x_all, k).start()
        for load in loads[:3]:
            load.wait()
        lax.fori_loop(0, A, cast_qkv, 0)
        loads[3].wait()
        lax.fori_loop(0, A, cast_out, 0)

    def forward_scope(n_rows, stage, stage_sems):
        r["n_rows"] = n_rows
        own_dy = pltpu.make_async_copy(r["dy"].at[0], dy_all.at[0], local_sems.at[1])
        ff = (("w_gate", p.gate), ("w_up", p.up), ("w_down", p.down))
        slots = FF_SLOTS
        chunks = A * B * 2

        def ff_load(name, n):
            rows = pl.ds(n * S, S)
            return pltpu.make_async_copy(r[name].at[rows], stage.at[lax.rem(n, slots)], stage_sems.at[lax.rem(n, slots)])

        def prime(which):
            for n in range(slots - 1):
                ff_load(ff[which][0], n).start()

        def cast_ff(which):
            name, first = ff[which]
            def step(n, _):
                @pl.when(n + slots - 1 < chunks)
                def _():
                    ff_load(name, n + slots - 1).start()
                ff_load(name, n).wait()
                aa, bb, cc = n // (2 * B), lax.rem(n // 2, B), lax.rem(n, 2)
                for t in range(p.nt):
                    part_of = stage[lax.rem(n, slots), :, t * TILE:(t + 1) * TILE]
                    wall[first + t, aa // 2, lax.rem(aa, 2), bb, cc] = part_of.astype(BF16)
                return 0
            lax.fori_loop(0, chunks, step, 0)
            if which + 1 < len(ff):
                prime(which + 1)

        prime(0)
        own_dy.start()
        project(0)
        spread(0, 0)
        attend(0, place, 0, True)
        own_dy.wait()
        cast_ff(0)
        from_columns(0, 0)
        from_plane(1, 0)
        for k in others:
            gathered(AG_AUX, aux, k).wait_recv()
            gathered(AG_X, x_all, k).wait_recv()
            gather(AG_DY, dy_all, k).start()
            project(k)
            spread(0, k)
        from_columns(1, 0)
        from_plane(2, 0)
        for k in others:
            attend(0, place, k, True)
        from_sibling(0, 0)
        attend_plane(0, 0)
        for k in others:
            from_columns(0, k)
            from_plane(1, k)
        from_columns(2, 0)
        from_sibling(1, 0)
        attend_plane(1, 0)
        for k in others:
            from_columns(1, k)
            from_plane(2, k)
            from_sibling(0, k)
            attend_plane(0, k)
            from_sibling(1, k)
            attend_plane(1, k)
            from_columns(2, k)
            from_sibling(2, k)
            attend_plane(2, k)
            project_out(k)
            scatter(RS_P, y_send, y_recv, k).start()
        from_sibling(2, 0)
        attend_plane(2, 0)
        project_out(0)
        cast_ff(1)
        cast_ff(2)
        for k in range(G):
            all_sent(k)

    pl.run_scoped(
        load_scope,
        pltpu.VMEM((D, 128 * KV), F32),
        pltpu.VMEM((D, 64 * KV), F32),
        pltpu.VMEM((D, 64 * KV), F32),
        pltpu.VMEM((D, 128 * KV), F32),
    )
    pl.run_scoped(
        forward_scope,
        pltpu.VMEM((R, D), BF16),
        pltpu.VMEM((FF_SLOTS, S, p.FL), F32),
        pltpu.SemaphoreType.DMA((FF_SLOTS,)),
    )
    for k in others:
        gather(AG_X, x_all, k).wait_send()
        gather(AG_AUX, aux, k).wait_send()

    n2_all = gb_all = r["n2_all"]

    rc, r1, r2, r3 = r["rc"], r["r1"], r["r2"], r["r3"]
    w_sems = r["w_sems"]
    stage_c, fetch_sems = r["stage_c"], r["fetch_sems"]
    high, low = a // 2, lax.rem(a, 2)
    column_device = at(a, 1 - b, c)
    pair_device = at(2 * high + 1 - low, b, c)

    def sum_core(n):
        t, m = p.batches[n]
        source = wall.at[pl.ds(t, m), :, :, :, 1 - c]
        return remote(source, rc.at[pl.ds(t, m)], w_sems.at[0, 0, n], w_sems.at[1, 0, n], sibling)

    def sum_first(n):
        t, m = p.batches[n]
        if n in p.pair_first:
            source, device = wall.at[pl.ds(t, m), :, 1 - low, :, c], pair_device
        else:
            source, device = wall.at[pl.ds(t, m), :, :, 1 - b, c], column_device
        return remote(source, r1.at[pl.ds(t, m)], w_sems.at[0, 1, n], w_sems.at[1, 1, n], device)

    def sum_second(n):
        t, m = p.batches[n]
        if n in p.pair_first:
            source, device = wall.at[pl.ds(t, m), :, low, 1 - b, c], column_device
        else:
            source, device = wall.at[pl.ds(t, m), :, 1 - low, b, c], pair_device
        return remote(source, r2.at[pl.ds(t, m)], w_sems.at[0, 2, n], w_sems.at[1, 2, n], device)

    def sum_third(n):
        t, m = p.batches[n]
        source = wall.at[pl.ds(t, m), 1 - high, low, b, c]
        return remote(source, r3.at[pl.ds(t, m)], w_sems.at[0, 3, n], w_sems.at[1, 3, n], at(2 * (1 - high) + low, b, c))

    def fetch_core(n):
        t, m = p.batches[n]
        return pltpu.make_async_copy(rc.at[pl.ds(t, m)], stage_c.at[n % 2, pl.ds(0, m)], fetch_sems.at[n % 2])

    def step_core(n):
        sum_core(n).start()

    def step_fetch(n):
        sum_core(n).wait_recv()
        fetch_core(n).start()

    def step_first(n):
        t, m = p.batches[n]
        fetch_core(n).wait()
        def add(j, _):
            tile, hi, lo = j // A, lax.rem(j // 2, 2), lax.rem(j, 2)
            mine = wall[t + tile, hi, lo, :, c].astype(F32) + stage_c[n % 2, tile, hi, lo].astype(F32)
            wall[t + tile, hi, lo, :, c] = mine.astype(BF16)
            return 0
        lax.fori_loop(0, m * A, add, 0)
        sum_first(n).start()

    def step_second(n):
        t, m = p.batches[n]
        sum_first(n).wait_recv()
        def add(tile, _):
            if n in p.pair_first:
                mine = wall[t + tile, :, low, :, c].astype(F32) + r1[t + tile].astype(F32)
                wall[t + tile, :, low, :, c] = mine.astype(BF16)
            else:
                mine = wall[t + tile, :, :, b, c].astype(F32) + r1[t + tile].astype(F32)
                wall[t + tile, :, :, b, c] = mine.astype(BF16)
            return 0
        lax.fori_loop(0, m, add, 0)
        sum_second(n).start()

    def step_third(n):
        t, m = p.batches[n]
        sum_second(n).wait_recv()
        def add(tile, _):
            mine = wall[t + tile, :, low, b, c].astype(F32) + r2[t + tile].astype(F32)
            wall[t + tile, :, low, b, c] = mine.astype(BF16)
            return 0
        lax.fori_loop(0, m, add, 0)
        sum_third(n).start()

    out_stage, out_sems = r["out_stage"], r["out_sems"]

    def out_copy(n):
        t, m = p.batches[n]
        return pltpu.make_async_copy(out_stage.at[n % 2, pl.ds(0, m)], r["d_weights"].at[pl.ds(t, m)], out_sems.at[n % 2])

    out_order = []

    def step_out(n):
        t, m = p.batches[n]
        sum_third(n).wait_recv()
        for earlier in out_order:
            if earlier % 2 == n % 2:
                out_copy(earlier).wait()
        out_order[:] = [e for e in out_order if e % 2 != n % 2] + [n]
        def add(tile, _):
            out_stage[n % 2, tile] = wall[t + tile, high, low, b, c].astype(F32) + r3[t + tile].astype(F32)
            return 0
        lax.fori_loop(0, m, add, 0)
        out_copy(n).start()

    def feed_forward(hs, n2_t, dy_t):
        def turned(source, k, target):
            for piece in range(R // 128):
                rows = pl.ds(piece * 128, 128)
                target[:, k * R + piece * 128:k * R + (piece + 1) * 128] = jnp.transpose(source[k, rows].astype(F32)).astype(BF16)

        turned(dy_all, 0, dy_t)
        for k in others:
            gathered(AG_DY, dy_all, k).wait_recv()
            turned(dy_all, k, dy_t)
        for k in others:
            scattered(RS_P, y_send, y_recv, k).wait_recv()
        for piece in range(R // 128):
            rows = pl.ds(piece * 128, 128)
            v = x_all[0, rows].astype(F32) + part[rows]
            for k in others:
                v += y_recv[k - 1, rows].astype(F32)
            middle[rows] = v
            n2_all[0, rows] = (v * lax.rsqrt(jnp.mean(v * v, axis=1, keepdims=True) + EPS) * r["gain_two"][...]).astype(BF16)
        for k in others:
            gather(AG_N2, n2_all, k).start()
        turned(n2_all, 0, n2_t)

        def hidden(k):
            rows = slice(k * R, (k + 1) * R)
            def step(t, _):
                gate = dot(n2_all[k], weight(p.gate + t))
                up = dot(n2_all[k], weight(p.up + t))
                grad = dot(dy_all[k], weight(p.down + t))
                sig = 1.0 / (1.0 + jnp.exp(-gate))
                silu = gate * sig
                hs[2, t, rows] = (silu * up).astype(BF16)
                hs[0, t, rows] = (grad * up * (sig * (1.0 + gate * (1.0 - sig)))).astype(BF16)
                hs[1, t, rows] = (grad * silu).astype(BF16)
                return 0
            lax.fori_loop(0, p.nt, step, 0)

        def back_normed(k):
            rows = slice(k * R, (k + 1) * R)
            for aa in range(A):
                total = jnp.zeros((R, D // A), F32)
                for t in range(p.nt):
                    total += nt_dot(hs[0, t, rows], weight_rows(p.gate + t, aa))
                    total += nt_dot(hs[1, t, rows], weight_rows(p.up + t, aa))
                store_part(k, y_send, part, aa, total)

        def down(k):
            rows = slice(k * R, (k + 1) * R)
            for aa in range(A):
                total = jnp.zeros((R, D // A), F32)
                for t in range(p.nt):
                    total += nt_dot(hs[2, t, rows], weight_rows(p.down + t, aa))
                if k == 0:
                    columns = slice(aa * (D // A), (aa + 1) * (D // A))
                    out_acc[:, columns] = middle[:, columns] + total
                else:
                    store_part(k, fo_send, None, aa, total)

        hidden(0)
        back_normed(0)
        down(0)
        for k in others:
            scatter(RS_P, y_send, y_recv, k).wait_send()
            gathered(AG_N2, n2_all, k).wait_recv()
            turned(n2_all, k, n2_t)
            hidden(k)
            back_normed(k)
            scatter(RS_GN2, y_send, y_recv, k).start()

        def weight_gradients(n):
            t, m = p.batches[n]
            for tile in range(t, t + m):
                kind, u = tile // p.nt, tile % p.nt
                left = dy_t if kind == 2 else n2_t
                for aa in range(A):
                    rows = slice(aa * (D // A), (aa + 1) * (D // A))
                    wall[tile, aa // 2, aa % 2] = dot(left[rows], hs[kind, u]).astype(BF16).reshape(B, 2, S, TILE)

        begun = False
        for n in range(p.ff_batches):
            t, m = p.batches[n]
            if t + m > p.down and not begun:
                begun = True
                for k in others:
                    down(k)
            weight_gradients(n)
            step_core(n)
            if 2 <= n <= 5:
                step_fetch(n - 2)
            if 3 <= n <= 6:
                step_first(n - 3)
        step_fetch(4)

    pl.run_scoped(
        feed_forward,
        pltpu.VMEM((3, p.nt, G * R, TILE), BF16),
        pltpu.VMEM((D, G * R), BF16),
        pltpu.VMEM((D, G * R), BF16),
    )
    last = p.ff_batches

    gb_t = r["gb_t"]
    for k in others:
        scattered(RS_GN2, y_send, y_recv, k).wait_recv()
    gain_grad = jnp.zeros((1, D), F32)
    for piece in range(R // 128):
        rows = pl.ds(piece * 128, 128)
        e = part[rows]
        for k in others:
            e += y_recv[k - 1, rows].astype(F32)
        v = middle[rows]
        rr = lax.rsqrt(jnp.mean(v * v, axis=1, keepdims=True) + EPS)
        vh = v * rr
        gain_grad += jnp.sum(e * vh, axis=0, keepdims=True)
        ge = e * r["gain_two"][...]
        gm = dy_all[0, rows].astype(F32) + rr * (ge - vh * jnp.mean(vh * ge, axis=1, keepdims=True))
        middle[rows] = gm
        gb_t[:, piece * 128:(piece + 1) * 128] = jnp.transpose(gm).astype(BF16)
    gains[...] = jnp.zeros((8, D), F32)
    gains[0:1] = gain_grad
    for k in others:
        gather(AG_N2, n2_all, k).wait_send()
    gb_all[0] = middle[...].astype(BF16)
    for k in others:
        gather(AG_GB, gb_all, k).start()
    step_fetch(5)

    dm = r["dm"]
    graw = r["graw"]
    kvr, xr, zr = r["kvr"], r["xr"], r["zr"]
    kc_sems, kx_sems, kz_sems = r["kc_sems"], r["kx_sems"], r["kz_sems"]
    head_sums = r["head_sums"]
    head_sums[...] = jnp.zeros((128, R), F32)

    def mixed_gradient(k):
        for t in range(p.no):
            dm[:, t * TILE:(t + 1) * TILE] = dot(gb_all[k], weight(p.out + t)).astype(BF16)

    def k_core(d, column, k):
        return remote(kvw.at[d, 2 * column + 1 - c, k], kvr.at[d, column, k], kc_sems.at[0, d, column, k], kc_sems.at[1, d, column, k], sibling)

    def k_column(d, shift, k):
        target = lax.rem(b + shift, B)
        return remote(kvw.at[d, 2 * target + c, k], xr.at[d, shift - 1, k], kx_sems.at[0, d, shift, k], kx_sems.at[1, d, shift, k], at(a, target, c))

    def k_plane(d, k):
        return remote(kvw.at[d, place, k], zr.at[d - 1, k], kz_sems.at[0, d - 1, k], kz_sems.at[1, d - 1, k], at(lax.rem(a + A - 1, A), b, c))

    def in_window(d, column, core, from_core):
        if d == 0:
            return jnp.logical_or(column < b, jnp.logical_and(column == b, core <= from_core))
        if d == 1:
            return column >= 0
        return jnp.logical_or(column > b, jnp.logical_and(column == b, core >= from_core))

    def column_reached(d, target, source):
        if d == 0:
            return target < source
        if d == 1:
            return target >= 0
        return target > source

    def keys_core(d, k):
        for column in range(B):
            @when_all(a >= d, in_window(d, column, 1 - c, c))
            def _():
                k_core(d, column, k).start()

    def keys_add(d, k, kv_stage, kv_sems):
        def fetch(column):
            return pltpu.make_async_copy(kvr.at[d, column, k], kv_stage.at[column], kv_sems.at[column])

        for column in range(B):
            @when_all(a >= d, in_window(d, column, c, 1 - c))
            def _():
                k_core(d, column, k).wait_recv()
                fetch(column).start()
        for column in range(B):
            @when_all(a >= d, in_window(d, column, c, 1 - c))
            def _():
                fetch(column).wait()
                for h in range(KV):
                    slot = 2 * column + c
                    kvw[d, slot, k, h] = (kvw[d, slot, k, h].astype(F32) + kv_stage[column, h].astype(F32)).astype(BF16)
        for shift in range(1, B):
            @when_all(a >= d, column_reached(d, lax.rem(b + shift, B), b))
            def _():
                k_column(d, shift, k).start()

    def keys_columns(d, k):
        for shift in range(1, B):
            @when_all(a >= d, column_reached(d, b, lax.rem(b + B - shift, B)))
            def _():
                k_column(d, shift, k).wait_recv()
                for h in range(KV):
                    kvw[d, place, k, h] = (kvw[d, place, k, h].astype(F32) + xr[d, shift - 1, k, h].astype(F32)).astype(BF16)

    def keys_plane(d, k):
        @pl.when(a >= d)
        def _():
            k_plane(d, k).start()

    def keys_from_plane(d, k):
        @when_all(a + 1 < A, a + 1 >= d)
        def _():
            k_plane(d, k).wait_recv()
            for h in range(KV):
                kvw[d - 1, place, k, h] = (kvw[d - 1, place, k, h].astype(F32) + zr[d - 1, k, h].astype(F32)).astype(BF16)

    def keys_sent(k):
        for d in range(WINDOW):
            for column in range(B):
                @when_all(a >= d, in_window(d, column, 1 - c, c))
                def _():
                    k_core(d, column, k).wait_send()
            for shift in range(1, B):
                @when_all(a >= d, column_reached(d, lax.rem(b + shift, B), b))
                def _():
                    k_column(d, shift, k).wait_send()
            if d:
                @pl.when(a >= d)
                def _():
                    k_plane(d, k).wait_send()

    def rms_back(raw, e, gain):
        rr = lax.rsqrt(jnp.mean(raw * raw, axis=1, keepdims=True) + EPS)
        vh = raw * rr
        ge = e * gain
        return jnp.sum(e * vh, axis=0), rr * (ge - vh * jnp.mean(vh * ge, axis=1, keepdims=True))

    def attention_back(k, do_t, do_rows, q_rows, dq, rows_of, between):
        mixed_gradient(k)
        for h in range(KV):
            turned = jnp.transpose(dm[:, 128 * h:128 * h + 128].astype(F32))
            grad = jnp.concatenate([turned[0:64], turned[64:128]], axis=1)
            rows_of[h, 0:1] = jnp.log2(o_acc[k, h, 64:65])
            rows_of[h, 1:2] = jnp.sum(grad * o_acc[k, h, 0:64], axis=0, keepdims=True)
            padded = jnp.concatenate([jnp.zeros((64, 2 * R), F32), grad], axis=0)
            do_t[h] = padded.astype(BF16)
            do_rows[h] = jnp.transpose(padded).astype(BF16)
            q_rows[h] = (jnp.transpose(q_t[k, h].astype(F32)) * (1.0 / math.sqrt(HEAD))).astype(BF16)

        def block(d, other, diagonal=False):
            key_start = ((a - d) * 2 * B + other) * R
            allowed = mask_of(k, key_start, diagonal)
            for h in range(KV):
                kv = kvw[d, other, k, h]
                scores = dot(kv, q_t[k, h])
                probs = jnp.where(allowed, jnp.exp2(scores * EXP2_SCALE - rows_of[h, 0:1]), 0.0)
                grad = dot(kv, do_t[h])
                grad_scores = (probs * (grad - rows_of[h, 1:2])).astype(BF16)
                kvw[d, other, k, h] = (dot(grad_scores, q_rows[h]) + dot(probs.astype(BF16), do_rows[h])).astype(BF16)
                keys = jnp.transpose(kv)[0:64]
                if diagonal:
                    dq[h] = dot(keys, grad_scores)
                else:
                    dq[h] += dot(keys, grad_scores)

        def plane(d):
            low, high = attended(d)
            def step(other, _):
                block(d, other)
                return 0
            lax.fori_loop(low, high, step, 0)

        block(0, place, True)
        plane(2)
        keys_core(2, k)
        between(0)
        plane(1)
        keys_core(1, k)
        between(1)
        plane(0)
        keys_core(0, k)
        between(2)
        cos, sin = aux[k, 0:32], aux[k, 32:64]
        for h in range(KV):
            e = (dq[h] * (1.0 / math.sqrt(HEAD))).astype(BF16).astype(F32)
            e = rotate_back(jnp.stack([e[:, 0:R], e[:, R:2 * R]]), cos, sin)
            gain_part, grad = rms_back(raws[k, h, 0:128].reshape(2, HEAD, R), e, r["gain_columns"][0:64, 0:1])
            head_sums[0:64] += gain_part
            graw[h, k * R:(k + 1) * R, 0:128] = jnp.transpose(grad.reshape(128, R)).astype(BF16)

    def keys_back(k):
        cos, sin = aux[k, 0:32], aux[k, 32:64]
        for h in range(KV):
            final = jnp.transpose(kvw[0, place, k, h].astype(F32))
            e = rotate_back(final[0:64].reshape(1, HEAD, R), cos, sin)
            gain_part, grad = rms_back(raws[k, h, 128:192].reshape(1, HEAD, R), e, r["gain_columns"][64:128, 0:1])
            head_sums[64:128] += gain_part
            both = jnp.concatenate([grad.reshape(HEAD, R), final[64:128]], axis=0)
            graw[h, k * R:(k + 1) * R, 128:256] = jnp.transpose(both).astype(BF16)

    xg = r["xg"]

    def input_gradient(k):
        for aa in range(A):
            columns = slice(aa * (D // A), (aa + 1) * (D // A))
            total = jnp.zeros((R, D // A), F32)
            for h in range(KV):
                total += nt_dot(graw[h, k * R:(k + 1) * R], weight_rows(p.qkv + h, aa))
            store_part(k, y_send, part, aa, total)
            x = x_all[k, :, columns].astype(F32)
            xg[:, columns] += jnp.sum(total * x * x_scale(k), axis=0, keepdims=True)

    def x_scale(k):
        return r["x_scale"][k, :, 0:1]

    def backward_scope(do_t, do_rows, q_rows, dq, rows_of, kv_stage, kv_sems):
        def first(n):
            if n == 0:
                step_first(4)
                step_fetch(6)
            elif n == 1:
                keys_add(2, 0, kv_stage, kv_sems)
                step_first(5)
                step_fetch(7)
            else:
                keys_add(1, 0, kv_stage, kv_sems)
                step_second(0)
                step_second(1)

        attention_back(0, do_t, do_rows, q_rows, dq, rows_of, first)
        keys_add(0, 0, kv_stage, kv_sems)
        for k in others:
            gathered(AG_GB, gb_all, k).wait_recv()
            scatter(RS_FO, fo_send, fo_recv, k).start()
            for piece in range(R // 128):
                rows = pl.ds(piece * 128, 128)
                gb_t[:, k * R + piece * 128:k * R + (piece + 1) * 128] = jnp.transpose(gb_all[k, rows].astype(F32)).astype(BF16)

        def second(k, n):
            if n == 0:
                keys_columns(2, 0)
                keys_plane(2, 0)
                step_second(2)
                step_second(3)
                step_first(6)
                step_fetch(8)
            elif n == 1:
                keys_add(2, k, kv_stage, kv_sems)
                keys_columns(1, 0)
                keys_columns(0, 0)
            else:
                keys_add(1, k, kv_stage, kv_sems)
                keys_from_plane(2, 0)
                keys_plane(1, 0)
                step_second(4)
                step_third(0)
                step_third(1)

        for k in others:
            attention_back(k, do_t, do_rows, q_rows, dq, rows_of, functools.partial(second, k))
            keys_add(0, k, kv_stage, kv_sems)
        step_first(7)
        for t in range(p.no):
            for aa in range(A):
                rows = slice(aa * (D // A), (aa + 1) * (D // A))
                total = jnp.zeros((D // A, TILE), F32)
                for k in range(G):
                    total += dot(gb_t[rows, k * R:(k + 1) * R], mixed[k, :, t * TILE:(t + 1) * TILE])
                wall[p.out + t, aa // 2, aa % 2] = total.astype(BF16).reshape(B, 2, S, TILE)
        step_core(last)
        for k in others:
            keys_columns(2, k)
            keys_plane(2, k)
        step_second(5)
        step_third(2)
        step_third(3)
        keys_from_plane(1, 0)
        keys_back(0)
        for k in others:
            keys_columns(1, k)
            keys_from_plane(2, k)
            keys_plane(1, k)
        step_second(6)
        step_first(8)
        step_fetch(last)
        for k in others:
            keys_columns(0, k)
        step_third(4)
        step_out(0)
        step_out(1)
        for k in others:
            keys_from_plane(1, k)
            keys_back(k)

    pl.run_scoped(
        backward_scope,
        pltpu.VMEM((KV, 128, 2 * R), BF16),
        pltpu.VMEM((KV, 2 * R, 128), BF16),
        pltpu.VMEM((KV, 2 * R, 128), BF16),
        pltpu.VMEM((KV, 64, 2 * R), F32),
        pltpu.VMEM((KV, 8, 2 * R), F32),
        pltpu.VMEM((B, KV, R, 128), BF16),
        pltpu.SemaphoreType.DMA((B,)),
    )

    xg[...] = jnp.zeros((1, D), F32)
    for k in range(G):
        x = x_all[k].astype(F32)
        r["x_scale"][k] = jnp.broadcast_to(lax.rsqrt(jnp.mean(x * x, axis=1, keepdims=True) + EPS), (R, 128))
    for k in others:
        scatter(RS_GN2, y_send, y_recv, k).wait_send()
        input_gradient(k)
        scatter(RS_GN, y_send, y_recv, k).start()
    input_gradient(0)
    gains[1:2] = xg[...]
    sums = jnp.sum(jnp.transpose(head_sums[...]), axis=0, keepdims=True)
    gains[2:3, 0:128] = sums
    g_land, g_sems = r["g_land"], r["g_sems"]
    stages = [
        (2, c, 0, lambda j: at(a, b, j)),
        (B, b, 2, lambda j: at(a, j, c)),
        (A, a, 2 + B, lambda j: at(j, b, c)),
        (G, f, 2 + B + A, lambda j: (i, j)),
    ]

    def gain_send(s, shift):
        size, mine, base, device = stages[s]
        return remote(gains, g_land.at[base + mine], g_sems.at[0, s, shift], g_sems.at[1, s, shift], device(lax.rem(mine + shift, size)))

    def gain_arrival(s, shift):
        size, mine, base, device = stages[s]
        slot = lax.rem(mine + size - shift, size)
        return remote(gains, g_land.at[base + slot], g_sems.at[0, s, shift], g_sems.at[1, s, shift], device(slot))

    def gain_start(s):
        size, mine, base, _ = stages[s]
        for shift in range(1, size):
            gain_send(s, shift).start()
        g_land[base + mine] = gains[...]

    def gain_finish(s):
        size, _, base, _ = stages[s]
        for shift in range(1, size):
            gain_arrival(s, shift).wait_recv()
            gain_send(s, shift).wait_send()
        total = g_land[base]
        for j in range(1, size):
            total += g_land[base + j]
        gains[...] = total

    gain_start(0)
    for n in (last + 1, last + 2):
        t, m = p.batches[n]
        for tile in range(t, t + m):
            for aa in range(A):
                rows = slice(aa * (D // A), (aa + 1) * (D // A))
                wall[tile, aa // 2, aa % 2] = dot(n_t[rows], graw[tile - p.qkv]).astype(BF16).reshape(B, 2, S, TILE)
        step_core(n)

    gain_finish(0)
    gain_start(1)
    step_first(last)
    for n in (last + 1, last + 2):
        step_fetch(n)
        step_first(n)
    step_second(7)
    step_third(5)
    step_third(6)
    step_out(2)
    step_out(3)
    step_second(8)
    for k in others:
        scattered(RS_FO, fo_send, fo_recv, k).wait_recv()
    for piece in range(R // 128):
        rows = pl.ds(piece * 128, 128)
        v = out_acc[rows]
        for k in others:
            v += fo_recv[k - 1, rows].astype(F32)
        r["block_out"][0, rows] = v.astype(BF16)
    gain_finish(1)
    gain_start(2)
    step_third(7)
    step_out(4)
    step_out(5)
    step_second(last)
    for k in others:
        scattered(RS_GN, y_send, y_recv, k).wait_recv()
    for piece in range(R // 128):
        rows = pl.ds(piece * 128, 128)
        e = part[rows]
        for k in others:
            e += y_recv[k - 1, rows].astype(F32)
        v = x_all[0, rows].astype(F32)
        rr = r["x_scale"][0, rows, 0:1]
        vh = v * rr
        ge = e * r["gain_one"][...]
        back = rr * (ge - vh * jnp.mean(vh * ge, axis=1, keepdims=True))
        r["grad_inputs"][0, rows] = (middle[rows] + back).astype(BF16)
    gain_finish(2)
    gain_start(3)
    step_third(8)
    step_second(last + 1)
    step_out(6)
    step_out(7)
    step_third(last)
    step_second(last + 2)
    step_out(8)
    step_third(last + 1)
    step_out(last)
    gain_finish(3)
    r["d_gains"][...] = gains[...]
    step_third(last + 2)
    step_out(last + 1)
    step_out(last + 2)
    for n in out_order:
        out_copy(n).wait()

    for k in range(G):
        keys_sent(k)
    for k in others:
        gather(AG_DY, dy_all, k).wait_send()
        gather(AG_GB, gb_all, k).wait_send()
        scatter(RS_FO, fo_send, fo_recv, k).wait_send()
        scatter(RS_GN, y_send, y_recv, k).wait_send()
    for n in range(len(p.batches)):
        sum_core(n).wait_send()
        sum_first(n).wait_send()
        sum_second(n).wait_send()
        sum_third(n).wait_send()


def local(p, x, dy, lengths, gain_one, gain_two, query_gain, key_gain, wq, wk, wv, wo, wg, wu, wd):
    A, B, G, R, D, KV, S = p.A, p.B, p.G, p.R, p.D, p.KV, p.S
    any_spec, vmem, smem = (pl.BlockSpec(memory_space=m) for m in (pl.ANY, pltpu.VMEM, pltpu.SMEM))
    ins = dict(
        x=(x, any_spec), dy=(dy, any_spec), lengths=(lengths, smem), gain_one=(gain_one[None], vmem),
        gain_two=(gain_two[None], vmem), query_gain=(query_gain[None], vmem), key_gain=(key_gain[None], vmem),
        w_query=(wq, any_spec), w_key=(wk, any_spec), w_value=(wv, any_spec), w_out=(wo, any_spec),
        w_gate=(wg, any_spec), w_up=(wu, any_spec), w_down=(wd, any_spec),
    )
    rows_out = ((1, R, D), BF16)
    outs = dict(
        block_out=rows_out, grad_inputs=rows_out, d_gains=((8, D), F32),
    )
    landing = dict(
        d_weights=((p.tiles, S, TILE), F32), rc=((p.tiles, 2, 2, B, S, TILE), BF16), kvr=((WINDOW, B, G, KV, R, 128), BF16),
    )
    DMA = pltpu.SemaphoreType.DMA
    n_batches, widest = len(p.batches), max(m for _, m in p.batches)
    scratch = dict(
        x_all=pltpu.VMEM((G, R, D), BF16), aux=pltpu.VMEM((G, 72, R), F32), dy_all=pltpu.VMEM((G, R, D), BF16),
        y_sems=DMA((9, 2, G)), local_sems=DMA((8,)),
        gain_columns=pltpu.VMEM((128, 128), F32),
        kvw=pltpu.VMEM((WINDOW, 2 * B, G, KV, R, 128), BF16),
        z_sems=DMA((2, 2, G)), x_sems=DMA((2, WINDOW, B, G)), c_sems=DMA((2, WINDOW, B, G)),
        wall=pltpu.VMEM((p.tiles, 2, 2, B, 2, S, TILE), BF16),
        n_t=pltpu.VMEM((D, G * R), BF16),
        raws=pltpu.VMEM((G, KV, 192, R), F32), q_t=pltpu.VMEM((G, KV, 128, 2 * R), BF16),
        o_acc=pltpu.VMEM((G, KV, 80, 2 * R), F32), mixed=pltpu.VMEM((G, R, p.HQ), BF16),
        y_send=pltpu.VMEM((G - 1, R, D), BF16), y_recv=pltpu.VMEM((G - 1, R, D), BF16),
        fo_send=pltpu.VMEM((G - 1, R, D), BF16), fo_recv=pltpu.VMEM((G - 1, R, D), BF16),
        part=pltpu.VMEM((R, D), F32), out_acc=pltpu.VMEM((R, D), F32), middle=pltpu.VMEM((R, D), F32),
        n2_all=pltpu.VMEM((G, R, D), BF16), gb_t=pltpu.VMEM((D, G * R), BF16),
        gains=pltpu.VMEM((8, D), F32), xg=pltpu.VMEM((1, D), F32), x_scale=pltpu.VMEM((G, R, 128), F32),
        w_sems=DMA((2, 4, n_batches)), fetch_sems=DMA((2,)), stage_c=pltpu.VMEM((2, widest, 2, 2, B, S, TILE), BF16),
        r1=pltpu.VMEM((p.tiles, 2, 2, S, TILE), BF16), r2=pltpu.VMEM((p.tiles, 2, S, TILE), BF16),
        r3=pltpu.VMEM((p.tiles, S, TILE), BF16), out_stage=pltpu.VMEM((2, widest, S, TILE), F32), out_sems=DMA((2,)),
        dm=pltpu.VMEM((R, p.HQ), BF16), graw=pltpu.VMEM((KV, G * R, TILE), BF16),
        xr=pltpu.VMEM((WINDOW, B - 1, G, KV, R, 128), BF16), zr=pltpu.VMEM((2, G, KV, R, 128), BF16),
        kc_sems=DMA((2, WINDOW, B, G)), kx_sems=DMA((2, WINDOW, B, G)), kz_sems=DMA((2, 2, G)),
        head_sums=pltpu.VMEM((128, R), F32),
        g_land=pltpu.VMEM((2 + B + A + G, 8, D), F32), g_sems=DMA((2, 4, max(A, B, G, 2))),
    )
    outs_all = dict(outs, **landing)
    out_specs = [vmem for _ in outs] + [any_spec for _ in landing]
    names = list(ins) + list(outs_all) + list(scratch)
    results = pl.pallas_call(
        functools.partial(kernel, p, names),
        out_shape=[jax.ShapeDtypeStruct(*o) for o in outs_all.values()],
        in_specs=[s for _, s in ins.values()],
        out_specs=out_specs,
        scratch_shapes=list(scratch.values()),
        compiler_params=pltpu.CompilerParams(collective_id=0, has_side_effects=True, vmem_limit_bytes=64 << 20),
        name="block",
    )(*[v for v, _ in ins.values()])
    o = dict(zip(outs_all, results))
    packed = [o[name] for name in ("block_out", "grad_inputs", "d_gains", "d_weights")]
    shapes = [(packed[0].shape, BF16), (packed[0].shape, BF16), ((D,), F32), ((D,), F32), ((HEAD,), F32), ((HEAD,), F32)]
    shapes += [((S, n), F32) for n in (128 * KV, 64 * KV, 64 * KV, 128 * KV, p.FL, p.FL, p.FL)]
    return pl.pallas_call(
        functools.partial(split_kernel, p),
        out_shape=[jax.ShapeDtypeStruct(*shape) for shape in shapes],
        in_specs=[vmem] * len(packed),
        out_specs=[vmem] * len(shapes),
        name="split",
    )(*packed)


def split_kernel(p, out_in, grad_in, gains, tiles, block_out, grad_inputs, g_one, g_two, g_query, g_key, d_query, d_key, d_value, d_out, d_gate, d_up, d_down):
    block_out[...] = out_in[...]
    grad_inputs[...] = grad_in[...]
    g_one[...] = gains[1]
    g_two[...] = gains[0]
    g_query[...] = gains[2, 0:HEAD]
    g_key[...] = gains[2, HEAD:2 * HEAD]
    for ref, first, count in ((d_gate, p.gate, p.nt), (d_up, p.up, p.nt), (d_down, p.down, p.nt), (d_out, p.out, p.no)):
        for t in range(count):
            ref[:, t * TILE:(t + 1) * TILE] = tiles[first + t]
    for h in range(p.KV):
        tile = tiles[p.qkv + h]
        d_query[:, 128 * h:128 * h + 128] = tile[:, 0:128]
        d_key[:, 64 * h:64 * h + 64] = tile[:, 128:192]
        d_value[:, 64 * h:64 * h + 64] = tile[:, 192:256]


QUERY_HEADS = 16
KEY_VALUE_HEADS = 8
HEAD_SIZE = HEAD


MASKED_FILL = -1e30


def swapped(value, axis, bit):
    mask = 2**bit
    pairs = [(source, source ^ mask) for source in range(lax.axis_size(axis))]
    return lax.ppermute(value, axis, pairs)


def root_mean_norm(values, gain):
    return values * lax.rsqrt(jnp.mean(values * values, axis=-1, keepdims=True) + EPS) * gain


def apply_rotary(values, cosine_table, sine_table):
    half_width = values.shape[-1] // 2
    turned = jnp.concatenate([-values[..., half_width:], values[..., :half_width]], axis=-1)
    return values * cosine_table + turned * sine_table


def places(lengths, where):
    ends = jnp.cumsum(lengths)
    before = (ends[None, :] <= where[:, None]).astype(jnp.int32)
    segment = jnp.sum(before, axis=1)
    offset = where - jnp.sum(before * lengths[None, :], axis=1)
    return (segment, offset)


def head_post(query_raw, unrotated_key, query_gain, key_norm_gain, cosine_table, sine_table):
    token_count = query_raw.shape[0]
    query_rot = apply_rotary(
        root_mean_norm(query_raw.reshape(token_count, QUERY_HEADS, HEAD_SIZE), query_gain),
        cosine_table,
        sine_table,
    )
    rotated_key = apply_rotary(
        root_mean_norm(
            unrotated_key.reshape(token_count, KEY_VALUE_HEADS, HEAD_SIZE), key_norm_gain
        ),
        cosine_table,
        sine_table,
    )
    return (query_rot, rotated_key)


def swiglu(gate, upward):
    return jax.nn.silu(gate) * upward


def matmul(left, right):
    return jnp.dot(left, right, preferred_element_type=jnp.float32)


def project_back(left, right):
    return lax.dot_general(
        left, right, (((1,), (1,)), ((), ())), preferred_element_type=jnp.float32
    )


def outer_sum(left, right):
    return lax.dot_general(
        left, right, (((0,), (0,)), ((), ())), preferred_element_type=jnp.float32
    )


def mirror_out(payload, steps):
    for bit in range(steps):
        payload = swapped(payload, "ctx", bit)
    return payload


def mirror_back(payload, steps):
    for bit in range(steps):
        payload = swapped(payload, "ctx", bit)
    return payload


def halves_order(array, parts):
    shaped = array.reshape((parts, 2, array.shape[0] // (2 * parts)) + array.shape[1:])
    return jnp.stack([shaped[:, 0], shaped[::-1, 1]], axis=1).reshape(array.shape)


def general(
    inputs,
    cotangent,
    lengths,
    gain_one,
    gain_two,
    query_gain,
    key_norm_gain,
    w_query,
    key_projection,
    value_projection,
    w_out,
    w_gate,
    w_up,
    w_down,
):
    brain_float = jnp.bfloat16
    parts = lax.axis_size("ctx")
    steps = parts.bit_length() - 1
    device_index = lax.axis_index("ctx")
    row_count = inputs.shape[1]
    head_group = row_count * parts
    half_width = row_count // 2
    own_lengths = lengths[0]
    offsets_half = jnp.arange(half_width, dtype=jnp.int32)
    arrived = mirror_out(jnp.stack([inputs[0][half_width:], cotangent[0][half_width:]]), steps)
    x_rows = jnp.concatenate([inputs[0][:half_width], arrived[0]], axis=0)
    dy_rows = jnp.concatenate([cotangent[0][:half_width], arrived[1]], axis=0)
    query_place = jnp.concatenate(
        [
            device_index * row_count + offsets_half,
            (parts - 1 - device_index) * row_count + half_width + offsets_half,
        ]
    )
    key_place = jnp.arange(head_group, dtype=jnp.int32)
    query_segment, query_offset = places(own_lengths, query_place)
    key_segment, key_offset = places(own_lengths, key_place)
    weight_query, weight_key, weight_value, weight_out = (
        lax.all_gather(w_query.astype(brain_float), "fsdp", axis=1, tiled=True),
        lax.all_gather(key_projection.astype(brain_float), "fsdp", axis=1, tiled=True),
        lax.all_gather(value_projection.astype(brain_float), "fsdp", axis=1, tiled=True),
        lax.all_gather(w_out.astype(brain_float), "fsdp", axis=1, tiled=True),
    )
    x_float = x_rows.astype(jnp.float32)
    normed_f, norm_one_back = jax.vjp(root_mean_norm, x_float, gain_one)
    normed_input = normed_f.astype(brain_float)
    query_raw = matmul(normed_input, weight_query)
    unrotated_key = matmul(normed_input, weight_key)
    value_b = matmul(normed_input, weight_value).astype(brain_float)
    freq = jnp.exp(
        jnp.arange(HEAD_SIZE // 2, dtype=jnp.float32) * (-2.0 * math.log(THETA) / HEAD_SIZE)
    )
    angle = query_offset.astype(jnp.float32)[:, None] * freq[None, :]
    cosine_table = jnp.concatenate([jnp.cos(angle), jnp.cos(angle)], axis=-1)[:, None, :]
    sine_table = jnp.concatenate([jnp.sin(angle), jnp.sin(angle)], axis=-1)[:, None, :]

    def post_local(query_in, key_in, gain_q, gain_k):
        return head_post(query_in, key_in, gain_q, gain_k, cosine_table, sine_table)

    (query_rot, rotated_key), post_back = jax.vjp(
        post_local, query_raw, unrotated_key, query_gain, key_norm_gain
    )
    query_batch = query_rot.astype(brain_float)
    key_batch = rotated_key.astype(brain_float).reshape(row_count, KEY_VALUE_HEADS * HEAD_SIZE)
    gathered_keys, gathered_values = (
        lax.all_gather(key_batch, "ctx", axis=0, tiled=True),
        lax.all_gather(value_b, "ctx", axis=0, tiled=True),
    )
    gathered_keys = halves_order(gathered_keys, parts)
    gathered_values = halves_order(gathered_values, parts)
    shared_heads = QUERY_HEADS // KEY_VALUE_HEADS
    score_scale = 1.0 / math.sqrt(HEAD_SIZE)
    keys_per_block = min(1024, head_group)
    block_count = head_group // keys_per_block
    query_quad = query_batch.reshape(row_count, KEY_VALUE_HEADS, shared_heads, HEAD_SIZE)
    blocked_keys = gathered_keys.reshape(block_count, keys_per_block, KEY_VALUE_HEADS, HEAD_SIZE)
    blocked_values = gathered_values.reshape(
        block_count, keys_per_block, KEY_VALUE_HEADS, HEAD_SIZE
    )
    segment_blocks = key_segment.reshape(block_count, keys_per_block)
    place_blocks = key_place.reshape(block_count, keys_per_block)

    def tile_backward(query_tile, tile_segment, tile_place, tile_log, grad_tile, tile_delta):

        def allowed_of(segment_block, place_block):
            return (tile_segment[:, None] == segment_block[None, :]) & (
                tile_place[:, None] >= place_block[None, :]
            )

        def back_step(carry, block):
            key_block, value_block, segment_block, place_block = block
            allowed = allowed_of(segment_block, place_block)

            def back_active(grad_query):
                raw_scores = (
                    jnp.einsum(
                        "qhgd,khd->hgqk", query_tile, key_block, preferred_element_type=jnp.float32
                    )
                    * score_scale
                )
                probs = jnp.exp(
                    jnp.where(allowed[None, None], raw_scores, MASKED_FILL) - tile_log[..., None]
                )
                grad_probs = jnp.einsum(
                    "qhgd,khd->hgqk", grad_tile, value_block, preferred_element_type=jnp.float32
                )
                grad_scores = (probs * (grad_probs - tile_delta[..., None])).astype(brain_float)
                grad_query = grad_query + jnp.einsum(
                    "hgqk,khd->qhgd", grad_scores, key_block, preferred_element_type=jnp.float32
                )
                grad_key_block = jnp.einsum(
                    "hgqk,qhgd->khd", grad_scores, query_tile, preferred_element_type=jnp.float32
                )
                grad_value_block = jnp.einsum(
                    "hgqk,qhgd->khd",
                    probs.astype(brain_float),
                    grad_tile,
                    preferred_element_type=jnp.float32,
                )
                return (grad_query, (grad_key_block, grad_value_block))

            def skipped(grad_query):
                empty_result = jnp.zeros((keys_per_block, KEY_VALUE_HEADS, HEAD_SIZE), jnp.float32)
                return (grad_query, (empty_result, empty_result))

            return lax.cond(jnp.any(allowed), back_active, skipped, carry)

        initial_gradient = jnp.zeros(
            (half_width, KEY_VALUE_HEADS, shared_heads, HEAD_SIZE), jnp.float32
        )
        return lax.scan(
            back_step,
            initial_gradient,
            (blocked_keys, blocked_values, segment_blocks, place_blocks),
        )

    heads_list = []
    extra_list = []
    log_list = []
    for tile in range(2):
        rows_tile = slice(tile * half_width, (tile + 1) * half_width)
        tile_query_tile = query_quad[rows_tile]
        tile_tile_segment = query_segment[rows_tile]
        tile_tile_place = query_place[rows_tile]

        def tile_allowed_of(segment_block, place_block):
            return (tile_tile_segment[:, None] == segment_block[None, :]) & (
                tile_tile_place[:, None] >= place_block[None, :]
            )

        def scores_of(key_block, allowed):
            raw_scores = (
                jnp.einsum(
                    "qhgd,khd->hgqk", tile_query_tile, key_block, preferred_element_type=jnp.float32
                )
                * score_scale
            )
            return jnp.where(allowed[None, None], raw_scores, MASKED_FILL)

        def stats_step(carry, block):
            key_block, segment_block, place_block = block
            allowed = tile_allowed_of(segment_block, place_block)

            def stats_active(state):
                peak, total = state
                scores = scores_of(key_block, allowed)
                newest = jnp.maximum(peak, jnp.max(scores, axis=-1))
                total = total * jnp.exp(peak - newest) + jnp.sum(
                    jnp.exp(scores - newest[..., None]), axis=-1
                )
                return (newest, total)

            return (lax.cond(jnp.any(allowed), stats_active, lambda state: state, carry), None)

        initial_peak = jnp.full(
            (KEY_VALUE_HEADS, shared_heads, half_width), MASKED_FILL, jnp.float32
        )
        initial_total = jnp.zeros((KEY_VALUE_HEADS, shared_heads, half_width), jnp.float32)
        (peak, total), unused = lax.scan(
            stats_step, (initial_peak, initial_total), (blocked_keys, segment_blocks, place_blocks)
        )
        tile_tile_log = peak + jnp.log(total)

        def output_step(carry, block):
            key_block, value_block, segment_block, place_block = block
            allowed = tile_allowed_of(segment_block, place_block)

            def output_active(state):
                upper, lower = state
                probs = jnp.exp(scores_of(key_block, allowed) - tile_tile_log[..., None])
                probs_high = probs.astype(brain_float)
                probs_low = (probs - probs_high.astype(jnp.float32)).astype(brain_float)
                upper = upper + jnp.einsum(
                    "hgqk,khd->qhgd", probs_high, value_block, preferred_element_type=jnp.float32
                )
                lower = lower + jnp.einsum(
                    "hgqk,khd->qhgd", probs_low, value_block, preferred_element_type=jnp.float32
                )
                return (upper, lower)

            return (lax.cond(jnp.any(allowed), output_active, lambda state: state, carry), None)

        initial_accumulator = jnp.zeros(
            (half_width, KEY_VALUE_HEADS, shared_heads, HEAD_SIZE), jnp.float32
        )
        (tile_heads, tile_extra), unused = lax.scan(
            output_step,
            (initial_accumulator, initial_accumulator),
            (blocked_keys, blocked_values, segment_blocks, place_blocks),
        )
        tile_heads, tile_extra, tile_log = (tile_heads, tile_extra, tile_tile_log)
        heads_list.append(tile_heads)
        extra_list.append(tile_extra)
        log_list.append(tile_log)
    heads_four = jnp.concatenate(heads_list, axis=0)
    heads_extra = jnp.concatenate(extra_list, axis=0)
    mixed = heads_four.reshape(row_count, QUERY_HEADS * HEAD_SIZE).astype(brain_float)
    middle = x_float + project_back(mixed, weight_out)
    normed_two_f, norm_two_back = jax.vjp(root_mean_norm, middle, gain_two)
    normed_two = normed_two_f.astype(brain_float)
    weight_gate, weight_up, weight_down = (
        lax.all_gather(w_gate.astype(brain_float), "fsdp", axis=1, tiled=True),
        lax.all_gather(w_up.astype(brain_float), "fsdp", axis=1, tiled=True),
        lax.all_gather(w_down.astype(brain_float), "fsdp", axis=1, tiled=True),
    )
    gate = matmul(normed_two, weight_gate)
    upward = matmul(normed_two, weight_up)
    hidden_f, swiglu_back = jax.vjp(swiglu, gate, upward)
    hidden = hidden_f.astype(brain_float)
    ffn_out = project_back(hidden, weight_down)
    grad_gate_f, grad_up_f = swiglu_back(matmul(dy_rows, weight_down))
    grad_gate = grad_gate_f.astype(brain_float)
    grad_up = grad_up_f.astype(brain_float)
    grad_normed_two = project_back(grad_gate, weight_gate) + project_back(grad_up, weight_up)
    grad_gate_weight = outer_sum(normed_two, grad_gate)
    grad_up_weight = outer_sum(normed_two, grad_up)
    grad_down_weight = outer_sum(dy_rows, hidden)
    grad_middle_norm, grad_gain_two = norm_two_back(grad_normed_two)
    grad_middle = dy_rows.astype(jnp.float32) + grad_middle_norm
    grad_branch = grad_middle.astype(brain_float)
    grad_out_weight = outer_sum(grad_branch, mixed)
    mixed_gradient = matmul(grad_branch, weight_out).astype(brain_float)
    mixed_gradient_quad = mixed_gradient.reshape(
        row_count, KEY_VALUE_HEADS, shared_heads, HEAD_SIZE
    )
    exact_heads = heads_four + heads_extra
    delta = jnp.sum(mixed_gradient_quad.astype(jnp.float32) * exact_heads, axis=-1).transpose(
        1, 2, 0
    )
    grad_query_list = []
    all_key_gradients = jnp.zeros((head_group, KEY_VALUE_HEADS * HEAD_SIZE), jnp.float32)
    all_value_gradients = jnp.zeros((head_group, KEY_VALUE_HEADS * HEAD_SIZE), jnp.float32)
    for tile in range(2):
        rows_tile = slice(tile * half_width, (tile + 1) * half_width)
        tile_grad_query, (key_block_gradients, value_block_gradients) = tile_backward(
            query_quad[rows_tile],
            query_segment[rows_tile],
            query_place[rows_tile],
            log_list[tile],
            mixed_gradient_quad[rows_tile],
            delta[:, :, rows_tile],
        )
        grad_query_list.append(tile_grad_query)
        all_key_gradients = all_key_gradients + key_block_gradients.reshape(
            head_group, KEY_VALUE_HEADS * HEAD_SIZE
        )
        all_value_gradients = all_value_gradients + value_block_gradients.reshape(
            head_group, KEY_VALUE_HEADS * HEAD_SIZE
        )
    grad_query_four = jnp.concatenate(grad_query_list, axis=0)
    all_key_gradients = all_key_gradients * score_scale
    all_key_gradients = halves_order(all_key_gradients, parts)
    all_value_gradients = halves_order(all_value_gradients, parts)
    own_key_gradient, grad_value_own = (
        lax.psum_scatter(
            all_key_gradients.astype(jnp.bfloat16), "ctx", scatter_dimension=0, tiled=True
        ).astype(jnp.float32),
        lax.psum_scatter(
            all_value_gradients.astype(jnp.bfloat16), "ctx", scatter_dimension=0, tiled=True
        ).astype(jnp.float32),
    )
    rotated_key_gradient = (
        own_key_gradient.astype(brain_float)
        .astype(jnp.float32)
        .reshape(row_count, KEY_VALUE_HEADS, HEAD_SIZE)
    )
    grad_value = grad_value_own.astype(brain_float)
    grad_query_rot = (
        (grad_query_four * score_scale)
        .astype(brain_float)
        .astype(jnp.float32)
        .reshape(row_count, QUERY_HEADS, HEAD_SIZE)
    )
    grad_query_raw_f, grad_key_raw_f, grad_query_gain, grad_key_gain = post_back(
        (grad_query_rot, rotated_key_gradient)
    )
    grad_query_raw = grad_query_raw_f.astype(brain_float)
    grad_key_raw = grad_key_raw_f.astype(brain_float)
    grad_normed = (
        project_back(grad_query_raw, weight_query)
        + project_back(grad_key_raw, weight_key)
        + project_back(grad_value, weight_value)
    )
    grad_query_weight = outer_sum(normed_input, grad_query_raw)
    grad_key_weight = outer_sum(normed_input, grad_key_raw)
    grad_value_weight = outer_sum(normed_input, grad_value)
    grad_x_norm, grad_gain_one = norm_one_back(grad_normed)
    out_rows = (middle + ffn_out).astype(brain_float)
    grad_rows = (grad_middle + grad_x_norm).astype(brain_float)
    returned = mirror_back(jnp.stack([out_rows[half_width:], grad_rows[half_width:]]), steps)
    out_rows = jnp.concatenate([out_rows[:half_width], returned[0]], axis=0)
    grad_rows = jnp.concatenate([grad_rows[:half_width], returned[1]], axis=0)
    summed = (
        lax.psum_scatter(
            grad_query_weight.astype(jnp.bfloat16), "fsdp", scatter_dimension=1, tiled=True
        ).astype(jnp.float32),
        lax.psum_scatter(
            grad_key_weight.astype(jnp.bfloat16), "fsdp", scatter_dimension=1, tiled=True
        ).astype(jnp.float32),
        lax.psum_scatter(
            grad_value_weight.astype(jnp.bfloat16), "fsdp", scatter_dimension=1, tiled=True
        ).astype(jnp.float32),
        lax.psum_scatter(
            grad_out_weight.astype(jnp.bfloat16), "fsdp", scatter_dimension=1, tiled=True
        ).astype(jnp.float32),
        lax.psum_scatter(
            grad_gate_weight.astype(jnp.bfloat16), "fsdp", scatter_dimension=1, tiled=True
        ).astype(jnp.float32),
        lax.psum_scatter(
            grad_up_weight.astype(jnp.bfloat16), "fsdp", scatter_dimension=1, tiled=True
        ).astype(jnp.float32),
        lax.psum_scatter(
            grad_down_weight.astype(jnp.bfloat16), "fsdp", scatter_dimension=1, tiled=True
        ).astype(jnp.float32),
    )
    final_grads = (
        lax.psum_scatter(
            summed[0].astype(jnp.bfloat16), "ctx", scatter_dimension=0, tiled=True
        ).astype(jnp.float32),
        lax.psum_scatter(
            summed[1].astype(jnp.bfloat16), "ctx", scatter_dimension=0, tiled=True
        ).astype(jnp.float32),
        lax.psum_scatter(
            summed[2].astype(jnp.bfloat16), "ctx", scatter_dimension=0, tiled=True
        ).astype(jnp.float32),
        lax.psum_scatter(
            summed[3].astype(jnp.bfloat16), "ctx", scatter_dimension=0, tiled=True
        ).astype(jnp.float32),
        lax.psum_scatter(
            summed[4].astype(jnp.bfloat16), "ctx", scatter_dimension=0, tiled=True
        ).astype(jnp.float32),
        lax.psum_scatter(
            summed[5].astype(jnp.bfloat16), "ctx", scatter_dimension=0, tiled=True
        ).astype(jnp.float32),
        lax.psum_scatter(
            summed[6].astype(jnp.bfloat16), "ctx", scatter_dimension=0, tiled=True
        ).astype(jnp.float32),
    )
    gains_total = lax.psum(
        (grad_gain_one, grad_gain_two, grad_query_gain, grad_key_gain), ("ctx", "fsdp")
    )
    return (
        out_rows[None],
        grad_rows[None],
        gains_total[0],
        gains_total[1],
        gains_total[2],
        gains_total[3],
        final_grads[0],
        final_grads[1],
        final_grads[2],
        final_grads[3],
        final_grads[4],
        final_grads[5],
        final_grads[6],
    )


def solution(mesh):
    row, whole, split = P("fsdp", "ctx", None), P(), P(None, "fsdp")
    out_split = P("ctx", "fsdp")

    def step(x, dy, lengths, *rest):
        p = Plan(mesh.shape["ctx"], mesh.shape["fsdp"], x.shape[1], x.shape[2], rest[5].shape[1] // HEAD, rest[8].shape[1])
        p.nseq = lengths.shape[1]
        if not p.fits():
            return general(x, dy, lengths, *rest)
        return tuple(local(p, x, dy, lengths, *rest))

    return jax.shard_map(
        step, mesh=mesh,
        in_specs=(row, row, P("fsdp", None), whole, whole, whole, whole) + (split,) * 7,
        out_specs=(row, row, whole, whole, whole, whole) + (out_split,) * 7,
        check_vma=False,
    )
```

```python
import functools
import math
import types

import jax
import jax.numpy as jnp
import numpy as np
from jax import lax
from jax.experimental import pallas as pl
from jax.experimental.pallas import tpu as pltpu
from jax.sharding import PartitionSpec as P

MESH = pl.DeviceIdType.MESH
BF16, F32 = jnp.bfloat16, jnp.float32
HEAD = 64
TILE = 256
EPS = 1e-05
THETA = 1000000.0
PLANES = 4
WINDOW = 3
OUT_SLOTS = 4
FF_SLOTS = 12
EXP2_SCALE = math.log2(math.e) / math.sqrt(HEAD)


def nt_dot(left, right):
    return lax.dot_general(left, right, (((1,), (1,)), ((), ())), preferred_element_type=F32)


def dot(left, right):
    return jnp.dot(left, right, preferred_element_type=F32)


(
    BZ,
    HID,
    DOWN,
    DW,
    BN,
    F,
    S1,
    S2,
    S3,
    S4,
    GM,
    BS,
    BP,
    GB,
    KA,
    KX,
    KZ,
    BF,
    DWO,
    DWQ,
    IG,
    GS,
    GF,
    BO,
    GX,
) = range(25)
PAIR_FIRST = (1, 3, 5, 6)
ORDER = (
    (DOWN, 0), (DW, 0), (HID,), (DOWN, 1), (DW, 1), (F, 0), (BN, 0), (DW, 2), (S1, 0), (F, 1), (BZ,), (S1, 1), (BN, 1),
    (F, 2), (DW, 3), (S1, 2), (DW, 4), (DW, 5), (F, 3), (DW, 6), (S1, 3), (F, 4), (F, 5), (S1, 4), (DW, 7), (S1, 5),
    (S2, 1), (DW, 8), (GM,), (F, 6), (BS, 0), (BP, 0, 0), (BP, 0, 2), (S2, 0), (S2, 3), (S1, 6), (KA, 0, 0), (KA, 0, 2),
    (GB, 1), (BS, 1), (S2, 4), (S2, 5), (F, 7), (BP, 1, 0), (S3, 1), (BP, 1, 2), (S1, 7), (S3, 3), (KA, 1, 0), (S3, 0),
    (S2, 2), (DWO,), (KX, 0, 2), (BP, 0, 1), (KA, 1, 2), (S3, 5), (BP, 1, 1), (KA, 0, 1), (KX, 0, 0), (KA, 1, 1),
    (F, 8), (KX, 1, 2), (KX, 0, 1), (BF, 1), (KZ, 0, 2), (F, 9), (S1, 8), (KX, 1, 1), (KZ, 1, 2), (S2, 8), (S2, 6),
    (S1, 9), (BF, 0), (S3, 2), (BO,), (KZ, 0, 1), (S4, 3), (IG, 0), (S3, 4), (KX, 1, 0), (S2, 7), (KZ, 1, 1), (IG, 1),
    (DWQ, 10), (F, 10), (GS, 0), (S1, 10), (S3, 6), (GF, 0), (DWQ, 11), (GS, 1), (F, 11), (S2, 9), (S3, 8), (S1, 11),
    (GF, 1), (S2, 10), (GX,), (GS, 2), (S3, 7), (S3, 9), (S4, 4), (S2, 11), (GF, 2), (S4, 1), (S4, 7), (GS, 3), (S4, 2),
    (S4, 5), (S3, 10), (S3, 11), (S4, 10), (S4, 6), (GF, 3), (S4, 9), (S4, 0), (S4, 8), (S4, 11),
)


class Plan:
    def __init__(self, ctx, groups, rows, width, kv_heads, ff):
        self.A, self.B, self.G = PLANES, ctx // (2 * PLANES), groups
        self.R, self.D, self.KV, self.FL = rows, width, kv_heads, ff
        self.S = width // ctx
        self.nt = ff // TILE
        self.HQ = 128 * kv_heads
        self.no = self.HQ // TILE
        self.tiles = 3 * self.nt + self.no + kv_heads
        self.down, self.gate, self.up, self.out = 0, self.nt, 2 * self.nt, 3 * self.nt
        self.qkv = self.out + self.no
        self.batches = []
        for first, count, step in ((0, 3 * self.nt, 3), (self.out, self.no, 2), (self.qkv, kv_heads, 2)):
            self.batches += [(t, min(step, first + count - t)) for t in range(first, first + count, step)]
        self.ff_batches = -(-3 * self.nt // 3)
        self.pair_first = PAIR_FIRST
        split = ORDER.index((GM,))
        self.order_forward, self.order_backward = ORDER[:split], ORDER[split:]

    def fits(self):
        rows = self.G * self.R
        weights = 2 * self.tiles * self.D * TILE
        keys = 2 * WINDOW * 2 * self.B * self.G * self.KV * self.R * 128
        activations = 2 * rows * (13 * self.D + 3 * self.FL)
        even = self.G == 2 and self.B == 2 and self.no == 2 and self.FL % TILE == 0 and self.HQ % TILE == 0 and self.R % 128 == 0
        return even and weights + keys + activations < 45 << 20


def rotate(u, cos, sin):
    low, high = u[:, :32], u[:, 32:]
    return jnp.concatenate([low * cos - high * sin, high * cos + low * sin], axis=1)


def rotate_back(u, cos, sin):
    low, high = u[:, :32], u[:, 32:]
    return jnp.concatenate([low * cos + high * sin, high * cos - low * sin], axis=1)


AG_AUX, AG_DY, AG_GB, RS_FO, RS_GN2, RS_GN, HEADS, WO = range(8)


def kernel(p, names, *refs):
    r = types.SimpleNamespace(**dict(zip(names, refs)))
    A, B, G, R, D, KV, S = p.A, p.B, p.G, p.R, p.D, p.KV, p.S
    i, f = lax.axis_index("ctx"), lax.axis_index("fsdp")
    c = lax.rem(i, 2)
    b = lax.rem(i // 2, B)
    a = i // (2 * B)
    place = 2 * b + c
    others = range(1, G)

    def at(aa, bb, cc):
        return ((aa * B + bb) * 2 + cc, f)

    def group_device(k):
        return (i, lax.rem(f + k, G))

    def remote(src, dst, send, recv, device):
        return pltpu.make_async_remote_copy(
            src_ref=src, dst_ref=dst, send_sem=send, recv_sem=recv, device_id=device, device_id_type=MESH
        )

    sibling = at(a, b, 1 - c)

    peers = [sibling]
    peers += [at(a, lax.rem(b + k, B), c) for k in range(1, B)]
    peers += [at(lax.rem(a + k, A), b, c) for k in range(1, A)]
    peers += [group_device(k) for k in others]
    barrier = pltpu.get_barrier_semaphore()
    for peer in peers:
        pl.semaphore_signal(barrier, inc=1, device_id=peer, device_id_type=MESH)

    y_sems = r.y_sems

    def gather(kind, buffer, k):
        return remote(buffer.at[0], buffer.at[G - k], y_sems.at[kind, 0, k], y_sems.at[kind, 1, G - k], group_device(k))

    def gathered(kind, buffer, k):
        return remote(buffer.at[k], buffer.at[k], y_sems.at[kind, 0, k], y_sems.at[kind, 1, k], group_device(k))

    def scatter(kind, send, recv, k):
        return remote(send.at[k - 1], recv.at[G - k - 1], y_sems.at[kind, 0, k], y_sems.at[kind, 1, G - k], group_device(k))

    def scattered(kind, send, recv, k):
        return remote(send.at[k - 1], recv.at[k - 1], y_sems.at[kind, 0, k], y_sems.at[kind, 1, k], group_device(k))

    x_all, aux, dy_all = r.x_all, r.aux, r.dy_all
    x_sems_y = r.x_sems_y

    def gather_x(k, q):
        rows = pl.ds(q * (R // 2), R // 2)
        return remote(x_all.at[0, rows], x_all.at[G - k, rows], x_sems_y.at[0, k, q], x_sems_y.at[1, G - k, q], group_device(k))

    def gathered_x(k, q):
        rows = pl.ds(q * (R // 2), R // 2)
        return remote(x_all.at[k, rows], x_all.at[k, rows], x_sems_y.at[0, k, q], x_sems_y.at[1, k, q], group_device(k))

    local_sems = r.local_sems

    def tables():
        where = i * R + lax.broadcasted_iota(jnp.int32, (8, R), 1)
        start = jnp.zeros((8, R), jnp.int32)
        end = jnp.int32(0)
        for j in range(p.nseq):
            end = end + r.lengths[0, j]
            start = jnp.where(where >= end, end, start)
        offset = (where - start).astype(F32)
        steps = lax.broadcasted_iota(jnp.int32, (32, R), 0).astype(F32)
        angle = offset[0:1] * jnp.exp(steps * (-2.0 * math.log(THETA) / HEAD))
        aux[0, 0:32] = jnp.cos(angle)
        aux[0, 32:64] = jnp.sin(angle)
        aux[0, 64:72] = start.astype(F32)
        for j, gain in enumerate((r.query_gain, r.key_gain)):
            wide = jnp.concatenate([jnp.broadcast_to(gain[...], (128, HEAD))] * 2, axis=1)
            r.gain_columns[j * HEAD:(j + 1) * HEAD] = jnp.transpose(wide)[0:HEAD]

    kvw = r.kvw
    z_sems, x_sems, c_sems = r.z_sems, r.x_sems, r.c_sems
    wall = r.wall

    def weight(t):
        return wall[t].reshape(D, TILE)

    def weight_rows(t, aa):
        return wall[t, aa // 2, aa % 2].reshape(D // A, TILE)

    n_t = r.n_t
    raws, q_t, o_acc = r.raws, r.q_t, r.o_acc

    half = R // 2

    def block_half(d, slot, k, q):
        return kvw.at[d, slot, k, :, pl.ds(q * half, half)]

    def z_copy(d, k, q):
        source, target = block_half(d - 1, place, k, q), block_half(d, place, k, q)
        return remote(source, target, z_sems.at[0, d - 1, k, q], z_sems.at[1, d - 1, k, q], at(lax.rem(a + 1, A), b, c))

    def z_arrival(d, k, q):
        slot = block_half(d, place, k, q)
        return remote(slot, slot, z_sems.at[0, d - 1, k, q], z_sems.at[1, d - 1, k, q], at(lax.rem(a + A - 1, A), b, c))

    def x_copy(d, shift, k, q):
        slot = block_half(d, place, k, q)
        return remote(slot, slot, x_sems.at[0, d, shift, k, q], x_sems.at[1, d, shift, k, q], at(a, lax.rem(b + shift, B), c))

    def x_arrival(d, shift, k, q):
        other = lax.rem(b + B - shift, B)
        slot = block_half(d, 2 * other + c, k, q)
        return remote(slot, slot, x_sems.at[0, d, shift, k, q], x_sems.at[1, d, shift, k, q], at(a, other, c))

    def c_copy(d, column, k, q):
        slot = block_half(d, 2 * column + c, k, q)
        return remote(slot, slot, c_sems.at[0, d, column, k, q], c_sems.at[1, d, column, k, q], sibling)

    def c_arrival(d, column, k, q):
        slot = block_half(d, 2 * column + 1 - c, k, q)
        return remote(slot, slot, c_sems.at[0, d, column, k, q], c_sems.at[1, d, column, k, q], sibling)

    def x_needed(d, source, target):
        if d == 0:
            return target > source
        if d == 1:
            return target >= 0
        return target < source

    def c_needed(d, column, core):
        if d == 0:
            return jnp.logical_or(column < b, jnp.logical_and(column == b, core == 0))
        if d == 1:
            return column >= 0
        return jnp.logical_or(column > b, jnp.logical_and(column == b, core == 1))

    def when_all(*conditions):
        whole = conditions[0]
        for condition in conditions[1:]:
            whole = jnp.logical_and(whole, condition)
        return pl.when(whole)

    def onward(d, k, q):
        @when_all(a + 1 < A, a >= d)
        def _():
            z_copy(d + 1, k, q).start()

    def spread(d, k, q):
        for shift in range(1, B):
            @when_all(a >= d, x_needed(d, b, lax.rem(b + shift, B)))
            def _():
                x_copy(d, shift, k, q).start()
        @when_all(a >= d, c_needed(d, b, c))
        def _():
            c_copy(d, b, k, q).start()

    def from_plane(d, k, q):
        @pl.when(a >= d)
        def _():
            z_arrival(d, k, q).wait_recv()

    def from_columns(d, k, q):
        for shift in range(1, B):
            other = lax.rem(b + B - shift, B)
            @when_all(a >= d, x_needed(d, other, b))
            def _():
                x_arrival(d, shift, k, q).wait_recv()
                c_copy(d, other, k, q).start()

    def from_sibling(d, k):
        def step(column, _):
            @when_all(a >= d, c_needed(d, column, 1 - c))
            def _():
                for q in range(2):
                    c_arrival(d, column, k, q).wait_recv()
            return 0
        lax.fori_loop(0, B, step, 0)

    def all_sent(k):
        for q in range(2):
            for d in range(WINDOW):
                if d + 1 < WINDOW:
                    @when_all(a + 1 < A, a >= d)
                    def _():
                        z_copy(d + 1, k, q).wait_send()
                for shift in range(1, B):
                    @when_all(a >= d, x_needed(d, b, lax.rem(b + shift, B)))
                    def _():
                        x_copy(d, shift, k, q).wait_send()
                def step(column, _):
                    @when_all(a >= d, c_needed(d, column, c))
                    def _():
                        c_copy(d, column, k, q).wait_send()
                    return 0
                lax.fori_loop(0, B, step, 0)

    def project(k, first, count):
        rows, lanes = pl.ds(first, count), slice(first, first + count)
        x = x_all[k, rows].astype(F32)
        n = x * lax.rsqrt(jnp.mean(x * x, axis=1, keepdims=True) + EPS) * r.gain_one[...]
        n_rows = n.astype(BF16)
        n_t[:, k * R + first:k * R + first + count] = jnp.transpose(n).astype(BF16)
        cos, sin = aux[k, 0:32, lanes], aux[k, 32:64, lanes]
        q_gain, k_gain = r.gain_columns[0:64, 0:1], r.gain_columns[64:128, 0:1]
        for h in range(KV):
            raw = jnp.transpose(dot(n_rows, weight(p.qkv + h)))
            raws[k, h, :, lanes] = raw[0:192]
            query = raw[0:128].reshape(2, HEAD, count)
            query = query * lax.rsqrt(jnp.mean(query * query, axis=1, keepdims=True) + EPS) * q_gain
            query = rotate(query, cos, sin).astype(BF16)
            for j in range(2):
                q_t[k, h, 0:64, j * R + first:j * R + first + count] = query[j]
                q_t[k, h, 64:128, j * R + first:j * R + first + count] = jnp.zeros((64, count), BF16)
            key = raw[128:192].reshape(1, HEAD, count)
            key = key * lax.rsqrt(jnp.mean(key * key, axis=1, keepdims=True) + EPS) * k_gain
            key = rotate(key, cos, sin).reshape(HEAD, count)
            kv = jnp.concatenate([key, raw[192:256]], axis=0)
            kvw[0, place, k, h, rows] = jnp.transpose(kv).astype(BF16)

    def mask_of(k, key_start, diagonal):
        keys = lax.broadcasted_iota(jnp.int32, (R, 2 * R), 0)
        start = jnp.concatenate([aux[k, 64:65], aux[k, 64:65]], axis=1)
        allowed = (keys + key_start).astype(F32) >= start
        if diagonal:
            query = lax.broadcasted_iota(jnp.int32, (R, 2 * R), 1)
            query = jnp.where(query >= R, query - R, query)
            allowed = jnp.logical_and(allowed, keys <= query)
        return allowed

    def attend(d, other, k, diagonal=False):
        key_start = ((a - d) * 2 * B + other) * R
        allowed = mask_of(k, key_start, diagonal)
        for h in range(KV):
            kv = kvw[d, other, k, h]
            scores = dot(kv, q_t[k, h])
            weights = jnp.where(allowed, jnp.exp2(scores * EXP2_SCALE), 0.0).astype(BF16)
            values = jnp.concatenate([jnp.transpose(kv)[64:128], jnp.ones((16, R), BF16)], axis=0)
            added = dot(values, weights)
            if diagonal:
                o_acc[k, h] = added
            else:
                o_acc[k, h] += added

    def attended(d):
        if d == 0:
            return 0, place
        if d == 1:
            return 0, jnp.where(a >= 1, 2 * B, 0)
        return place, jnp.where(a >= 2, 2 * B, 0)

    def attend_plane(d, k):
        low, high = attended(d)
        def step(other, _):
            attend(d, other, k)
            return 0
        lax.fori_loop(low, high, step, 0)

    mixed = r.mixed
    n2_all = gb_all = r.n2_all
    y_send, y_recv, fo_send, fo_recv = r.y_send, r.y_recv, r.fo_send, r.fo_recv
    part, out_acc, middle = r.part, r.out_acc, r.middle
    gains = r.gains

    def store_part(k, send, own, aa, value):
        columns = slice(aa * (D // A), (aa + 1) * (D // A))
        if k == 0:
            own[:, columns] = value
        else:
            send[k - 1, :, columns] = value.astype(BF16)

    def finish_heads(k):
        for h in range(KV):
            o = o_acc[k, h]
            o_n = o[0:64] / o[64:65]
            o_acc[k, h, 0:64] = o_n
            both = jnp.concatenate([o_n[:, 0:R], o_n[:, R:2 * R]], axis=0)
            mixed[k, :, 128 * h:128 * h + 128] = jnp.transpose(both).astype(BF16)

    mixed_in, wo_other = r.mixed_in, r.wo_other

    def heads_out(k):
        return remote(mixed.at[k], mixed_in.at[1 - k], y_sems.at[HEADS, 0, k], y_sems.at[HEADS, 1, 1 - k], group_device(1))

    def heads_in(k):
        return remote(mixed.at[k], mixed_in.at[k], y_sems.at[HEADS, 0, k], y_sems.at[HEADS, 1, k], group_device(1))

    def out_tile():
        return remote(wall.at[p.out + c], wo_other.at[c], y_sems.at[WO, 0, 0], y_sems.at[WO, 1, 0], group_device(1))

    def out_tile_on():
        return remote(wo_other.at[c], wo_other.at[c], y_sems.at[WO, 0, 1], y_sems.at[WO, 1, 1], sibling)

    def out_tile_in():
        return remote(wo_other.at[1 - c], wo_other.at[1 - c], y_sems.at[WO, 0, 1], y_sems.at[WO, 1, 1], sibling)

    def project_out(k, target):
        for aa in range(A):
            total = jnp.zeros((R, D // A), F32)
            for t in range(p.no):
                lanes = slice(t * TILE, (t + 1) * TILE)
                total += nt_dot(mixed[k, :, lanes], weight_rows(p.out + t, aa))
                other = wo_other[t, aa // 2, aa % 2].reshape(D // A, TILE)
                total += nt_dot(mixed_in[k, :, lanes], other)
            target[:, aa * (D // A):(aa + 1) * (D // A)] = total

    def normed_middle(k, branch, keep):
        for piece in range(R // 128):
            rows = pl.ds(piece * 128, 128)
            v = x_all[k, rows].astype(F32) + branch[rows]
            if keep:
                middle[rows] = v
            n2_all[k, rows] = (v * lax.rsqrt(jnp.mean(v * v, axis=1, keepdims=True) + EPS) * r.gain_two[...]).astype(BF16)

    def load_scope(s_q, s_k, s_v, s_o):
        own_x = pltpu.make_async_copy(r.x.at[0], x_all.at[0], local_sems.at[0])
        loads = [
            pltpu.make_async_copy(source, s, local_sems.at[2 + j])
            for j, (source, s) in enumerate(((r.w_query, s_q), (r.w_key, s_k), (r.w_value, s_v), (r.w_out, s_o)))
        ]
        own_x.start()
        for load in loads:
            load.start()

        def cast_qkv(aa, _):
            rows = pl.ds(aa * (D // A), D // A)
            for h in range(KV):
                whole = jnp.concatenate(
                    [s_q[rows, 128 * h:128 * h + 128], s_k[rows, 64 * h:64 * h + 64], s_v[rows, 64 * h:64 * h + 64]], axis=1
                ).astype(BF16)
                wall[p.qkv + h, aa // 2, lax.rem(aa, 2)] = whole.reshape(B, 2, S, TILE)
            return 0

        def cast_out(aa, _):
            rows = pl.ds(aa * (D // A), D // A)
            for t in range(p.no):
                wall[p.out + t, aa // 2, lax.rem(aa, 2)] = s_o[rows, TILE * t:TILE * (t + 1)].astype(BF16).reshape(B, 2, S, TILE)
            return 0

        tables()
        own_x.wait()
        pl.semaphore_wait(barrier, len(peers))
        for k in others:
            gather(AG_AUX, aux, k).start()
            for q in range(2):
                gather_x(k, q).start()
        for load in loads[:3]:
            load.wait()
        lax.fori_loop(0, A, cast_qkv, 0)
        loads[3].wait()
        lax.fori_loop(0, A, cast_out, 0)

    def forward_scope(stage, stage_sems):
        own_dy = pltpu.make_async_copy(r.dy.at[0], dy_all.at[0], local_sems.at[1])
        ff = ((r.w_gate, p.gate), (r.w_up, p.up), (r.w_down, p.down))
        slots = FF_SLOTS
        chunks = A * B * 2

        def ff_load(source, n):
            rows = pl.ds(n * S, S)
            return pltpu.make_async_copy(source.at[rows], stage.at[lax.rem(n, slots)], stage_sems.at[lax.rem(n, slots)])

        def prime(which):
            for n in range(slots - 1):
                ff_load(ff[which][0], n).start()

        def cast_ff(which):
            source, first = ff[which]
            def step(n, _):
                @pl.when(n + slots - 1 < chunks)
                def _():
                    ff_load(source, n + slots - 1).start()
                ff_load(source, n).wait()
                aa, bb, cc = n // (2 * B), lax.rem(n // 2, B), lax.rem(n, 2)
                for t in range(p.nt):
                    part_of = stage[lax.rem(n, slots), :, t * TILE:(t + 1) * TILE]
                    wall[first + t, aa // 2, lax.rem(aa, 2), bb, cc] = part_of.astype(BF16)
                return 0
            lax.fori_loop(0, chunks, step, 0)
            if which + 1 < len(ff):
                prime(which + 1)

        prime(0)
        own_dy.start()
        halves = range(2)
        project(0, 0, R)
        for q in halves:
            onward(0, 0, q)
            spread(0, 0, q)
        attend(0, place, 0, True)
        own_dy.wait()
        cast_ff(0)
        from_plane(1, 0, 0)
        onward(1, 0, 0)
        spread(1, 0, 0)
        from_columns(0, 0, 0)
        for k in others:
            gathered(AG_AUX, aux, k).wait_recv()
            gathered_x(k, 0).wait_recv()
            project(k, 0, half)
            onward(0, k, 0)
            spread(0, k, 0)
        from_plane(1, 0, 1)
        spread(1, 0, 1)
        from_columns(0, 0, 1)
        cast_ff(1)
        for k in others:
            gathered_x(k, 1).wait_recv()
            project(k, half, half)
            onward(0, k, 1)
            spread(0, k, 1)
        out_tile().start()
        from_columns(1, 0, 0)
        for k in others:
            from_plane(1, k, 0)
            onward(1, k, 0)
            spread(1, k, 0)
        from_columns(1, 0, 1)
        from_sibling(0, 0)
        attend_plane(0, 0)
        for k in others:
            attend(0, place, k, True)
            from_plane(1, k, 1)
            onward(1, k, 1)
            spread(1, k, 1)
            for q in halves:
                from_columns(0, k, q)
        onward(1, 0, 1)
        from_sibling(1, 0)
        for k in others:
            from_plane(2, k, 0)
            spread(2, k, 0)
        attend_plane(1, 0)
        for k in others:
            from_plane(2, k, 1)
            spread(2, k, 1)
            for q in halves:
                from_columns(1, k, q)
            from_sibling(0, k)
            attend_plane(0, k)
        out_tile().wait_recv()
        out_tile_on().start()
        for k in others:
            gather(AG_DY, dy_all, k).start()
        for k in others:
            from_sibling(1, k)
            attend_plane(1, k)
        for q in halves:
            from_plane(2, 0, q)
            spread(2, 0, q)
        for k in others:
            for q in halves:
                from_columns(2, k, q)
            from_sibling(2, k)
            attend_plane(2, k)
            finish_heads(k)
            heads_out(k).start()
        for q in halves:
            from_columns(2, 0, q)
        from_sibling(2, 0)
        attend_plane(2, 0)
        finish_heads(0)
        heads_out(0).start()
        out_tile_in().wait_recv()
        heads_in(0).wait_recv()
        project_out(0, part)
        normed_middle(0, part, True)
        cast_ff(2)
        for k in range(G):
            all_sent(k)
        out_tile().wait_send()
        out_tile_on().wait_send()

    pl.run_scoped(
        load_scope,
        pltpu.VMEM((D, 128 * KV), F32),
        pltpu.VMEM((D, 64 * KV), F32),
        pltpu.VMEM((D, 64 * KV), F32),
        pltpu.VMEM((D, 128 * KV), F32),
    )
    pl.run_scoped(
        forward_scope,
        pltpu.VMEM((FF_SLOTS, S, p.FL), F32),
        pltpu.SemaphoreType.DMA((FF_SLOTS,)),
    )
    for k in others:
        for q in range(2):
            gather_x(k, q).wait_send()
        gather(AG_AUX, aux, k).wait_send()

    rc, r1, r2, r3 = r.rc, r.r1, r.r2, r.r3
    w_sems = r.w_sems
    stage_c, fetch_sems = r.stage_c, r.fetch_sems
    high, low = a // 2, lax.rem(a, 2)
    column_device = at(a, 1 - b, c)
    pair_device = at(2 * high + 1 - low, b, c)

    def sum_core(n):
        t, m = p.batches[n]
        source = wall.at[pl.ds(t, m), :, :, :, 1 - c]
        return remote(source, rc.at[pl.ds(t, m)], w_sems.at[0, 0, n], w_sems.at[1, 0, n], sibling)

    def sum_first(n):
        t, m = p.batches[n]
        if n in p.pair_first:
            source, device = wall.at[pl.ds(t, m), :, 1 - low, :, c], pair_device
        else:
            source, device = wall.at[pl.ds(t, m), :, :, 1 - b, c], column_device
        return remote(source, r1.at[pl.ds(t, m)], w_sems.at[0, 1, n], w_sems.at[1, 1, n], device)

    def sum_second(n):
        t, m = p.batches[n]
        if n in p.pair_first:
            source, device = wall.at[pl.ds(t, m), :, low, 1 - b, c], column_device
        else:
            source, device = wall.at[pl.ds(t, m), :, 1 - low, b, c], pair_device
        return remote(source, r2.at[pl.ds(t, m)], w_sems.at[0, 2, n], w_sems.at[1, 2, n], device)

    def sum_third(n):
        t, m = p.batches[n]
        source = wall.at[pl.ds(t, m), 1 - high, low, b, c]
        return remote(source, r3.at[pl.ds(t, m)], w_sems.at[0, 3, n], w_sems.at[1, 3, n], at(2 * (1 - high) + low, b, c))

    def fetch_core(n):
        t, m = p.batches[n]
        return pltpu.make_async_copy(rc.at[pl.ds(t, m)], stage_c.at[n % 2, pl.ds(0, m)], fetch_sems.at[n % 2])

    def step_core(n):
        sum_core(n).start()

    def step_fetch(n):
        sum_core(n).wait_recv()
        fetch_core(n).start()

    def step_first(n):
        t, m = p.batches[n]
        fetch_core(n).wait()
        def add(j, _):
            tile, hi, lo = j // A, lax.rem(j // 2, 2), lax.rem(j, 2)
            mine = wall[t + tile, hi, lo, :, c].astype(F32) + stage_c[n % 2, tile, hi, lo].astype(F32)
            wall[t + tile, hi, lo, :, c] = mine.astype(BF16)
            return 0
        lax.fori_loop(0, m * A, add, 0)
        sum_first(n).start()

    def step_second(n):
        t, m = p.batches[n]
        sum_first(n).wait_recv()
        def add(tile, _):
            if n in p.pair_first:
                mine = wall[t + tile, :, low, :, c].astype(F32) + r1[t + tile].astype(F32)
                wall[t + tile, :, low, :, c] = mine.astype(BF16)
            else:
                mine = wall[t + tile, :, :, b, c].astype(F32) + r1[t + tile].astype(F32)
                wall[t + tile, :, :, b, c] = mine.astype(BF16)
            return 0
        lax.fori_loop(0, m, add, 0)
        sum_second(n).start()

    def step_third(n):
        t, m = p.batches[n]
        sum_second(n).wait_recv()
        def add(tile, _):
            mine = wall[t + tile, :, low, b, c].astype(F32) + r2[t + tile].astype(F32)
            wall[t + tile, :, low, b, c] = mine.astype(BF16)
            return 0
        lax.fori_loop(0, m, add, 0)
        sum_third(n).start()

    out_stage, out_sems = r.out_stage, r.out_sems

    def out_copy(n):
        t, m = p.batches[n]
        return pltpu.make_async_copy(out_stage.at[n % OUT_SLOTS, pl.ds(0, m)], r.d_weights.at[pl.ds(t, m)], out_sems.at[n % OUT_SLOTS])

    out_order = []

    def step_out(n):
        t, m = p.batches[n]
        sum_third(n).wait_recv()
        for earlier in out_order:
            if earlier % OUT_SLOTS == n % OUT_SLOTS:
                out_copy(earlier).wait()
        out_order[:] = [e for e in out_order if e % OUT_SLOTS != n % OUT_SLOTS] + [n]
        def add(tile, _):
            out_stage[n % OUT_SLOTS, tile] = wall[t + tile, high, low, b, c].astype(F32) + r3[t + tile].astype(F32)
            return 0
        lax.fori_loop(0, m, add, 0)
        out_copy(n).start()

    def run(order, steps):
        steps = {**steps, F: step_fetch, S1: step_first, S2: step_second, S3: step_third, S4: step_out}
        for step, *numbers in order:
            steps[step](*numbers)

    def feed_forward(hs, n2_t, dy_t):
        def turned(source, k, target):
            for piece in range(R // 128):
                rows = pl.ds(piece * 128, 128)
                target[:, k * R + piece * 128:k * R + (piece + 1) * 128] = jnp.transpose(source[k, rows].astype(F32)).astype(BF16)

        def hidden(k, first, count):
            rows = slice(k * R, (k + 1) * R)
            def step(t, _):
                gate = dot(n2_all[k], weight(p.gate + t))
                up = dot(n2_all[k], weight(p.up + t))
                grad = dot(dy_all[k], weight(p.down + t))
                sig = 1.0 / (1.0 + jnp.exp(-gate))
                silu = gate * sig
                hs[2, t, rows] = (silu * up).astype(BF16)
                hs[0, t, rows] = (grad * up * (sig * (1.0 + gate * (1.0 - sig)))).astype(BF16)
                hs[1, t, rows] = (grad * silu).astype(BF16)
                return 0
            lax.fori_loop(first, first + count, step, 0)

        def back_normed(k, parts):
            rows = slice(k * R, (k + 1) * R)
            for aa in parts:
                total = jnp.zeros((R, D // A), F32)
                for t in range(p.nt):
                    total += nt_dot(hs[0, t, rows], weight_rows(p.gate + t, aa))
                    total += nt_dot(hs[1, t, rows], weight_rows(p.up + t, aa))
                store_part(k, y_send, part, aa, total)

        def down(k, first, count):
            rows = slice(k * R, (k + 1) * R)
            for aa in range(A):
                columns = slice(aa * (D // A), (aa + 1) * (D // A))
                total = jnp.zeros((R, D // A), F32)
                for t in range(first, first + count):
                    total += nt_dot(hs[2, t, rows], weight_rows(p.down + t, aa))
                if k == 0:
                    out_acc[:, columns] = middle[:, columns] + total
                elif first:
                    store_part(k, fo_send, None, aa, fo_send[k - 1, :, columns].astype(F32) + total)
                else:
                    store_part(k, fo_send, None, aa, total)

        def weight_gradients(n):
            t, m = p.batches[n]
            for tile in range(t, t + m):
                kind, u = (2, 0, 1)[tile // p.nt], tile % p.nt
                left = dy_t if kind == 2 else n2_t
                for aa in range(A):
                    rows = slice(aa * (D // A), (aa + 1) * (D // A))
                    wall[tile, aa // 2, aa % 2] = dot(left[rows], hs[kind, u]).astype(BF16).reshape(B, 2, S, TILE)

        hidden(0, 0, p.nt)
        turned(dy_all, 0, dy_t)
        turned(n2_all, 0, n2_t)
        for k in others:
            heads_in(k).wait_recv()
            project_out(k, out_acc)
            normed_middle(k, out_acc, False)
            gathered(AG_DY, dy_all, k).wait_recv()
            hidden(k, 0, p.batches[0][1])
            turned(dy_all, k, dy_t)
        down(0, 0, p.nt)

        first_tiles = p.batches[0][1]

        def hidden_others():
            for k in others:
                hidden(k, first_tiles, p.nt - first_tiles)
                turned(n2_all, k, n2_t)

        def down_others(part):
            for k in others:
                if part == 0:
                    down(k, 0, first_tiles)
                else:
                    down(k, first_tiles, p.nt - first_tiles)

        def gradients_and_core(n):
            weight_gradients(n)
            step_core(n)

        def back_normed_half(half):
            for k in others:
                back_normed(k, range(half * A // 2, (half + 1) * A // 2))
                if half:
                    scatter(RS_GN2, y_send, y_recv, k).start()

        run(p.order_forward, {
            HID: hidden_others, DOWN: down_others, DW: gradients_and_core, BN: back_normed_half,
            BZ: lambda: back_normed(0, range(A)),
        })

    pl.run_scoped(
        feed_forward,
        pltpu.VMEM((3, p.nt, G * R, TILE), BF16),
        pltpu.VMEM((D, G * R), BF16),
        pltpu.VMEM((D, G * R), BF16),
    )
    last = p.ff_batches


    def middle_gradient():
        for k in others:
            scattered(RS_GN2, y_send, y_recv, k).wait_recv()
        gain_grad = jnp.zeros((1, D), F32)
        for piece in range(R // 128):
            rows = pl.ds(piece * 128, 128)
            e = part[rows]
            for k in others:
                e += y_recv[k - 1, rows].astype(F32)
            v = middle[rows]
            rr = lax.rsqrt(jnp.mean(v * v, axis=1, keepdims=True) + EPS)
            vh = v * rr
            gain_grad += jnp.sum(e * vh, axis=0, keepdims=True)
            ge = e * r.gain_two[...]
            gm = dy_all[0, rows].astype(F32) + rr * (ge - vh * jnp.mean(vh * ge, axis=1, keepdims=True))
            middle[rows] = gm
            r.gb_t[:, piece * 128:(piece + 1) * 128] = jnp.transpose(gm).astype(BF16)
        gains[...] = jnp.zeros((8, D), F32)
        gains[0:1] = gain_grad
        gb_all[0] = middle[...].astype(BF16)
        for k in others:
            gather(AG_GB, gb_all, k).start()

    dm = r.dm
    graw = r.graw
    kvr, xr, zr = r.kvr, r.xr, r.zr
    kc_sems, kx_sems, kz_sems = r.kc_sems, r.kx_sems, r.kz_sems
    head_sums = r.head_sums
    head_sums[...] = jnp.zeros((128, R), F32)

    def k_core(d, column, k):
        return remote(kvw.at[d, 2 * column + 1 - c, k], kvr.at[d, column, k], kc_sems.at[0, d, column, k], kc_sems.at[1, d, column, k], sibling)

    def k_column(d, shift, k):
        target = lax.rem(b + shift, B)
        return remote(kvw.at[d, 2 * target + c, k], xr.at[d, shift - 1, k], kx_sems.at[0, d, shift, k], kx_sems.at[1, d, shift, k], at(a, target, c))

    def k_plane(d, k):
        return remote(kvw.at[d, place, k], zr.at[d - 1, k], kz_sems.at[0, d - 1, k], kz_sems.at[1, d - 1, k], at(lax.rem(a + A - 1, A), b, c))

    def in_window(d, column, core, from_core):
        if d == 0:
            return jnp.logical_or(column < b, jnp.logical_and(column == b, core <= from_core))
        if d == 1:
            return column >= 0
        return jnp.logical_or(column > b, jnp.logical_and(column == b, core >= from_core))

    def column_reached(d, target, source):
        if d == 0:
            return target < source
        if d == 1:
            return target >= 0
        return target > source

    def keys_core(d, k):
        for column in range(B):
            @when_all(a >= d, in_window(d, column, 1 - c, c))
            def _():
                k_core(d, column, k).start()

    def keys_add(d, k, kv_stage, kv_sems):
        def fetch(column):
            return pltpu.make_async_copy(kvr.at[d, column, k], kv_stage.at[column], kv_sems.at[column])

        for column in range(B):
            @when_all(a >= d, in_window(d, column, c, 1 - c))
            def _():
                k_core(d, column, k).wait_recv()
                fetch(column).start()
        for column in range(B):
            @when_all(a >= d, in_window(d, column, c, 1 - c))
            def _():
                fetch(column).wait()
                for h in range(KV):
                    slot = 2 * column + c
                    kvw[d, slot, k, h] = (kvw[d, slot, k, h].astype(F32) + kv_stage[column, h].astype(F32)).astype(BF16)
        for shift in range(1, B):
            @when_all(a >= d, column_reached(d, lax.rem(b + shift, B), b))
            def _():
                k_column(d, shift, k).start()

    def keys_columns(d, k):
        for shift in range(1, B):
            @when_all(a >= d, column_reached(d, b, lax.rem(b + B - shift, B)))
            def _():
                k_column(d, shift, k).wait_recv()
                for h in range(KV):
                    kvw[d, place, k, h] = (kvw[d, place, k, h].astype(F32) + xr[d, shift - 1, k, h].astype(F32)).astype(BF16)

    def keys_plane(d, k):
        @pl.when(a >= d)
        def _():
            k_plane(d, k).start()

    def keys_from_plane(d, k):
        @when_all(a + 1 < A, a + 1 >= d)
        def _():
            k_plane(d, k).wait_recv()
            for h in range(KV):
                kvw[d - 1, place, k, h] = (kvw[d - 1, place, k, h].astype(F32) + zr[d - 1, k, h].astype(F32)).astype(BF16)

    def keys_sent(k):
        for d in range(WINDOW):
            for column in range(B):
                @when_all(a >= d, in_window(d, column, 1 - c, c))
                def _():
                    k_core(d, column, k).wait_send()
            for shift in range(1, B):
                @when_all(a >= d, column_reached(d, lax.rem(b + shift, B), b))
                def _():
                    k_column(d, shift, k).wait_send()
            if d:
                @pl.when(a >= d)
                def _():
                    k_plane(d, k).wait_send()

    def rms_back(raw, e, gain):
        rr = lax.rsqrt(jnp.mean(raw * raw, axis=1, keepdims=True) + EPS)
        vh = raw * rr
        ge = e * gain
        return jnp.sum(e * vh, axis=0), rr * (ge - vh * jnp.mean(vh * ge, axis=1, keepdims=True))

    def back_start(k, do_t, do_rows, q_rows, dq, rows_of):
        for t in range(p.no):
            dm[:, t * TILE:(t + 1) * TILE] = dot(gb_all[k], weight(p.out + t)).astype(BF16)
        for h in range(KV):
            turned = jnp.transpose(dm[:, 128 * h:128 * h + 128].astype(F32))
            grad = jnp.concatenate([turned[0:64], turned[64:128]], axis=1)
            rows_of[k, h, 0:1] = jnp.log2(o_acc[k, h, 64:65])
            rows_of[k, h, 1:2] = jnp.sum(grad * o_acc[k, h, 0:64], axis=0, keepdims=True)
            padded = jnp.concatenate([jnp.zeros((64, 2 * R), F32), grad], axis=0)
            do_t[k, h] = padded.astype(BF16)
            do_rows[k, h] = jnp.transpose(padded).astype(BF16)
            q_rows[k, h] = (jnp.transpose(q_t[k, h].astype(F32)) * (1.0 / math.sqrt(HEAD))).astype(BF16)
            dq[k, h] = jnp.zeros((64, 2 * R), F32)

    def back_block(k, d, other, do_t, do_rows, q_rows, dq, rows_of, diagonal=False):
        key_start = ((a - d) * 2 * B + other) * R
        allowed = mask_of(k, key_start, diagonal)
        for h in range(KV):
            kv = kvw[d, other, k, h]
            scores = dot(kv, q_t[k, h])
            probs = jnp.where(allowed, jnp.exp2(scores * EXP2_SCALE - rows_of[k, h, 0:1]), 0.0)
            grad = dot(kv, do_t[k, h])
            grad_scores = (probs * (grad - rows_of[k, h, 1:2])).astype(BF16)
            kvw[d, other, k, h] = (dot(grad_scores, q_rows[k, h]) + dot(probs.astype(BF16), do_rows[k, h])).astype(BF16)
            dq[k, h] += dot(jnp.transpose(kv)[0:64], grad_scores)

    def back_plane(k, d, *scratch):
        if d == 0:
            back_block(k, 0, place, *scratch, diagonal=True)
        low, high = attended(d)
        def step(other, _):
            back_block(k, d, other, *scratch)
            return 0
        lax.fori_loop(low, high, step, 0)
        keys_core(d, k)

    def back_finish(k, dq):
        cos, sin = aux[k, 0:32], aux[k, 32:64]
        for h in range(KV):
            e = (dq[k, h] * (1.0 / math.sqrt(HEAD))).astype(BF16).astype(F32)
            e = rotate_back(jnp.stack([e[:, 0:R], e[:, R:2 * R]]), cos, sin)
            gain_part, grad = rms_back(raws[k, h, 0:128].reshape(2, HEAD, R), e, r.gain_columns[0:64, 0:1])
            head_sums[0:64] += gain_part
            graw[h, k * R:(k + 1) * R, 0:128] = jnp.transpose(grad.reshape(128, R)).astype(BF16)

    def keys_back(k):
        cos, sin = aux[k, 0:32], aux[k, 32:64]
        for h in range(KV):
            final = jnp.transpose(kvw[0, place, k, h].astype(F32))
            e = rotate_back(final[0:64].reshape(1, HEAD, R), cos, sin)
            gain_part, grad = rms_back(raws[k, h, 128:192].reshape(1, HEAD, R), e, r.gain_columns[64:128, 0:1])
            head_sums[64:128] += gain_part
            both = jnp.concatenate([grad.reshape(HEAD, R), final[64:128]], axis=0)
            graw[h, k * R:(k + 1) * R, 128:256] = jnp.transpose(both).astype(BF16)

    xg = r.xg

    def input_gradient(k):
        for aa in range(A):
            columns = slice(aa * (D // A), (aa + 1) * (D // A))
            total = jnp.zeros((R, D // A), F32)
            for h in range(KV):
                total += nt_dot(graw[h, k * R:(k + 1) * R], weight_rows(p.qkv + h, aa))
            store_part(k, y_send, part, aa, total)
            x = x_all[k, :, columns].astype(F32)
            xg[:, columns] += jnp.sum(total * x * x_scale(k), axis=0, keepdims=True)

    def x_scale(k):
        return r.x_scale[k, :, 0:1]

    def out_gradient():
        for t in range(p.no):
            for aa in range(A):
                rows = slice(aa * (D // A), (aa + 1) * (D // A))
                total = jnp.zeros((D // A, TILE), F32)
                for k in range(G):
                    total += dot(r.gb_t[rows, k * R:(k + 1) * R], mixed[k, :, t * TILE:(t + 1) * TILE])
                wall[p.out + t, aa // 2, aa % 2] = total.astype(BF16).reshape(B, 2, S, TILE)
        step_core(p.ff_batches)

    def qkv_gradient(n):
        t, m = p.batches[n]
        for tile in range(t, t + m):
            for aa in range(A):
                rows = slice(aa * (D // A), (aa + 1) * (D // A))
                wall[tile, aa // 2, aa % 2] = dot(n_t[rows], graw[tile - p.qkv]).astype(BF16).reshape(B, 2, S, TILE)
        step_core(n)

    def branch_arrives(k):
        gathered(AG_GB, gb_all, k).wait_recv()
        scatter(RS_FO, fo_send, fo_recv, k).start()
        for piece in range(R // 128):
            rows = pl.ds(piece * 128, 128)
            r.gb_t[:, k * R + piece * 128:k * R + (piece + 1) * 128] = jnp.transpose(gb_all[k, rows].astype(F32)).astype(BF16)

    def keys_over_columns(k, d):
        keys_columns(d, k)
        if d == 2:
            keys_plane(2, k)

    def keys_over_planes(k, d):
        keys_from_plane(d, k)
        if d == 2:
            keys_plane(1, k)
        else:
            keys_back(k)

    def input_step(k):
        if k:
            scatter(RS_GN2, y_send, y_recv, k).wait_send()
        input_gradient(k)
        if k:
            scatter(RS_GN, y_send, y_recv, k).start()

    g_land, g_sems = r.g_land, r.g_sems
    stages = [
        (2, c, 0, lambda j: at(a, b, j)),
        (G, f, 2, lambda j: (i, j)),
        (B, b, 2 + G, lambda j: at(a, j, c)),
        (A, a, 2 + G + B, lambda j: at(j, b, c)),
    ]

    def gain_send(s, shift):
        size, mine, base, device = stages[s]
        return remote(gains, g_land.at[base + mine], g_sems.at[0, s, shift], g_sems.at[1, s, shift], device(lax.rem(mine + shift, size)))

    def gain_arrival(s, shift):
        size, mine, base, device = stages[s]
        slot = lax.rem(mine + size - shift, size)
        return remote(gains, g_land.at[base + slot], g_sems.at[0, s, shift], g_sems.at[1, s, shift], device(slot))

    def gain_start(s):
        size, mine, base, _ = stages[s]
        for shift in range(1, size):
            gain_send(s, shift).start()
        g_land[base + mine] = gains[...]

    def gain_finish(s):
        size, _, base, _ = stages[s]
        for shift in range(1, size):
            gain_arrival(s, shift).wait_recv()
            gain_send(s, shift).wait_send()
        total = g_land[base]
        for j in range(1, size):
            total += g_land[base + j]
        gains[...] = total

    def gain_first(s):
        if s == 0:
            gains[1:2] = xg[...]
            gains[2:3, 0:128] = jnp.sum(jnp.transpose(head_sums[...]), axis=0, keepdims=True)
        gain_start(s)

    def rows_out(j):
        source, target = ((r.block_rows, r.block_out), (r.grad_rows, r.grad_inputs))[j]
        return pltpu.make_async_copy(source, target.at[0], local_sems.at[6 + j])

    def block_rows():
        for k in others:
            scattered(RS_FO, fo_send, fo_recv, k).wait_recv()
        for piece in range(R // 128):
            rows = pl.ds(piece * 128, 128)
            v = out_acc[rows]
            for k in others:
                v += fo_recv[k - 1, rows].astype(F32)
            r.block_rows[rows] = v.astype(BF16)

        rows_out(0).start()

    def input_rows():
        for k in others:
            scattered(RS_GN, y_send, y_recv, k).wait_recv()
        for piece in range(R // 128):
            rows = pl.ds(piece * 128, 128)
            e = part[rows]
            for k in others:
                e += y_recv[k - 1, rows].astype(F32)
            v = x_all[0, rows].astype(F32)
            rr = r.x_scale[0, rows, 0:1]
            vh = v * rr
            ge = e * r.gain_one[...]
            back = rr * (ge - vh * jnp.mean(vh * ge, axis=1, keepdims=True))
            r.grad_rows[rows] = (middle[rows] + back).astype(BF16)

        rows_out(1).start()

    def backward_scope(do_t, do_rows, q_rows, dq, rows_of, kv_stage, kv_sems, gb_t):
        r.gb_t = gb_t
        scratch = (do_t, do_rows, q_rows, dq, rows_of)
        steps = {
            GM: middle_gradient, BS: lambda k: back_start(k, *scratch), BP: lambda k, d: back_plane(k, d, *scratch),
            GB: branch_arrives, KA: lambda k, d: keys_add(d, k, kv_stage, kv_sems), KX: keys_over_columns, KZ: keys_over_planes,
            BF: lambda k: back_finish(k, dq), DWO: out_gradient, DWQ: qkv_gradient, IG: input_step, GS: gain_first,
            GF: gain_finish, BO: block_rows, GX: input_rows,
        }
        run(p.order_backward, steps)

    xg[...] = jnp.zeros((1, D), F32)
    for k in range(G):
        x = x_all[k].astype(F32)
        r.x_scale[k] = jnp.broadcast_to(lax.rsqrt(jnp.mean(x * x, axis=1, keepdims=True) + EPS), (R, 128))
    pl.run_scoped(
        backward_scope,
        pltpu.VMEM((G, KV, 128, 2 * R), BF16),
        pltpu.VMEM((G, KV, 2 * R, 128), BF16),
        pltpu.VMEM((G, KV, 2 * R, 128), BF16),
        pltpu.VMEM((G, KV, 64, 2 * R), F32),
        pltpu.VMEM((G, KV, 8, 2 * R), F32),
        pltpu.VMEM((B, KV, R, 128), BF16),
        pltpu.SemaphoreType.DMA((B,)),
        pltpu.VMEM((D, G * R), BF16),
    )
    r.d_gains[...] = gains[...]
    for n in out_order:
        out_copy(n).wait()
    for j in range(2):
        rows_out(j).wait()

    for k in range(G):
        keys_sent(k)
    for k in range(G):
        heads_out(k).wait_send()
    for k in others:
        gather(AG_DY, dy_all, k).wait_send()
        gather(AG_GB, gb_all, k).wait_send()
        scatter(RS_FO, fo_send, fo_recv, k).wait_send()
        scatter(RS_GN, y_send, y_recv, k).wait_send()
    for n in range(len(p.batches)):
        sum_core(n).wait_send()
        sum_first(n).wait_send()
        sum_second(n).wait_send()
        sum_third(n).wait_send()


def local(p, x, dy, lengths, gain_one, gain_two, query_gain, key_gain, wq, wk, wv, wo, wg, wu, wd):
    A, B, G, R, D, KV, S = p.A, p.B, p.G, p.R, p.D, p.KV, p.S
    any_spec, vmem, smem = (pl.BlockSpec(memory_space=m) for m in (pl.ANY, pltpu.VMEM, pltpu.SMEM))
    ins = dict(
        x=(x, any_spec), dy=(dy, any_spec), lengths=(lengths, smem), gain_one=(gain_one[None], vmem),
        gain_two=(gain_two[None], vmem), query_gain=(query_gain[None], vmem), key_gain=(key_gain[None], vmem),
        w_query=(wq, any_spec), w_key=(wk, any_spec), w_value=(wv, any_spec), w_out=(wo, any_spec),
        w_gate=(wg, any_spec), w_up=(wu, any_spec), w_down=(wd, any_spec),
    )
    rows_out = ((1, R, D), BF16)
    outs = dict(d_gains=((8, D), F32))
    landing = dict(
        block_out=rows_out, grad_inputs=rows_out,
        d_weights=((p.tiles, S, TILE), F32), rc=((p.tiles, 2, 2, B, S, TILE), BF16), kvr=((WINDOW, B, G, KV, R, 128), BF16),
    )
    DMA = pltpu.SemaphoreType.DMA
    n_batches, widest = len(p.batches), max(m for _, m in p.batches)
    scratch = dict(
        x_all=pltpu.VMEM((G, R, D), BF16), aux=pltpu.VMEM((G, 72, R), F32), dy_all=pltpu.VMEM((G, R, D), BF16),
        y_sems=DMA((8, 2, G)), x_sems_y=DMA((2, G, 2)), local_sems=DMA((8,)),
        gain_columns=pltpu.VMEM((128, 128), F32),
        kvw=pltpu.VMEM((WINDOW, 2 * B, G, KV, R, 128), BF16),
        z_sems=DMA((2, 2, G, 2)), x_sems=DMA((2, WINDOW, B, G, 2)), c_sems=DMA((2, WINDOW, B, G, 2)),
        wall=pltpu.VMEM((p.tiles, 2, 2, B, 2, S, TILE), BF16),
        n_t=pltpu.VMEM((D, G * R), BF16),
        raws=pltpu.VMEM((G, KV, 192, R), F32), q_t=pltpu.VMEM((G, KV, 128, 2 * R), BF16),
        o_acc=pltpu.VMEM((G, KV, 80, 2 * R), F32), mixed=pltpu.VMEM((G, R, p.HQ), BF16),
        y_send=pltpu.VMEM((G - 1, R, D), BF16), y_recv=pltpu.VMEM((G - 1, R, D), BF16),
        fo_send=pltpu.VMEM((G - 1, R, D), BF16), fo_recv=pltpu.VMEM((G - 1, R, D), BF16),
        part=pltpu.VMEM((R, D), F32), out_acc=pltpu.VMEM((R, D), F32), middle=pltpu.VMEM((R, D), F32),
        n2_all=pltpu.VMEM((G, R, D), BF16), mixed_in=pltpu.VMEM((G, R, p.HQ), BF16), wo_other=pltpu.VMEM((p.no, 2, 2, B, 2, S, TILE), BF16),
        block_rows=pltpu.VMEM((R, D), BF16), grad_rows=pltpu.VMEM((R, D), BF16), gains=pltpu.VMEM((8, D), F32), xg=pltpu.VMEM((1, D), F32), x_scale=pltpu.VMEM((G, R, 128), F32),
        w_sems=DMA((2, 4, n_batches)), fetch_sems=DMA((2,)), stage_c=pltpu.VMEM((2, widest, 2, 2, B, S, TILE), BF16),
        r1=pltpu.VMEM((p.tiles, 2, 2, S, TILE), BF16), r2=pltpu.VMEM((p.tiles, 2, S, TILE), BF16),
        r3=pltpu.VMEM((p.tiles, S, TILE), BF16), out_stage=pltpu.VMEM((OUT_SLOTS, widest, S, TILE), F32), out_sems=DMA((OUT_SLOTS,)),
        dm=pltpu.VMEM((R, p.HQ), BF16), graw=pltpu.VMEM((KV, G * R, TILE), BF16),
        xr=pltpu.VMEM((WINDOW, B - 1, G, KV, R, 128), BF16), zr=pltpu.VMEM((2, G, KV, R, 128), BF16),
        kc_sems=DMA((2, WINDOW, B, G)), kx_sems=DMA((2, WINDOW, B, G)), kz_sems=DMA((2, 2, G)),
        head_sums=pltpu.VMEM((128, R), F32),
        g_land=pltpu.VMEM((2 + B + A + G, 8, D), F32), g_sems=DMA((2, 4, max(A, B, G, 2))),
    )
    outs_all = dict(outs, **landing)
    out_specs = [vmem for _ in outs] + [any_spec for _ in landing]
    names = list(ins) + list(outs_all) + list(scratch)
    results = pl.pallas_call(
        functools.partial(kernel, p, names),
        out_shape=[jax.ShapeDtypeStruct(*o) for o in outs_all.values()],
        in_specs=[s for _, s in ins.values()],
        out_specs=out_specs,
        scratch_shapes=list(scratch.values()),
        compiler_params=pltpu.CompilerParams(collective_id=0, has_side_effects=True, vmem_limit_bytes=64 << 20),
        name="block",
    )(*[v for v, _ in ins.values()])
    o = dict(zip(outs_all, results))
    o = types.SimpleNamespace(**o)
    packed = [o.block_out, o.grad_inputs, o.d_gains, o.d_weights]
    shapes = [(packed[0].shape, BF16), (packed[0].shape, BF16), ((D,), F32), ((D,), F32), ((HEAD,), F32), ((HEAD,), F32)]
    shapes += [((S, n), F32) for n in (128 * KV, 64 * KV, 64 * KV, 128 * KV, p.FL, p.FL, p.FL)]
    return pl.pallas_call(
        functools.partial(split_kernel, p),
        out_shape=[jax.ShapeDtypeStruct(*shape) for shape in shapes],
        in_specs=[vmem] * len(packed),
        out_specs=[vmem] * len(shapes),
        name="split",
    )(*packed)


def split_kernel(p, out_in, grad_in, gains, tiles, block_out, grad_inputs, g_one, g_two, g_query, g_key, d_query, d_key, d_value, d_out, d_gate, d_up, d_down):
    block_out[...] = out_in[...]
    grad_inputs[...] = grad_in[...]
    g_one[...] = gains[1]
    g_two[...] = gains[0]
    g_query[...] = gains[2, 0:HEAD]
    g_key[...] = gains[2, HEAD:2 * HEAD]
    for ref, first, count in ((d_gate, p.gate, p.nt), (d_up, p.up, p.nt), (d_down, p.down, p.nt), (d_out, p.out, p.no)):
        for t in range(count):
            ref[:, t * TILE:(t + 1) * TILE] = tiles[first + t]
    for h in range(p.KV):
        tile = tiles[p.qkv + h]
        d_query[:, 128 * h:128 * h + 128] = tile[:, 0:128]
        d_key[:, 64 * h:64 * h + 64] = tile[:, 128:192]
        d_value[:, 64 * h:64 * h + 64] = tile[:, 192:256]


QUERY_HEADS = 16
KEY_VALUE_HEADS = 8
HEAD_SIZE = HEAD


MASKED_FILL = -1e30


def swapped(value, axis, bit):
    mask = 2**bit
    pairs = [(source, source ^ mask) for source in range(lax.axis_size(axis))]
    return lax.ppermute(value, axis, pairs)


def root_mean_norm(values, gain):
    return values * lax.rsqrt(jnp.mean(values * values, axis=-1, keepdims=True) + EPS) * gain


def apply_rotary(values, cosine_table, sine_table):
    half_width = values.shape[-1] // 2
    turned = jnp.concatenate([-values[..., half_width:], values[..., :half_width]], axis=-1)
    return values * cosine_table + turned * sine_table


def places(lengths, where):
    ends = jnp.cumsum(lengths)
    before = (ends[None, :] <= where[:, None]).astype(jnp.int32)
    segment = jnp.sum(before, axis=1)
    offset = where - jnp.sum(before * lengths[None, :], axis=1)
    return (segment, offset)


def head_post(query_raw, unrotated_key, query_gain, key_norm_gain, cosine_table, sine_table):
    token_count = query_raw.shape[0]
    query_rot = apply_rotary(
        root_mean_norm(query_raw.reshape(token_count, QUERY_HEADS, HEAD_SIZE), query_gain),
        cosine_table,
        sine_table,
    )
    rotated_key = apply_rotary(
        root_mean_norm(
            unrotated_key.reshape(token_count, KEY_VALUE_HEADS, HEAD_SIZE), key_norm_gain
        ),
        cosine_table,
        sine_table,
    )
    return (query_rot, rotated_key)


def swiglu(gate, upward):
    return jax.nn.silu(gate) * upward


def matmul(left, right):
    return jnp.dot(left, right, preferred_element_type=jnp.float32)


def project_back(left, right):
    return lax.dot_general(
        left, right, (((1,), (1,)), ((), ())), preferred_element_type=jnp.float32
    )


def outer_sum(left, right):
    return lax.dot_general(
        left, right, (((0,), (0,)), ((), ())), preferred_element_type=jnp.float32
    )


def mirror_out(payload, steps):
    for bit in range(steps):
        payload = swapped(payload, "ctx", bit)
    return payload


def mirror_back(payload, steps):
    for bit in range(steps):
        payload = swapped(payload, "ctx", bit)
    return payload


def halves_order(array, parts):
    shaped = array.reshape((parts, 2, array.shape[0] // (2 * parts)) + array.shape[1:])
    return jnp.stack([shaped[:, 0], shaped[::-1, 1]], axis=1).reshape(array.shape)


def general(
    inputs,
    cotangent,
    lengths,
    gain_one,
    gain_two,
    query_gain,
    key_norm_gain,
    w_query,
    key_projection,
    value_projection,
    w_out,
    w_gate,
    w_up,
    w_down,
):
    brain_float = jnp.bfloat16
    parts = lax.axis_size("ctx")
    steps = parts.bit_length() - 1
    device_index = lax.axis_index("ctx")
    row_count = inputs.shape[1]
    head_group = row_count * parts
    half_width = row_count // 2
    own_lengths = lengths[0]
    offsets_half = jnp.arange(half_width, dtype=jnp.int32)
    arrived = mirror_out(jnp.stack([inputs[0][half_width:], cotangent[0][half_width:]]), steps)
    x_rows = jnp.concatenate([inputs[0][:half_width], arrived[0]], axis=0)
    dy_rows = jnp.concatenate([cotangent[0][:half_width], arrived[1]], axis=0)
    query_place = jnp.concatenate(
        [
            device_index * row_count + offsets_half,
            (parts - 1 - device_index) * row_count + half_width + offsets_half,
        ]
    )
    key_place = jnp.arange(head_group, dtype=jnp.int32)
    query_segment, query_offset = places(own_lengths, query_place)
    key_segment, key_offset = places(own_lengths, key_place)
    weight_query, weight_key, weight_value, weight_out = (
        lax.all_gather(w_query.astype(brain_float), "fsdp", axis=1, tiled=True),
        lax.all_gather(key_projection.astype(brain_float), "fsdp", axis=1, tiled=True),
        lax.all_gather(value_projection.astype(brain_float), "fsdp", axis=1, tiled=True),
        lax.all_gather(w_out.astype(brain_float), "fsdp", axis=1, tiled=True),
    )
    x_float = x_rows.astype(jnp.float32)
    normed_f, norm_one_back = jax.vjp(root_mean_norm, x_float, gain_one)
    normed_input = normed_f.astype(brain_float)
    query_raw = matmul(normed_input, weight_query)
    unrotated_key = matmul(normed_input, weight_key)
    value_b = matmul(normed_input, weight_value).astype(brain_float)
    freq = jnp.exp(
        jnp.arange(HEAD_SIZE // 2, dtype=jnp.float32) * (-2.0 * math.log(THETA) / HEAD_SIZE)
    )
    angle = query_offset.astype(jnp.float32)[:, None] * freq[None, :]
    cosine_table = jnp.concatenate([jnp.cos(angle), jnp.cos(angle)], axis=-1)[:, None, :]
    sine_table = jnp.concatenate([jnp.sin(angle), jnp.sin(angle)], axis=-1)[:, None, :]

    def post_local(query_in, key_in, gain_q, gain_k):
        return head_post(query_in, key_in, gain_q, gain_k, cosine_table, sine_table)

    (query_rot, rotated_key), post_back = jax.vjp(
        post_local, query_raw, unrotated_key, query_gain, key_norm_gain
    )
    query_batch = query_rot.astype(brain_float)
    key_batch = rotated_key.astype(brain_float).reshape(row_count, KEY_VALUE_HEADS * HEAD_SIZE)
    gathered_keys, gathered_values = (
        lax.all_gather(key_batch, "ctx", axis=0, tiled=True),
        lax.all_gather(value_b, "ctx", axis=0, tiled=True),
    )
    gathered_keys = halves_order(gathered_keys, parts)
    gathered_values = halves_order(gathered_values, parts)
    shared_heads = QUERY_HEADS // KEY_VALUE_HEADS
    score_scale = 1.0 / math.sqrt(HEAD_SIZE)
    keys_per_block = min(1024, head_group)
    block_count = head_group // keys_per_block
    query_quad = query_batch.reshape(row_count, KEY_VALUE_HEADS, shared_heads, HEAD_SIZE)
    blocked_keys = gathered_keys.reshape(block_count, keys_per_block, KEY_VALUE_HEADS, HEAD_SIZE)
    blocked_values = gathered_values.reshape(
        block_count, keys_per_block, KEY_VALUE_HEADS, HEAD_SIZE
    )
    segment_blocks = key_segment.reshape(block_count, keys_per_block)
    place_blocks = key_place.reshape(block_count, keys_per_block)

    def tile_backward(query_tile, tile_segment, tile_place, tile_log, grad_tile, tile_delta):

        def allowed_of(segment_block, place_block):
            return (tile_segment[:, None] == segment_block[None, :]) & (
                tile_place[:, None] >= place_block[None, :]
            )

        def back_step(carry, block):
            key_block, value_block, segment_block, place_block = block
            allowed = allowed_of(segment_block, place_block)

            def back_active(grad_query):
                raw_scores = (
                    jnp.einsum(
                        "qhgd,khd->hgqk", query_tile, key_block, preferred_element_type=jnp.float32
                    )
                    * score_scale
                )
                probs = jnp.exp(
                    jnp.where(allowed[None, None], raw_scores, MASKED_FILL) - tile_log[..., None]
                )
                grad_probs = jnp.einsum(
                    "qhgd,khd->hgqk", grad_tile, value_block, preferred_element_type=jnp.float32
                )
                grad_scores = (probs * (grad_probs - tile_delta[..., None])).astype(brain_float)
                grad_query = grad_query + jnp.einsum(
                    "hgqk,khd->qhgd", grad_scores, key_block, preferred_element_type=jnp.float32
                )
                grad_key_block = jnp.einsum(
                    "hgqk,qhgd->khd", grad_scores, query_tile, preferred_element_type=jnp.float32
                )
                grad_value_block = jnp.einsum(
                    "hgqk,qhgd->khd",
                    probs.astype(brain_float),
                    grad_tile,
                    preferred_element_type=jnp.float32,
                )
                return (grad_query, (grad_key_block, grad_value_block))

            def skipped(grad_query):
                empty_result = jnp.zeros((keys_per_block, KEY_VALUE_HEADS, HEAD_SIZE), jnp.float32)
                return (grad_query, (empty_result, empty_result))

            return lax.cond(jnp.any(allowed), back_active, skipped, carry)

        initial_gradient = jnp.zeros(
            (half_width, KEY_VALUE_HEADS, shared_heads, HEAD_SIZE), jnp.float32
        )
        return lax.scan(
            back_step,
            initial_gradient,
            (blocked_keys, blocked_values, segment_blocks, place_blocks),
        )

    heads_list = []
    extra_list = []
    log_list = []
    for tile in range(2):
        rows_tile = slice(tile * half_width, (tile + 1) * half_width)
        tile_query_tile = query_quad[rows_tile]
        tile_tile_segment = query_segment[rows_tile]
        tile_tile_place = query_place[rows_tile]

        def tile_allowed_of(segment_block, place_block):
            return (tile_tile_segment[:, None] == segment_block[None, :]) & (
                tile_tile_place[:, None] >= place_block[None, :]
            )

        def scores_of(key_block, allowed):
            raw_scores = (
                jnp.einsum(
                    "qhgd,khd->hgqk", tile_query_tile, key_block, preferred_element_type=jnp.float32
                )
                * score_scale
            )
            return jnp.where(allowed[None, None], raw_scores, MASKED_FILL)

        def stats_step(carry, block):
            key_block, segment_block, place_block = block
            allowed = tile_allowed_of(segment_block, place_block)

            def stats_active(state):
                peak, total = state
                scores = scores_of(key_block, allowed)
                newest = jnp.maximum(peak, jnp.max(scores, axis=-1))
                total = total * jnp.exp(peak - newest) + jnp.sum(
                    jnp.exp(scores - newest[..., None]), axis=-1
                )
                return (newest, total)

            return (lax.cond(jnp.any(allowed), stats_active, lambda state: state, carry), None)

        initial_peak = jnp.full(
            (KEY_VALUE_HEADS, shared_heads, half_width), MASKED_FILL, jnp.float32
        )
        initial_total = jnp.zeros((KEY_VALUE_HEADS, shared_heads, half_width), jnp.float32)
        (peak, total), unused = lax.scan(
            stats_step, (initial_peak, initial_total), (blocked_keys, segment_blocks, place_blocks)
        )
        tile_tile_log = peak + jnp.log(total)

        def output_step(carry, block):
            key_block, value_block, segment_block, place_block = block
            allowed = tile_allowed_of(segment_block, place_block)

            def output_active(state):
                upper, lower = state
                probs = jnp.exp(scores_of(key_block, allowed) - tile_tile_log[..., None])
                probs_high = probs.astype(brain_float)
                probs_low = (probs - probs_high.astype(jnp.float32)).astype(brain_float)
                upper = upper + jnp.einsum(
                    "hgqk,khd->qhgd", probs_high, value_block, preferred_element_type=jnp.float32
                )
                lower = lower + jnp.einsum(
                    "hgqk,khd->qhgd", probs_low, value_block, preferred_element_type=jnp.float32
                )
                return (upper, lower)

            return (lax.cond(jnp.any(allowed), output_active, lambda state: state, carry), None)

        initial_accumulator = jnp.zeros(
            (half_width, KEY_VALUE_HEADS, shared_heads, HEAD_SIZE), jnp.float32
        )
        (tile_heads, tile_extra), unused = lax.scan(
            output_step,
            (initial_accumulator, initial_accumulator),
            (blocked_keys, blocked_values, segment_blocks, place_blocks),
        )
        tile_heads, tile_extra, tile_log = (tile_heads, tile_extra, tile_tile_log)
        heads_list.append(tile_heads)
        extra_list.append(tile_extra)
        log_list.append(tile_log)
    heads_four = jnp.concatenate(heads_list, axis=0)
    heads_extra = jnp.concatenate(extra_list, axis=0)
    mixed = heads_four.reshape(row_count, QUERY_HEADS * HEAD_SIZE).astype(brain_float)
    middle = x_float + project_back(mixed, weight_out)
    normed_two_f, norm_two_back = jax.vjp(root_mean_norm, middle, gain_two)
    normed_two = normed_two_f.astype(brain_float)
    weight_gate, weight_up, weight_down = (
        lax.all_gather(w_gate.astype(brain_float), "fsdp", axis=1, tiled=True),
        lax.all_gather(w_up.astype(brain_float), "fsdp", axis=1, tiled=True),
        lax.all_gather(w_down.astype(brain_float), "fsdp", axis=1, tiled=True),
    )
    gate = matmul(normed_two, weight_gate)
    upward = matmul(normed_two, weight_up)
    hidden_f, swiglu_back = jax.vjp(swiglu, gate, upward)
    hidden = hidden_f.astype(brain_float)
    ffn_out = project_back(hidden, weight_down)
    grad_gate_f, grad_up_f = swiglu_back(matmul(dy_rows, weight_down))
    grad_gate = grad_gate_f.astype(brain_float)
    grad_up = grad_up_f.astype(brain_float)
    grad_normed_two = project_back(grad_gate, weight_gate) + project_back(grad_up, weight_up)
    grad_gate_weight = outer_sum(normed_two, grad_gate)
    grad_up_weight = outer_sum(normed_two, grad_up)
    grad_down_weight = outer_sum(dy_rows, hidden)
    grad_middle_norm, grad_gain_two = norm_two_back(grad_normed_two)
    grad_middle = dy_rows.astype(jnp.float32) + grad_middle_norm
    grad_branch = grad_middle.astype(brain_float)
    grad_out_weight = outer_sum(grad_branch, mixed)
    mixed_gradient = matmul(grad_branch, weight_out).astype(brain_float)
    mixed_gradient_quad = mixed_gradient.reshape(
        row_count, KEY_VALUE_HEADS, shared_heads, HEAD_SIZE
    )
    exact_heads = heads_four + heads_extra
    delta = jnp.sum(mixed_gradient_quad.astype(jnp.float32) * exact_heads, axis=-1).transpose(
        1, 2, 0
    )
    grad_query_list = []
    all_key_gradients = jnp.zeros((head_group, KEY_VALUE_HEADS * HEAD_SIZE), jnp.float32)
    all_value_gradients = jnp.zeros((head_group, KEY_VALUE_HEADS * HEAD_SIZE), jnp.float32)
    for tile in range(2):
        rows_tile = slice(tile * half_width, (tile + 1) * half_width)
        tile_grad_query, (key_block_gradients, value_block_gradients) = tile_backward(
            query_quad[rows_tile],
            query_segment[rows_tile],
            query_place[rows_tile],
            log_list[tile],
            mixed_gradient_quad[rows_tile],
            delta[:, :, rows_tile],
        )
        grad_query_list.append(tile_grad_query)
        all_key_gradients = all_key_gradients + key_block_gradients.reshape(
            head_group, KEY_VALUE_HEADS * HEAD_SIZE
        )
        all_value_gradients = all_value_gradients + value_block_gradients.reshape(
            head_group, KEY_VALUE_HEADS * HEAD_SIZE
        )
    grad_query_four = jnp.concatenate(grad_query_list, axis=0)
    all_key_gradients = all_key_gradients * score_scale
    all_key_gradients = halves_order(all_key_gradients, parts)
    all_value_gradients = halves_order(all_value_gradients, parts)
    own_key_gradient, grad_value_own = (
        lax.psum_scatter(
            all_key_gradients.astype(jnp.bfloat16), "ctx", scatter_dimension=0, tiled=True
        ).astype(jnp.float32),
        lax.psum_scatter(
            all_value_gradients.astype(jnp.bfloat16), "ctx", scatter_dimension=0, tiled=True
        ).astype(jnp.float32),
    )
    rotated_key_gradient = (
        own_key_gradient.astype(brain_float)
        .astype(jnp.float32)
        .reshape(row_count, KEY_VALUE_HEADS, HEAD_SIZE)
    )
    grad_value = grad_value_own.astype(brain_float)
    grad_query_rot = (
        (grad_query_four * score_scale)
        .astype(brain_float)
        .astype(jnp.float32)
        .reshape(row_count, QUERY_HEADS, HEAD_SIZE)
    )
    grad_query_raw_f, grad_key_raw_f, grad_query_gain, grad_key_gain = post_back(
        (grad_query_rot, rotated_key_gradient)
    )
    grad_query_raw = grad_query_raw_f.astype(brain_float)
    grad_key_raw = grad_key_raw_f.astype(brain_float)
    grad_normed = (
        project_back(grad_query_raw, weight_query)
        + project_back(grad_key_raw, weight_key)
        + project_back(grad_value, weight_value)
    )
    grad_query_weight = outer_sum(normed_input, grad_query_raw)
    grad_key_weight = outer_sum(normed_input, grad_key_raw)
    grad_value_weight = outer_sum(normed_input, grad_value)
    grad_x_norm, grad_gain_one = norm_one_back(grad_normed)
    out_rows = (middle + ffn_out).astype(brain_float)
    grad_rows = (grad_middle + grad_x_norm).astype(brain_float)
    returned = mirror_back(jnp.stack([out_rows[half_width:], grad_rows[half_width:]]), steps)
    out_rows = jnp.concatenate([out_rows[:half_width], returned[0]], axis=0)
    grad_rows = jnp.concatenate([grad_rows[:half_width], returned[1]], axis=0)
    summed = (
        lax.psum_scatter(
            grad_query_weight.astype(jnp.bfloat16), "fsdp", scatter_dimension=1, tiled=True
        ).astype(jnp.float32),
        lax.psum_scatter(
            grad_key_weight.astype(jnp.bfloat16), "fsdp", scatter_dimension=1, tiled=True
        ).astype(jnp.float32),
        lax.psum_scatter(
            grad_value_weight.astype(jnp.bfloat16), "fsdp", scatter_dimension=1, tiled=True
        ).astype(jnp.float32),
        lax.psum_scatter(
            grad_out_weight.astype(jnp.bfloat16), "fsdp", scatter_dimension=1, tiled=True
        ).astype(jnp.float32),
        lax.psum_scatter(
            grad_gate_weight.astype(jnp.bfloat16), "fsdp", scatter_dimension=1, tiled=True
        ).astype(jnp.float32),
        lax.psum_scatter(
            grad_up_weight.astype(jnp.bfloat16), "fsdp", scatter_dimension=1, tiled=True
        ).astype(jnp.float32),
        lax.psum_scatter(
            grad_down_weight.astype(jnp.bfloat16), "fsdp", scatter_dimension=1, tiled=True
        ).astype(jnp.float32),
    )
    final_grads = (
        lax.psum_scatter(
            summed[0].astype(jnp.bfloat16), "ctx", scatter_dimension=0, tiled=True
        ).astype(jnp.float32),
        lax.psum_scatter(
            summed[1].astype(jnp.bfloat16), "ctx", scatter_dimension=0, tiled=True
        ).astype(jnp.float32),
        lax.psum_scatter(
            summed[2].astype(jnp.bfloat16), "ctx", scatter_dimension=0, tiled=True
        ).astype(jnp.float32),
        lax.psum_scatter(
            summed[3].astype(jnp.bfloat16), "ctx", scatter_dimension=0, tiled=True
        ).astype(jnp.float32),
        lax.psum_scatter(
            summed[4].astype(jnp.bfloat16), "ctx", scatter_dimension=0, tiled=True
        ).astype(jnp.float32),
        lax.psum_scatter(
            summed[5].astype(jnp.bfloat16), "ctx", scatter_dimension=0, tiled=True
        ).astype(jnp.float32),
        lax.psum_scatter(
            summed[6].astype(jnp.bfloat16), "ctx", scatter_dimension=0, tiled=True
        ).astype(jnp.float32),
    )
    gains_total = lax.psum(
        (grad_gain_one, grad_gain_two, grad_query_gain, grad_key_gain), ("ctx", "fsdp")
    )
    return (
        out_rows[None],
        grad_rows[None],
        gains_total[0],
        gains_total[1],
        gains_total[2],
        gains_total[3],
        final_grads[0],
        final_grads[1],
        final_grads[2],
        final_grads[3],
        final_grads[4],
        final_grads[5],
        final_grads[6],
    )


def solution(mesh):
    row, whole, split = P("fsdp", "ctx", None), P(), P(None, "fsdp")
    out_split = P("ctx", "fsdp")

    def step(x, dy, lengths, *rest):
        p = Plan(mesh.shape["ctx"], mesh.shape["fsdp"], x.shape[1], x.shape[2], rest[5].shape[1] // HEAD, rest[8].shape[1])
        p.nseq = lengths.shape[1]
        if not p.fits():
            return general(x, dy, lengths, *rest)
        return tuple(local(p, x, dy, lengths, *rest))

    return jax.shard_map(
        step, mesh=mesh,
        in_specs=(row, row, P("fsdp", None), whole, whole, whole, whole) + (split,) * 7,
        out_specs=(row, row, whole, whole, whole, whole) + (out_split,) * 7,
        check_vma=False,
    )
```

```python
import functools
import math
import types

import jax
import jax.numpy as jnp
import numpy as np
from jax import lax
from jax.experimental import pallas as pl
from jax.experimental.pallas import tpu as pltpu
from jax.sharding import PartitionSpec as P

MESH = pl.DeviceIdType.MESH
BF16, F32 = jnp.bfloat16, jnp.float32
HEAD = 64
TILE = 256
EPS = 1e-05
THETA = 1000000.0
PLANES = 4
WINDOW = 3
OUT_SLOTS = 4
FF_SLOTS = 12
EXP2_SCALE = math.log2(math.e) / math.sqrt(HEAD)


def nt_dot(left, right):
    return lax.dot_general(left, right, (((1,), (1,)), ((), ())), preferred_element_type=F32)


def dot(left, right):
    return jnp.dot(left, right, preferred_element_type=F32)


(
    BZ,
    HID,
    DOWN,
    DW,
    BN,
    F,
    S1,
    S2,
    S3,
    S4,
    GM,
    BS,
    BP,
    GB,
    KA,
    KX,
    KZ,
    BF,
    DWO,
    DWQ,
    IG,
    GS,
    GF,
    BO,
    GX,
) = range(25)
PAIR_FIRST = (1, 3, 5, 6)
ORDER = (
    (DOWN, 0), (DW, 0), (HID, 1), (F, 0), (DOWN, 1), (DW, 1), (S1, 0), (HID, 2), (F, 1), (DOWN, 2), (DW, 2), (S1, 1),
    (BN, 0), (BN, 1), (BZ,), (F, 2), (DW, 3), (S1, 2), (DW, 4), (DW, 5), (F, 3), (DW, 6), (S1, 3), (F, 4), (F, 5),
    (S1, 4), (DW, 7), (S1, 5), (S2, 1), (DW, 8), (GM,), (F, 6), (BS, 0), (BP, 0, 0), (BP, 0, 2), (S2, 0), (S2, 3),
    (S1, 6), (KA, 0, 0), (KA, 0, 2), (GB, 1), (BS, 1), (S2, 4), (S2, 5), (F, 7), (BP, 1, 0), (S3, 1), (BP, 1, 2),
    (S1, 7), (S3, 3), (KA, 1, 0), (S3, 0), (S2, 2), (DWO,), (KX, 0, 2), (BP, 0, 1), (KA, 1, 2), (S3, 5), (BP, 1, 1),
    (KA, 0, 1), (KX, 0, 0), (KA, 1, 1), (F, 8), (KX, 1, 2), (KX, 0, 1), (BF, 1), (KZ, 0, 2), (F, 9), (S1, 8),
    (KX, 1, 1), (KZ, 1, 2), (S2, 8), (S2, 6), (S1, 9), (BF, 0), (S3, 2), (BO,), (KZ, 0, 1), (S4, 3), (IG, 0), (S3, 4),
    (KX, 1, 0), (S2, 7), (KZ, 1, 1), (IG, 1), (DWQ, 10), (F, 10), (GS, 0), (S1, 10), (S3, 6), (GF, 0), (DWQ, 11),
    (GS, 1), (F, 11), (S2, 9), (S3, 8), (S1, 11), (GF, 1), (S2, 10), (GX,), (GS, 2), (S3, 7), (S3, 9), (S4, 4),
    (S2, 11), (GF, 2), (S4, 1), (S4, 7), (GS, 3), (S4, 2), (S4, 5), (S3, 10), (S3, 11), (S4, 10), (S4, 6), (GF, 3),
    (S4, 9), (S4, 0), (S4, 8), (S4, 11),
)


class Plan:
    def __init__(self, ctx, groups, rows, width, kv_heads, ff):
        self.A, self.B, self.G = PLANES, ctx // (2 * PLANES), groups
        self.R, self.D, self.KV, self.FL = rows, width, kv_heads, ff
        self.S = width // ctx
        self.nt = ff // TILE
        self.HQ = 128 * kv_heads
        self.no = self.HQ // TILE
        self.tiles = 3 * self.nt + self.no + kv_heads
        self.down, self.gate, self.up, self.out = 0, self.nt, 2 * self.nt, 3 * self.nt
        self.qkv = self.out + self.no
        self.batches = []
        for first, count, step in ((0, 3 * self.nt, 3), (self.out, self.no, 2), (self.qkv, kv_heads, 2)):
            self.batches += [(t, min(step, first + count - t)) for t in range(first, first + count, step)]
        self.ff_batches = -(-3 * self.nt // 3)
        self.pair_first = PAIR_FIRST
        split = ORDER.index((GM,))
        self.order_forward, self.order_backward = ORDER[:split], ORDER[split:]

    def fits(self):
        rows = self.G * self.R
        weights = 2 * self.tiles * self.D * TILE
        keys = 2 * WINDOW * 2 * self.B * self.G * self.KV * self.R * 128
        activations = 2 * rows * (13 * self.D + 3 * self.FL)
        even = self.nt == 9 and self.G == 2 and self.B == 2 and self.no == 2 and self.FL % TILE == 0 and self.HQ % TILE == 0 and self.R % 128 == 0
        return even and weights + keys + activations < 45 << 20


def rotate(u, cos, sin):
    low, high = u[:, :32], u[:, 32:]
    return jnp.concatenate([low * cos - high * sin, high * cos + low * sin], axis=1)


def rotate_back(u, cos, sin):
    low, high = u[:, :32], u[:, 32:]
    return jnp.concatenate([low * cos + high * sin, high * cos - low * sin], axis=1)


AG_AUX, AG_DY, AG_GB, RS_FO, RS_GN2, RS_GN, HEADS, WO = range(8)


def kernel(p, names, *refs):
    r = types.SimpleNamespace(**dict(zip(names, refs)))
    A, B, G, R, D, KV, S = p.A, p.B, p.G, p.R, p.D, p.KV, p.S
    i, f = lax.axis_index("ctx"), lax.axis_index("fsdp")
    c = lax.rem(i, 2)
    b = lax.rem(i // 2, B)
    a = i // (2 * B)
    place = 2 * b + c
    others = range(1, G)

    def at(aa, bb, cc):
        return ((aa * B + bb) * 2 + cc, f)

    def group_device(k):
        return (i, lax.rem(f + k, G))

    def remote(src, dst, send, recv, device):
        return pltpu.make_async_remote_copy(
            src_ref=src, dst_ref=dst, send_sem=send, recv_sem=recv, device_id=device, device_id_type=MESH
        )

    sibling = at(a, b, 1 - c)

    peers = [sibling]
    peers += [at(a, lax.rem(b + k, B), c) for k in range(1, B)]
    peers += [at(lax.rem(a + k, A), b, c) for k in range(1, A)]
    peers += [group_device(k) for k in others]
    barrier = pltpu.get_barrier_semaphore()
    for peer in peers:
        pl.semaphore_signal(barrier, inc=1, device_id=peer, device_id_type=MESH)

    y_sems = r.y_sems

    def gather(kind, buffer, k):
        return remote(buffer.at[0], buffer.at[G - k], y_sems.at[kind, 0, k], y_sems.at[kind, 1, G - k], group_device(k))

    def gathered(kind, buffer, k):
        return remote(buffer.at[k], buffer.at[k], y_sems.at[kind, 0, k], y_sems.at[kind, 1, k], group_device(k))

    def scatter(kind, send, recv, k):
        return remote(send.at[k - 1], recv.at[G - k - 1], y_sems.at[kind, 0, k], y_sems.at[kind, 1, G - k], group_device(k))

    def scattered(kind, send, recv, k):
        return remote(send.at[k - 1], recv.at[k - 1], y_sems.at[kind, 0, k], y_sems.at[kind, 1, k], group_device(k))

    x_all, aux, dy_all = r.x_all, r.aux, r.dy_all
    x_sems_y = r.x_sems_y

    def gather_x(k, q):
        rows = pl.ds(q * (R // 2), R // 2)
        return remote(x_all.at[0, rows], x_all.at[G - k, rows], x_sems_y.at[0, k, q], x_sems_y.at[1, G - k, q], group_device(k))

    def gathered_x(k, q):
        rows = pl.ds(q * (R // 2), R // 2)
        return remote(x_all.at[k, rows], x_all.at[k, rows], x_sems_y.at[0, k, q], x_sems_y.at[1, k, q], group_device(k))

    local_sems = r.local_sems

    def tables():
        where = i * R + lax.broadcasted_iota(jnp.int32, (8, R), 1)
        start = jnp.zeros((8, R), jnp.int32)
        end = jnp.int32(0)
        for j in range(p.nseq):
            end = end + r.lengths[0, j]
            start = jnp.where(where >= end, end, start)
        offset = (where - start).astype(F32)
        steps = lax.broadcasted_iota(jnp.int32, (32, R), 0).astype(F32)
        angle = offset[0:1] * jnp.exp(steps * (-2.0 * math.log(THETA) / HEAD))
        aux[0, 0:32] = jnp.cos(angle)
        aux[0, 32:64] = jnp.sin(angle)
        aux[0, 64:72] = start.astype(F32)
        for j, gain in enumerate((r.query_gain, r.key_gain)):
            wide = jnp.concatenate([jnp.broadcast_to(gain[...], (128, HEAD))] * 2, axis=1)
            r.gain_columns[j * HEAD:(j + 1) * HEAD] = jnp.transpose(wide)[0:HEAD]

    kvw = r.kvw
    z_sems, x_sems, c_sems = r.z_sems, r.x_sems, r.c_sems
    wall = r.wall

    def weight(t):
        return wall[t].reshape(D, TILE)

    def weight_rows(t, aa):
        return wall[t, aa // 2, aa % 2].reshape(D // A, TILE)

    n_t = r.n_t
    raws, q_t, o_acc = r.raws, r.q_t, r.o_acc

    half = R // 2

    def block_half(d, slot, k, q):
        return kvw.at[d, slot, k, :, pl.ds(q * half, half)]

    def z_copy(d, k, q):
        source, target = block_half(d - 1, place, k, q), block_half(d, place, k, q)
        return remote(source, target, z_sems.at[0, d - 1, k, q], z_sems.at[1, d - 1, k, q], at(lax.rem(a + 1, A), b, c))

    def z_arrival(d, k, q):
        slot = block_half(d, place, k, q)
        return remote(slot, slot, z_sems.at[0, d - 1, k, q], z_sems.at[1, d - 1, k, q], at(lax.rem(a + A - 1, A), b, c))

    def x_copy(d, shift, k, q):
        slot = block_half(d, place, k, q)
        return remote(slot, slot, x_sems.at[0, d, shift, k, q], x_sems.at[1, d, shift, k, q], at(a, lax.rem(b + shift, B), c))

    def x_arrival(d, shift, k, q):
        other = lax.rem(b + B - shift, B)
        slot = block_half(d, 2 * other + c, k, q)
        return remote(slot, slot, x_sems.at[0, d, shift, k, q], x_sems.at[1, d, shift, k, q], at(a, other, c))

    def c_copy(d, column, k, q):
        slot = block_half(d, 2 * column + c, k, q)
        return remote(slot, slot, c_sems.at[0, d, column, k, q], c_sems.at[1, d, column, k, q], sibling)

    def c_arrival(d, column, k, q):
        slot = block_half(d, 2 * column + 1 - c, k, q)
        return remote(slot, slot, c_sems.at[0, d, column, k, q], c_sems.at[1, d, column, k, q], sibling)

    def x_needed(d, source, target):
        if d == 0:
            return target > source
        if d == 1:
            return target >= 0
        return target < source

    def c_needed(d, column, core):
        if d == 0:
            return jnp.logical_or(column < b, jnp.logical_and(column == b, core == 0))
        if d == 1:
            return column >= 0
        return jnp.logical_or(column > b, jnp.logical_and(column == b, core == 1))

    def when_all(*conditions):
        whole = conditions[0]
        for condition in conditions[1:]:
            whole = jnp.logical_and(whole, condition)
        return pl.when(whole)

    def onward(d, k, q):
        @when_all(a + 1 < A, a >= d)
        def _():
            z_copy(d + 1, k, q).start()

    def spread(d, k, q):
        for shift in range(1, B):
            @when_all(a >= d, x_needed(d, b, lax.rem(b + shift, B)))
            def _():
                x_copy(d, shift, k, q).start()
        @when_all(a >= d, c_needed(d, b, c))
        def _():
            c_copy(d, b, k, q).start()

    def from_plane(d, k, q):
        @pl.when(a >= d)
        def _():
            z_arrival(d, k, q).wait_recv()

    def from_columns(d, k, q):
        for shift in range(1, B):
            other = lax.rem(b + B - shift, B)
            @when_all(a >= d, x_needed(d, other, b))
            def _():
                x_arrival(d, shift, k, q).wait_recv()
                c_copy(d, other, k, q).start()

    def from_sibling(d, k):
        def step(column, _):
            @when_all(a >= d, c_needed(d, column, 1 - c))
            def _():
                for q in range(2):
                    c_arrival(d, column, k, q).wait_recv()
            return 0
        lax.fori_loop(0, B, step, 0)

    def all_sent(k):
        for q in range(2):
            for d in range(WINDOW):
                if d + 1 < WINDOW:
                    @when_all(a + 1 < A, a >= d)
                    def _():
                        z_copy(d + 1, k, q).wait_send()
                for shift in range(1, B):
                    @when_all(a >= d, x_needed(d, b, lax.rem(b + shift, B)))
                    def _():
                        x_copy(d, shift, k, q).wait_send()
                def step(column, _):
                    @when_all(a >= d, c_needed(d, column, c))
                    def _():
                        c_copy(d, column, k, q).wait_send()
                    return 0
                lax.fori_loop(0, B, step, 0)

    def project(k, first, count):
        rows, lanes = pl.ds(first, count), slice(first, first + count)
        x = x_all[k, rows].astype(F32)
        n = x * lax.rsqrt(jnp.mean(x * x, axis=1, keepdims=True) + EPS) * r.gain_one[...]
        n_rows = n.astype(BF16)
        n_t[:, k * R + first:k * R + first + count] = jnp.transpose(n).astype(BF16)
        cos, sin = aux[k, 0:32, lanes], aux[k, 32:64, lanes]
        q_gain, k_gain = r.gain_columns[0:64, 0:1], r.gain_columns[64:128, 0:1]
        for h in range(KV):
            raw = jnp.transpose(dot(n_rows, weight(p.qkv + h)))
            raws[k, h, :, lanes] = raw[0:192]
            query = raw[0:128].reshape(2, HEAD, count)
            query = query * lax.rsqrt(jnp.mean(query * query, axis=1, keepdims=True) + EPS) * q_gain
            query = rotate(query, cos, sin).astype(BF16)
            for j in range(2):
                q_t[k, h, 0:64, j * R + first:j * R + first + count] = query[j]
                q_t[k, h, 64:128, j * R + first:j * R + first + count] = jnp.zeros((64, count), BF16)
            key = raw[128:192].reshape(1, HEAD, count)
            key = key * lax.rsqrt(jnp.mean(key * key, axis=1, keepdims=True) + EPS) * k_gain
            key = rotate(key, cos, sin).reshape(HEAD, count)
            kv = jnp.concatenate([key, raw[192:256]], axis=0)
            kvw[0, place, k, h, rows] = jnp.transpose(kv).astype(BF16)

    def mask_of(k, key_start, diagonal):
        keys = lax.broadcasted_iota(jnp.int32, (R, 2 * R), 0)
        start = jnp.concatenate([aux[k, 64:65], aux[k, 64:65]], axis=1)
        allowed = (keys + key_start).astype(F32) >= start
        if diagonal:
            query = lax.broadcasted_iota(jnp.int32, (R, 2 * R), 1)
            query = jnp.where(query >= R, query - R, query)
            allowed = jnp.logical_and(allowed, keys <= query)
        return allowed

    def attend(d, other, k, diagonal=False):
        key_start = ((a - d) * 2 * B + other) * R
        allowed = mask_of(k, key_start, diagonal)
        for h in range(KV):
            kv = kvw[d, other, k, h]
            scores = dot(kv, q_t[k, h])
            weights = jnp.where(allowed, jnp.exp2(scores * EXP2_SCALE), 0.0).astype(BF16)
            values = jnp.concatenate([jnp.transpose(kv)[64:128], jnp.ones((16, R), BF16)], axis=0)
            added = dot(values, weights)
            if diagonal:
                o_acc[k, h] = added
            else:
                o_acc[k, h] += added

    def attended(d):
        if d == 0:
            return 0, place
        if d == 1:
            return 0, jnp.where(a >= 1, 2 * B, 0)
        return place, jnp.where(a >= 2, 2 * B, 0)

    def attend_plane(d, k):
        low, high = attended(d)
        def step(other, _):
            attend(d, other, k)
            return 0
        lax.fori_loop(low, high, step, 0)

    mixed = r.mixed
    n2_all = gb_all = r.n2_all
    y_send, y_recv, fo_send, fo_recv = r.y_send, r.y_recv, r.fo_send, r.fo_recv
    part, out_acc, middle = r.part, r.out_acc, r.middle
    gains = r.gains

    def store_part(k, send, own, aa, value):
        columns = slice(aa * (D // A), (aa + 1) * (D // A))
        if k == 0:
            own[:, columns] = value
        else:
            send[k - 1, :, columns] = value.astype(BF16)

    def finish_heads(k):
        for h in range(KV):
            o = o_acc[k, h]
            o_n = o[0:64] / o[64:65]
            o_acc[k, h, 0:64] = o_n
            both = jnp.concatenate([o_n[:, 0:R], o_n[:, R:2 * R]], axis=0)
            mixed[k, :, 128 * h:128 * h + 128] = jnp.transpose(both).astype(BF16)

    mixed_in, wo_other = r.mixed_in, r.wo_other

    def heads_out(k):
        return remote(mixed.at[k], mixed_in.at[1 - k], y_sems.at[HEADS, 0, k], y_sems.at[HEADS, 1, 1 - k], group_device(1))

    def heads_in(k):
        return remote(mixed.at[k], mixed_in.at[k], y_sems.at[HEADS, 0, k], y_sems.at[HEADS, 1, k], group_device(1))

    def out_tile():
        return remote(wall.at[p.out + c], wo_other.at[c], y_sems.at[WO, 0, 0], y_sems.at[WO, 1, 0], group_device(1))

    def out_tile_on():
        return remote(wo_other.at[c], wo_other.at[c], y_sems.at[WO, 0, 1], y_sems.at[WO, 1, 1], sibling)

    def out_tile_in():
        return remote(wo_other.at[1 - c], wo_other.at[1 - c], y_sems.at[WO, 0, 1], y_sems.at[WO, 1, 1], sibling)

    def project_out(k, target):
        for aa in range(A):
            total = jnp.zeros((R, D // A), F32)
            for t in range(p.no):
                lanes = slice(t * TILE, (t + 1) * TILE)
                total += nt_dot(mixed[k, :, lanes], weight_rows(p.out + t, aa))
                other = wo_other[t, aa // 2, aa % 2].reshape(D // A, TILE)
                total += nt_dot(mixed_in[k, :, lanes], other)
            target[:, aa * (D // A):(aa + 1) * (D // A)] = total

    def normed_middle(k, branch, keep):
        for piece in range(R // 128):
            rows = pl.ds(piece * 128, 128)
            v = x_all[k, rows].astype(F32) + branch[rows]
            if keep:
                middle[rows] = v
            n2_all[k, rows] = (v * lax.rsqrt(jnp.mean(v * v, axis=1, keepdims=True) + EPS) * r.gain_two[...]).astype(BF16)

    def load_scope(s_q, s_k, s_v, s_o):
        own_x = pltpu.make_async_copy(r.x.at[0], x_all.at[0], local_sems.at[0])
        loads = [
            pltpu.make_async_copy(source, s, local_sems.at[2 + j])
            for j, (source, s) in enumerate(((r.w_query, s_q), (r.w_key, s_k), (r.w_value, s_v), (r.w_out, s_o)))
        ]
        own_x.start()
        for load in loads:
            load.start()

        def cast_qkv(aa, _):
            rows = pl.ds(aa * (D // A), D // A)
            for h in range(KV):
                whole = jnp.concatenate(
                    [s_q[rows, 128 * h:128 * h + 128], s_k[rows, 64 * h:64 * h + 64], s_v[rows, 64 * h:64 * h + 64]], axis=1
                ).astype(BF16)
                wall[p.qkv + h, aa // 2, lax.rem(aa, 2)] = whole.reshape(B, 2, S, TILE)
            return 0

        def cast_out(aa, _):
            rows = pl.ds(aa * (D // A), D // A)
            for t in range(p.no):
                wall[p.out + t, aa // 2, lax.rem(aa, 2)] = s_o[rows, TILE * t:TILE * (t + 1)].astype(BF16).reshape(B, 2, S, TILE)
            return 0

        tables()
        own_x.wait()
        pl.semaphore_wait(barrier, len(peers))
        for k in others:
            gather(AG_AUX, aux, k).start()
            for q in range(2):
                gather_x(k, q).start()
        for load in loads[:3]:
            load.wait()
        lax.fori_loop(0, A, cast_qkv, 0)
        loads[3].wait()
        lax.fori_loop(0, A, cast_out, 0)

    def forward_scope(stage, stage_sems):
        own_dy = pltpu.make_async_copy(r.dy.at[0], dy_all.at[0], local_sems.at[1])
        ff = ((r.w_gate, p.gate), (r.w_up, p.up), (r.w_down, p.down))
        slots = FF_SLOTS
        chunks = A * B * 2

        def ff_load(source, n):
            rows = pl.ds(n * S, S)
            return pltpu.make_async_copy(source.at[rows], stage.at[lax.rem(n, slots)], stage_sems.at[lax.rem(n, slots)])

        def prime(which):
            for n in range(slots - 1):
                ff_load(ff[which][0], n).start()

        def cast_ff(which):
            source, first = ff[which]
            def step(n, _):
                @pl.when(n + slots - 1 < chunks)
                def _():
                    ff_load(source, n + slots - 1).start()
                ff_load(source, n).wait()
                aa, bb, cc = n // (2 * B), lax.rem(n // 2, B), lax.rem(n, 2)
                for t in range(p.nt):
                    part_of = stage[lax.rem(n, slots), :, t * TILE:(t + 1) * TILE]
                    wall[first + t, aa // 2, lax.rem(aa, 2), bb, cc] = part_of.astype(BF16)
                return 0
            lax.fori_loop(0, chunks, step, 0)
            if which + 1 < len(ff):
                prime(which + 1)

        prime(0)
        own_dy.start()
        halves = range(2)
        project(0, 0, R)
        for q in halves:
            onward(0, 0, q)
            spread(0, 0, q)
        attend(0, place, 0, True)
        own_dy.wait()
        cast_ff(0)
        from_plane(1, 0, 0)
        onward(1, 0, 0)
        spread(1, 0, 0)
        from_columns(0, 0, 0)
        for k in others:
            gathered(AG_AUX, aux, k).wait_recv()
            gathered_x(k, 0).wait_recv()
            project(k, 0, half)
            onward(0, k, 0)
            spread(0, k, 0)
        from_plane(1, 0, 1)
        onward(1, 0, 1)
        spread(1, 0, 1)
        from_columns(0, 0, 1)
        cast_ff(1)
        for k in others:
            gathered_x(k, 1).wait_recv()
            project(k, half, half)
            onward(0, k, 1)
            spread(0, k, 1)
        for k in others:
            gather(AG_DY, dy_all, k).start()
        out_tile().start()
        from_columns(1, 0, 0)
        from_plane(2, 0, 0)
        spread(2, 0, 0)
        for k in others:
            from_plane(1, k, 0)
            onward(1, k, 0)
            spread(1, k, 0)
        cast_ff(2)
        from_columns(1, 0, 1)
        from_sibling(0, 0)
        attend_plane(0, 0)
        for k in others:
            attend(0, place, k, True)
        from_plane(2, 0, 1)
        spread(2, 0, 1)
        for k in others:
            from_plane(1, k, 1)
            onward(1, k, 1)
            spread(1, k, 1)
            for q in halves:
                from_columns(0, k, q)
        from_sibling(1, 0)
        attend_plane(1, 0)
        for k in others:
            @pl.when(b > 0)
            def _():
                for q in halves:
                    from_plane(2, k, q)
                    spread(2, k, q)
        for q in halves:
            from_columns(2, 0, q)
        from_sibling(2, 0)
        attend_plane(2, 0)
        finish_heads(0)
        heads_out(0).start()
        for k in others:
            for q in halves:
                from_columns(1, k, q)
            from_sibling(0, k)
            attend_plane(0, k)
        for k in others:
            from_sibling(1, k)
            attend_plane(1, k)

            @pl.when(b == 0)
            def _():
                for q in halves:
                    from_plane(2, k, q)
                    spread(2, k, q)
            for q in halves:
                from_columns(2, k, q)
            from_sibling(2, k)
            attend_plane(2, k)
            finish_heads(k)
            heads_out(k).start()
        out_tile().wait_recv()
        out_tile_on().start()
        out_tile_in().wait_recv()
        for k in others:
            heads_in(k).wait_recv()
            project_out(k, out_acc)
            normed_middle(k, out_acc, False)
        for k in range(G):
            all_sent(k)
        out_tile().wait_send()
        out_tile_on().wait_send()

    pl.run_scoped(
        load_scope,
        pltpu.VMEM((D, 128 * KV), F32),
        pltpu.VMEM((D, 64 * KV), F32),
        pltpu.VMEM((D, 64 * KV), F32),
        pltpu.VMEM((D, 128 * KV), F32),
    )
    pl.run_scoped(
        forward_scope,
        pltpu.VMEM((FF_SLOTS, S, p.FL), F32),
        pltpu.SemaphoreType.DMA((FF_SLOTS,)),
    )
    for k in others:
        for q in range(2):
            gather_x(k, q).wait_send()
        gather(AG_AUX, aux, k).wait_send()

    rc, r1, r2, r3 = r.rc, r.r1, r.r2, r.r3
    w_sems = r.w_sems
    stage_c, fetch_sems = r.stage_c, r.fetch_sems
    high, low = a // 2, lax.rem(a, 2)
    column_device = at(a, 1 - b, c)
    pair_device = at(2 * high + 1 - low, b, c)

    def sum_core(n):
        t, m = p.batches[n]
        source = wall.at[pl.ds(t, m), :, :, :, 1 - c]
        return remote(source, rc.at[pl.ds(t, m)], w_sems.at[0, 0, n], w_sems.at[1, 0, n], sibling)

    def sum_first(n):
        t, m = p.batches[n]
        if n in p.pair_first:
            source, device = wall.at[pl.ds(t, m), :, 1 - low, :, c], pair_device
        else:
            source, device = wall.at[pl.ds(t, m), :, :, 1 - b, c], column_device
        return remote(source, r1.at[pl.ds(t, m)], w_sems.at[0, 1, n], w_sems.at[1, 1, n], device)

    def sum_second(n):
        t, m = p.batches[n]
        if n in p.pair_first:
            source, device = wall.at[pl.ds(t, m), :, low, 1 - b, c], column_device
        else:
            source, device = wall.at[pl.ds(t, m), :, 1 - low, b, c], pair_device
        return remote(source, r2.at[pl.ds(t, m)], w_sems.at[0, 2, n], w_sems.at[1, 2, n], device)

    def sum_third(n):
        t, m = p.batches[n]
        source = wall.at[pl.ds(t, m), 1 - high, low, b, c]
        return remote(source, r3.at[pl.ds(t, m)], w_sems.at[0, 3, n], w_sems.at[1, 3, n], at(2 * (1 - high) + low, b, c))

    def fetch_core(n):
        t, m = p.batches[n]
        return pltpu.make_async_copy(rc.at[pl.ds(t, m)], stage_c.at[n % 2, pl.ds(0, m)], fetch_sems.at[n % 2])

    def step_core(n):
        sum_core(n).start()

    def step_fetch(n):
        sum_core(n).wait_recv()
        fetch_core(n).start()

    def step_first(n):
        t, m = p.batches[n]
        fetch_core(n).wait()
        def add(j, _):
            tile, hi, lo = j // A, lax.rem(j // 2, 2), lax.rem(j, 2)
            mine = wall[t + tile, hi, lo, :, c].astype(F32) + stage_c[n % 2, tile, hi, lo].astype(F32)
            wall[t + tile, hi, lo, :, c] = mine.astype(BF16)
            return 0
        lax.fori_loop(0, m * A, add, 0)
        sum_first(n).start()

    def step_second(n):
        t, m = p.batches[n]
        sum_first(n).wait_recv()
        def add(tile, _):
            if n in p.pair_first:
                mine = wall[t + tile, :, low, :, c].astype(F32) + r1[t + tile].astype(F32)
                wall[t + tile, :, low, :, c] = mine.astype(BF16)
            else:
                mine = wall[t + tile, :, :, b, c].astype(F32) + r1[t + tile].astype(F32)
                wall[t + tile, :, :, b, c] = mine.astype(BF16)
            return 0
        lax.fori_loop(0, m, add, 0)
        sum_second(n).start()

    def step_third(n):
        t, m = p.batches[n]
        sum_second(n).wait_recv()
        def add(tile, _):
            mine = wall[t + tile, :, low, b, c].astype(F32) + r2[t + tile].astype(F32)
            wall[t + tile, :, low, b, c] = mine.astype(BF16)
            return 0
        lax.fori_loop(0, m, add, 0)
        sum_third(n).start()

    out_stage, out_sems = r.out_stage, r.out_sems

    def out_copy(n):
        t, m = p.batches[n]
        return pltpu.make_async_copy(out_stage.at[n % OUT_SLOTS, pl.ds(0, m)], r.d_weights.at[pl.ds(t, m)], out_sems.at[n % OUT_SLOTS])

    out_order = []

    def step_out(n):
        t, m = p.batches[n]
        for earlier in (sum_core, sum_first, sum_second):
            earlier(n).wait_send()
        sum_third(n).wait_recv()
        for earlier in out_order:
            if earlier % OUT_SLOTS == n % OUT_SLOTS:
                out_copy(earlier).wait()
        out_order[:] = [e for e in out_order if e % OUT_SLOTS != n % OUT_SLOTS] + [n]
        def add(tile, _):
            out_stage[n % OUT_SLOTS, tile] = wall[t + tile, high, low, b, c].astype(F32) + r3[t + tile].astype(F32)
            return 0
        lax.fori_loop(0, m, add, 0)
        out_copy(n).start()

    def run(order, steps):
        steps = {**steps, F: step_fetch, S1: step_first, S2: step_second, S3: step_third, S4: step_out}
        for step, *numbers in order:
            steps[step](*numbers)

    def feed_forward(hs, n2_t, dy_t):
        def turned(source, k, target):
            for piece in range(R // 128):
                rows = pl.ds(piece * 128, 128)
                target[:, k * R + piece * 128:k * R + (piece + 1) * 128] = jnp.transpose(source[k, rows].astype(F32)).astype(BF16)

        def hidden(k, first, count):
            rows = slice(k * R, (k + 1) * R)
            def step(t, _):
                gate = dot(n2_all[k], weight(p.gate + t))
                up = dot(n2_all[k], weight(p.up + t))
                grad = dot(dy_all[k], weight(p.down + t))
                sig = 1.0 / (1.0 + jnp.exp(-gate))
                silu = gate * sig
                hs[2, t, rows] = (silu * up).astype(BF16)
                hs[0, t, rows] = (grad * up * (sig * (1.0 + gate * (1.0 - sig)))).astype(BF16)
                hs[1, t, rows] = (grad * silu).astype(BF16)
                return 0
            lax.fori_loop(first, first + count, step, 0)

        def back_normed(k, parts):
            rows = slice(k * R, (k + 1) * R)
            for aa in parts:
                total = jnp.zeros((R, D // A), F32)
                for t in range(p.nt):
                    total += nt_dot(hs[0, t, rows], weight_rows(p.gate + t, aa))
                    total += nt_dot(hs[1, t, rows], weight_rows(p.up + t, aa))
                store_part(k, y_send, part, aa, total)

        def down(k, first, count):
            rows = slice(k * R, (k + 1) * R)
            for aa in range(A):
                columns = slice(aa * (D // A), (aa + 1) * (D // A))
                total = jnp.zeros((R, D // A), F32)
                for t in range(first, first + count):
                    total += nt_dot(hs[2, t, rows], weight_rows(p.down + t, aa))
                if k:
                    store_part(k, fo_send, None, aa, total)
                else:
                    out_acc[:, columns] = (out_acc if first else middle)[:, columns] + total

        def weight_gradients(n):
            t, m = p.batches[n]
            for tile in range(t, t + m):
                kind, u = (2, 0, 1)[tile // p.nt], tile % p.nt
                left = dy_t if kind == 2 else n2_t
                for aa in range(A):
                    rows = slice(aa * (D // A), (aa + 1) * (D // A))
                    wall[tile, aa // 2, aa % 2] = dot(left[rows], hs[kind, u]).astype(BF16).reshape(B, 2, S, TILE)

        third = p.batches[0][1]
        for k in others:
            gathered(AG_DY, dy_all, k).wait_recv()
            hidden(k, 0, p.nt)
            turned(dy_all, k, dy_t)
            turned(n2_all, k, n2_t)
            down(k, 0, p.nt)
        turned(dy_all, 0, dy_t)
        heads_in(0).wait_recv()
        project_out(0, part)
        normed_middle(0, part, True)
        turned(n2_all, 0, n2_t)
        hidden(0, 0, third)

        def hidden_part(j):
            hidden(0, j * third, third)

        def down_part(j):
            down(0, j * third, third)

        def gradients_and_core(n):
            weight_gradients(n)
            step_core(n)

        def back_normed_half(half):
            for k in others:
                back_normed(k, range(half * A // 2, (half + 1) * A // 2))
                if half:
                    scatter(RS_GN2, y_send, y_recv, k).start()

        run(p.order_forward, {
            HID: hidden_part, DOWN: down_part, DW: gradients_and_core, BN: back_normed_half,
            BZ: lambda: back_normed(0, range(A)),
        })

    pl.run_scoped(
        feed_forward,
        pltpu.VMEM((3, p.nt, G * R, TILE), BF16),
        pltpu.VMEM((D, G * R), BF16),
        pltpu.VMEM((D, G * R), BF16),
    )
    last = p.ff_batches


    def middle_gradient():
        for k in others:
            scattered(RS_GN2, y_send, y_recv, k).wait_recv()
        gain_grad = jnp.zeros((1, D), F32)
        for piece in range(R // 128):
            rows = pl.ds(piece * 128, 128)
            e = part[rows]
            for k in others:
                e += y_recv[k - 1, rows].astype(F32)
            v = middle[rows]
            rr = lax.rsqrt(jnp.mean(v * v, axis=1, keepdims=True) + EPS)
            vh = v * rr
            gain_grad += jnp.sum(e * vh, axis=0, keepdims=True)
            ge = e * r.gain_two[...]
            gm = dy_all[0, rows].astype(F32) + rr * (ge - vh * jnp.mean(vh * ge, axis=1, keepdims=True))
            middle[rows] = gm
            r.gb_t[:, piece * 128:(piece + 1) * 128] = jnp.transpose(gm).astype(BF16)
        gains[...] = jnp.zeros((8, D), F32)
        gains[0:1] = gain_grad
        gb_all[0] = middle[...].astype(BF16)
        for k in others:
            gather(AG_GB, gb_all, k).start()

    dm = r.dm
    graw = r.graw
    kvr, xr, zr = r.kvr, r.xr, r.zr
    kc_sems, kx_sems, kz_sems = r.kc_sems, r.kx_sems, r.kz_sems
    head_sums = r.head_sums
    head_sums[...] = jnp.zeros((128, R), F32)

    def k_core(d, column, k):
        return remote(kvw.at[d, 2 * column + 1 - c, k], kvr.at[d, column, k], kc_sems.at[0, d, column, k], kc_sems.at[1, d, column, k], sibling)

    def k_column(d, shift, k):
        target = lax.rem(b + shift, B)
        return remote(kvw.at[d, 2 * target + c, k], xr.at[d, shift - 1, k], kx_sems.at[0, d, shift, k], kx_sems.at[1, d, shift, k], at(a, target, c))

    def k_plane(d, k):
        return remote(kvw.at[d, place, k], zr.at[d - 1, k], kz_sems.at[0, d - 1, k], kz_sems.at[1, d - 1, k], at(lax.rem(a + A - 1, A), b, c))

    def in_window(d, column, core, from_core):
        if d == 0:
            return jnp.logical_or(column < b, jnp.logical_and(column == b, core <= from_core))
        if d == 1:
            return column >= 0
        return jnp.logical_or(column > b, jnp.logical_and(column == b, core >= from_core))

    def column_reached(d, target, source):
        if d == 0:
            return target < source
        if d == 1:
            return target >= 0
        return target > source

    def keys_core(d, k):
        for column in range(B):
            @when_all(a >= d, in_window(d, column, 1 - c, c))
            def _():
                k_core(d, column, k).start()

    def keys_add(d, k, kv_stage, kv_sems):
        def fetch(column):
            return pltpu.make_async_copy(kvr.at[d, column, k], kv_stage.at[column], kv_sems.at[column])

        for column in range(B):
            @when_all(a >= d, in_window(d, column, c, 1 - c))
            def _():
                k_core(d, column, k).wait_recv()
                fetch(column).start()
        for column in range(B):
            @when_all(a >= d, in_window(d, column, c, 1 - c))
            def _():
                fetch(column).wait()
                for h in range(KV):
                    slot = 2 * column + c
                    kvw[d, slot, k, h] = (kvw[d, slot, k, h].astype(F32) + kv_stage[column, h].astype(F32)).astype(BF16)
        for shift in range(1, B):
            @when_all(a >= d, column_reached(d, lax.rem(b + shift, B), b))
            def _():
                k_column(d, shift, k).start()

    def keys_columns(d, k):
        for shift in range(1, B):
            @when_all(a >= d, column_reached(d, b, lax.rem(b + B - shift, B)))
            def _():
                k_column(d, shift, k).wait_recv()
                for h in range(KV):
                    kvw[d, place, k, h] = (kvw[d, place, k, h].astype(F32) + xr[d, shift - 1, k, h].astype(F32)).astype(BF16)

    def keys_plane(d, k):
        @pl.when(a >= d)
        def _():
            k_plane(d, k).start()

    def keys_from_plane(d, k):
        @when_all(a + 1 < A, a + 1 >= d)
        def _():
            k_plane(d, k).wait_recv()
            for h in range(KV):
                kvw[d - 1, place, k, h] = (kvw[d - 1, place, k, h].astype(F32) + zr[d - 1, k, h].astype(F32)).astype(BF16)

    def keys_sent(k):
        for d in range(WINDOW):
            for column in range(B):
                @when_all(a >= d, in_window(d, column, 1 - c, c))
                def _():
                    k_core(d, column, k).wait_send()
            for shift in range(1, B):
                @when_all(a >= d, column_reached(d, lax.rem(b + shift, B), b))
                def _():
                    k_column(d, shift, k).wait_send()
            if d:
                @pl.when(a >= d)
                def _():
                    k_plane(d, k).wait_send()

    def rms_back(raw, e, gain):
        rr = lax.rsqrt(jnp.mean(raw * raw, axis=1, keepdims=True) + EPS)
        vh = raw * rr
        ge = e * gain
        return jnp.sum(e * vh, axis=0), rr * (ge - vh * jnp.mean(vh * ge, axis=1, keepdims=True))

    def back_start(k, do_t, do_rows, q_rows, dq, rows_of):
        for t in range(p.no):
            dm[:, t * TILE:(t + 1) * TILE] = dot(gb_all[k], weight(p.out + t)).astype(BF16)
        for h in range(KV):
            turned = jnp.transpose(dm[:, 128 * h:128 * h + 128].astype(F32))
            grad = jnp.concatenate([turned[0:64], turned[64:128]], axis=1)
            rows_of[k, h, 0:1] = jnp.log2(o_acc[k, h, 64:65])
            rows_of[k, h, 1:2] = jnp.sum(grad * o_acc[k, h, 0:64], axis=0, keepdims=True)
            padded = jnp.concatenate([jnp.zeros((64, 2 * R), F32), grad], axis=0)
            do_t[k, h] = padded.astype(BF16)
            do_rows[k, h] = jnp.transpose(padded).astype(BF16)
            q_rows[k, h] = (jnp.transpose(q_t[k, h].astype(F32)) * (1.0 / math.sqrt(HEAD))).astype(BF16)
            dq[k, h] = jnp.zeros((64, 2 * R), F32)

    def back_block(k, d, other, do_t, do_rows, q_rows, dq, rows_of, diagonal=False):
        key_start = ((a - d) * 2 * B + other) * R
        allowed = mask_of(k, key_start, diagonal)
        for h in range(KV):
            kv = kvw[d, other, k, h]
            scores = dot(kv, q_t[k, h])
            probs = jnp.where(allowed, jnp.exp2(scores * EXP2_SCALE - rows_of[k, h, 0:1]), 0.0)
            grad = dot(kv, do_t[k, h])
            grad_scores = (probs * (grad - rows_of[k, h, 1:2])).astype(BF16)
            kvw[d, other, k, h] = (dot(grad_scores, q_rows[k, h]) + dot(probs.astype(BF16), do_rows[k, h])).astype(BF16)
            dq[k, h] += dot(jnp.transpose(kv)[0:64], grad_scores)

    def back_plane(k, d, *scratch):
        if d == 0:
            back_block(k, 0, place, *scratch, diagonal=True)
        low, high = attended(d)
        def step(other, _):
            back_block(k, d, other, *scratch)
            return 0
        lax.fori_loop(low, high, step, 0)
        keys_core(d, k)

    def back_finish(k, dq):
        cos, sin = aux[k, 0:32], aux[k, 32:64]
        for h in range(KV):
            e = (dq[k, h] * (1.0 / math.sqrt(HEAD))).astype(BF16).astype(F32)
            e = rotate_back(jnp.stack([e[:, 0:R], e[:, R:2 * R]]), cos, sin)
            gain_part, grad = rms_back(raws[k, h, 0:128].reshape(2, HEAD, R), e, r.gain_columns[0:64, 0:1])
            head_sums[0:64] += gain_part
            graw[h, k * R:(k + 1) * R, 0:128] = jnp.transpose(grad.reshape(128, R)).astype(BF16)

    def keys_back(k):
        cos, sin = aux[k, 0:32], aux[k, 32:64]
        for h in range(KV):
            final = jnp.transpose(kvw[0, place, k, h].astype(F32))
            e = rotate_back(final[0:64].reshape(1, HEAD, R), cos, sin)
            gain_part, grad = rms_back(raws[k, h, 128:192].reshape(1, HEAD, R), e, r.gain_columns[64:128, 0:1])
            head_sums[64:128] += gain_part
            both = jnp.concatenate([grad.reshape(HEAD, R), final[64:128]], axis=0)
            graw[h, k * R:(k + 1) * R, 128:256] = jnp.transpose(both).astype(BF16)

    xg = r.xg

    def input_gradient(k):
        for aa in range(A):
            columns = slice(aa * (D // A), (aa + 1) * (D // A))
            total = jnp.zeros((R, D // A), F32)
            for h in range(KV):
                total += nt_dot(graw[h, k * R:(k + 1) * R], weight_rows(p.qkv + h, aa))
            store_part(k, y_send, part, aa, total)
            x = x_all[k, :, columns].astype(F32)
            xg[:, columns] += jnp.sum(total * x * x_scale(k), axis=0, keepdims=True)

    def x_scale(k):
        return r.x_scale[k, :, 0:1]

    def out_gradient():
        for t in range(p.no):
            for aa in range(A):
                rows = slice(aa * (D // A), (aa + 1) * (D // A))
                total = jnp.zeros((D // A, TILE), F32)
                for k in range(G):
                    total += dot(r.gb_t[rows, k * R:(k + 1) * R], mixed[k, :, t * TILE:(t + 1) * TILE])
                wall[p.out + t, aa // 2, aa % 2] = total.astype(BF16).reshape(B, 2, S, TILE)
        step_core(p.ff_batches)

    def qkv_gradient(n):
        t, m = p.batches[n]
        for tile in range(t, t + m):
            for aa in range(A):
                rows = slice(aa * (D // A), (aa + 1) * (D // A))
                wall[tile, aa // 2, aa % 2] = dot(n_t[rows], graw[tile - p.qkv]).astype(BF16).reshape(B, 2, S, TILE)
        step_core(n)

    def branch_arrives(k):
        gathered(AG_GB, gb_all, k).wait_recv()
        scatter(RS_FO, fo_send, fo_recv, k).start()
        for piece in range(R // 128):
            rows = pl.ds(piece * 128, 128)
            r.gb_t[:, k * R + piece * 128:k * R + (piece + 1) * 128] = jnp.transpose(gb_all[k, rows].astype(F32)).astype(BF16)

    def keys_over_columns(k, d):
        keys_columns(d, k)
        if d == 2:
            keys_plane(2, k)

    def keys_over_planes(k, d):
        keys_from_plane(d, k)
        if d == 2:
            keys_plane(1, k)
        else:
            keys_back(k)

    def input_step(k):
        if k:
            scatter(RS_GN2, y_send, y_recv, k).wait_send()
        input_gradient(k)
        if k:
            scatter(RS_GN, y_send, y_recv, k).start()

    g_land, g_sems = r.g_land, r.g_sems
    stages = [
        (2, c, 0, lambda j: at(a, b, j)),
        (G, f, 2, lambda j: (i, j)),
        (B, b, 2 + G, lambda j: at(a, j, c)),
        (A, a, 2 + G + B, lambda j: at(j, b, c)),
    ]

    def gain_send(s, shift):
        size, mine, base, device = stages[s]
        return remote(gains, g_land.at[base + mine], g_sems.at[0, s, shift], g_sems.at[1, s, shift], device(lax.rem(mine + shift, size)))

    def gain_arrival(s, shift):
        size, mine, base, device = stages[s]
        slot = lax.rem(mine + size - shift, size)
        return remote(gains, g_land.at[base + slot], g_sems.at[0, s, shift], g_sems.at[1, s, shift], device(slot))

    def gain_start(s):
        size, mine, base, _ = stages[s]
        for shift in range(1, size):
            gain_send(s, shift).start()
        g_land[base + mine] = gains[...]

    def gain_finish(s):
        size, _, base, _ = stages[s]
        for shift in range(1, size):
            gain_arrival(s, shift).wait_recv()
            gain_send(s, shift).wait_send()
        total = g_land[base]
        for j in range(1, size):
            total += g_land[base + j]
        gains[...] = total

    def gain_first(s):
        if s == 0:
            gains[1:2] = xg[...]
            gains[2:3, 0:128] = jnp.sum(jnp.transpose(head_sums[...]), axis=0, keepdims=True)
        gain_start(s)

    def rows_out(j):
        source, target = ((r.block_rows, r.block_out), (r.grad_rows, r.grad_inputs))[j]
        return pltpu.make_async_copy(source, target.at[0], local_sems.at[6 + j])

    def block_rows():
        for k in others:
            scattered(RS_FO, fo_send, fo_recv, k).wait_recv()
        for piece in range(R // 128):
            rows = pl.ds(piece * 128, 128)
            v = out_acc[rows]
            for k in others:
                v += fo_recv[k - 1, rows].astype(F32)
            r.block_rows[rows] = v.astype(BF16)

        rows_out(0).start()

    def input_rows():
        for k in range(G):
            keys_sent(k)
            heads_out(k).wait_send()
        for k in others:
            gather(AG_DY, dy_all, k).wait_send()
            gather(AG_GB, gb_all, k).wait_send()
            scatter(RS_FO, fo_send, fo_recv, k).wait_send()
            scatter(RS_GN, y_send, y_recv, k).wait_send()
        for k in others:
            scattered(RS_GN, y_send, y_recv, k).wait_recv()
        for piece in range(R // 128):
            rows = pl.ds(piece * 128, 128)
            e = part[rows]
            for k in others:
                e += y_recv[k - 1, rows].astype(F32)
            v = x_all[0, rows].astype(F32)
            rr = r.x_scale[0, rows, 0:1]
            vh = v * rr
            ge = e * r.gain_one[...]
            back = rr * (ge - vh * jnp.mean(vh * ge, axis=1, keepdims=True))
            r.grad_rows[rows] = (middle[rows] + back).astype(BF16)

        rows_out(1).start()

    def backward_scope(do_t, do_rows, q_rows, dq, rows_of, kv_stage, kv_sems, gb_t):
        r.gb_t = gb_t
        scratch = (do_t, do_rows, q_rows, dq, rows_of)
        steps = {
            GM: middle_gradient, BS: lambda k: back_start(k, *scratch), BP: lambda k, d: back_plane(k, d, *scratch),
            GB: branch_arrives, KA: lambda k, d: keys_add(d, k, kv_stage, kv_sems), KX: keys_over_columns, KZ: keys_over_planes,
            BF: lambda k: back_finish(k, dq), DWO: out_gradient, DWQ: qkv_gradient, IG: input_step, GS: gain_first,
            GF: gain_finish, BO: block_rows, GX: input_rows,
        }
        run(p.order_backward, steps)

    xg[...] = jnp.zeros((1, D), F32)
    for k in range(G):
        x = x_all[k].astype(F32)
        r.x_scale[k] = jnp.broadcast_to(lax.rsqrt(jnp.mean(x * x, axis=1, keepdims=True) + EPS), (R, 128))
    pl.run_scoped(
        backward_scope,
        pltpu.VMEM((G, KV, 128, 2 * R), BF16),
        pltpu.VMEM((G, KV, 2 * R, 128), BF16),
        pltpu.VMEM((G, KV, 2 * R, 128), BF16),
        pltpu.VMEM((G, KV, 64, 2 * R), F32),
        pltpu.VMEM((G, KV, 8, 2 * R), F32),
        pltpu.VMEM((B, KV, R, 128), BF16),
        pltpu.SemaphoreType.DMA((B,)),
        pltpu.VMEM((D, G * R), BF16),
    )
    r.d_gains[...] = gains[...]
    for n in out_order:
        out_copy(n).wait()
    for j in range(2):
        rows_out(j).wait()

    for n in range(len(p.batches)):
        sum_third(n).wait_send()


def local(p, x, dy, lengths, gain_one, gain_two, query_gain, key_gain, wq, wk, wv, wo, wg, wu, wd):
    A, B, G, R, D, KV, S = p.A, p.B, p.G, p.R, p.D, p.KV, p.S
    any_spec, vmem, smem = (pl.BlockSpec(memory_space=m) for m in (pl.ANY, pltpu.VMEM, pltpu.SMEM))
    ins = dict(
        x=(x, any_spec), dy=(dy, any_spec), lengths=(lengths, smem), gain_one=(gain_one[None], vmem),
        gain_two=(gain_two[None], vmem), query_gain=(query_gain[None], vmem), key_gain=(key_gain[None], vmem),
        w_query=(wq, any_spec), w_key=(wk, any_spec), w_value=(wv, any_spec), w_out=(wo, any_spec),
        w_gate=(wg, any_spec), w_up=(wu, any_spec), w_down=(wd, any_spec),
    )
    rows_out = ((1, R, D), BF16)
    outs = dict(d_gains=((8, D), F32))
    landing = dict(
        block_out=rows_out, grad_inputs=rows_out,
        d_weights=((p.tiles, S, TILE), F32), rc=((p.tiles, 2, 2, B, S, TILE), BF16), kvr=((WINDOW, B, G, KV, R, 128), BF16),
    )
    DMA = pltpu.SemaphoreType.DMA
    n_batches, widest = len(p.batches), max(m for _, m in p.batches)
    scratch = dict(
        x_all=pltpu.VMEM((G, R, D), BF16), aux=pltpu.VMEM((G, 72, R), F32), dy_all=pltpu.VMEM((G, R, D), BF16),
        y_sems=DMA((8, 2, G)), x_sems_y=DMA((2, G, 2)), local_sems=DMA((8,)),
        gain_columns=pltpu.VMEM((128, 128), F32),
        kvw=pltpu.VMEM((WINDOW, 2 * B, G, KV, R, 128), BF16),
        z_sems=DMA((2, 2, G, 2)), x_sems=DMA((2, WINDOW, B, G, 2)), c_sems=DMA((2, WINDOW, B, G, 2)),
        wall=pltpu.VMEM((p.tiles, 2, 2, B, 2, S, TILE), BF16),
        n_t=pltpu.VMEM((D, G * R), BF16),
        raws=pltpu.VMEM((G, KV, 192, R), F32), q_t=pltpu.VMEM((G, KV, 128, 2 * R), BF16),
        o_acc=pltpu.VMEM((G, KV, 80, 2 * R), F32), mixed=pltpu.VMEM((G, R, p.HQ), BF16),
        y_send=pltpu.VMEM((G - 1, R, D), BF16), y_recv=pltpu.VMEM((G - 1, R, D), BF16),
        fo_send=pltpu.VMEM((G - 1, R, D), BF16), fo_recv=pltpu.VMEM((G - 1, R, D), BF16),
        part=pltpu.VMEM((R, D), F32), out_acc=pltpu.VMEM((R, D), F32), middle=pltpu.VMEM((R, D), F32),
        n2_all=pltpu.VMEM((G, R, D), BF16), mixed_in=pltpu.VMEM((G, R, p.HQ), BF16), wo_other=pltpu.VMEM((p.no, 2, 2, B, 2, S, TILE), BF16),
        block_rows=pltpu.VMEM((R, D), BF16), grad_rows=pltpu.VMEM((R, D), BF16), gains=pltpu.VMEM((8, D), F32), xg=pltpu.VMEM((1, D), F32), x_scale=pltpu.VMEM((G, R, 128), F32),
        w_sems=DMA((2, 4, n_batches)), fetch_sems=DMA((2,)), stage_c=pltpu.VMEM((2, widest, 2, 2, B, S, TILE), BF16),
        r1=pltpu.VMEM((p.tiles, 2, 2, S, TILE), BF16), r2=pltpu.VMEM((p.tiles, 2, S, TILE), BF16),
        r3=pltpu.VMEM((p.tiles, S, TILE), BF16), out_stage=pltpu.VMEM((OUT_SLOTS, widest, S, TILE), F32), out_sems=DMA((OUT_SLOTS,)),
        dm=pltpu.VMEM((R, p.HQ), BF16), graw=pltpu.VMEM((KV, G * R, TILE), BF16),
        xr=pltpu.VMEM((WINDOW, B - 1, G, KV, R, 128), BF16), zr=pltpu.VMEM((2, G, KV, R, 128), BF16),
        kc_sems=DMA((2, WINDOW, B, G)), kx_sems=DMA((2, WINDOW, B, G)), kz_sems=DMA((2, 2, G)),
        head_sums=pltpu.VMEM((128, R), F32),
        g_land=pltpu.VMEM((2 + B + A + G, 8, D), F32), g_sems=DMA((2, 4, max(A, B, G, 2))),
    )
    outs_all = dict(outs, **landing)
    out_specs = [vmem for _ in outs] + [any_spec for _ in landing]
    names = list(ins) + list(outs_all) + list(scratch)
    results = pl.pallas_call(
        functools.partial(kernel, p, names),
        out_shape=[jax.ShapeDtypeStruct(*o) for o in outs_all.values()],
        in_specs=[s for _, s in ins.values()],
        out_specs=out_specs,
        scratch_shapes=list(scratch.values()),
        compiler_params=pltpu.CompilerParams(collective_id=0, has_side_effects=True, vmem_limit_bytes=64 << 20),
        name="block",
    )(*[v for v, _ in ins.values()])
    o = dict(zip(outs_all, results))
    o = types.SimpleNamespace(**o)
    packed = [o.block_out, o.grad_inputs, o.d_gains, o.d_weights]
    shapes = [(packed[0].shape, BF16), (packed[0].shape, BF16), ((D,), F32), ((D,), F32), ((HEAD,), F32), ((HEAD,), F32)]
    shapes += [((S, n), F32) for n in (128 * KV, 64 * KV, 64 * KV, 128 * KV, p.FL, p.FL, p.FL)]
    return pl.pallas_call(
        functools.partial(split_kernel, p),
        out_shape=[jax.ShapeDtypeStruct(*shape) for shape in shapes],
        in_specs=[vmem] * len(packed),
        out_specs=[vmem] * len(shapes),
        name="split",
    )(*packed)


def split_kernel(p, out_in, grad_in, gains, tiles, block_out, grad_inputs, g_one, g_two, g_query, g_key, d_query, d_key, d_value, d_out, d_gate, d_up, d_down):
    block_out[...] = out_in[...]
    grad_inputs[...] = grad_in[...]
    g_one[...] = gains[1]
    g_two[...] = gains[0]
    g_query[...] = gains[2, 0:HEAD]
    g_key[...] = gains[2, HEAD:2 * HEAD]
    for ref, first, count in ((d_gate, p.gate, p.nt), (d_up, p.up, p.nt), (d_down, p.down, p.nt), (d_out, p.out, p.no)):
        for t in range(count):
            ref[:, t * TILE:(t + 1) * TILE] = tiles[first + t]
    for h in range(p.KV):
        tile = tiles[p.qkv + h]
        d_query[:, 128 * h:128 * h + 128] = tile[:, 0:128]
        d_key[:, 64 * h:64 * h + 64] = tile[:, 128:192]
        d_value[:, 64 * h:64 * h + 64] = tile[:, 192:256]


QUERY_HEADS = 16
KEY_VALUE_HEADS = 8
HEAD_SIZE = HEAD


MASKED_FILL = -1e30


def swapped(value, axis, bit):
    mask = 2**bit
    pairs = [(source, source ^ mask) for source in range(lax.axis_size(axis))]
    return lax.ppermute(value, axis, pairs)


def root_mean_norm(values, gain):
    return values * lax.rsqrt(jnp.mean(values * values, axis=-1, keepdims=True) + EPS) * gain


def apply_rotary(values, cosine_table, sine_table):
    half_width = values.shape[-1] // 2
    turned = jnp.concatenate([-values[..., half_width:], values[..., :half_width]], axis=-1)
    return values * cosine_table + turned * sine_table


def places(lengths, where):
    ends = jnp.cumsum(lengths)
    before = (ends[None, :] <= where[:, None]).astype(jnp.int32)
    segment = jnp.sum(before, axis=1)
    offset = where - jnp.sum(before * lengths[None, :], axis=1)
    return (segment, offset)


def head_post(query_raw, unrotated_key, query_gain, key_norm_gain, cosine_table, sine_table):
    token_count = query_raw.shape[0]
    query_rot = apply_rotary(
        root_mean_norm(query_raw.reshape(token_count, QUERY_HEADS, HEAD_SIZE), query_gain),
        cosine_table,
        sine_table,
    )
    rotated_key = apply_rotary(
        root_mean_norm(
            unrotated_key.reshape(token_count, KEY_VALUE_HEADS, HEAD_SIZE), key_norm_gain
        ),
        cosine_table,
        sine_table,
    )
    return (query_rot, rotated_key)


def swiglu(gate, upward):
    return jax.nn.silu(gate) * upward


def matmul(left, right):
    return jnp.dot(left, right, preferred_element_type=jnp.float32)


def project_back(left, right):
    return lax.dot_general(
        left, right, (((1,), (1,)), ((), ())), preferred_element_type=jnp.float32
    )


def outer_sum(left, right):
    return lax.dot_general(
        left, right, (((0,), (0,)), ((), ())), preferred_element_type=jnp.float32
    )


def mirror_out(payload, steps):
    for bit in range(steps):
        payload = swapped(payload, "ctx", bit)
    return payload


def mirror_back(payload, steps):
    for bit in range(steps):
        payload = swapped(payload, "ctx", bit)
    return payload


def halves_order(array, parts):
    shaped = array.reshape((parts, 2, array.shape[0] // (2 * parts)) + array.shape[1:])
    return jnp.stack([shaped[:, 0], shaped[::-1, 1]], axis=1).reshape(array.shape)


def general(
    inputs,
    cotangent,
    lengths,
    gain_one,
    gain_two,
    query_gain,
    key_norm_gain,
    w_query,
    key_projection,
    value_projection,
    w_out,
    w_gate,
    w_up,
    w_down,
):
    brain_float = jnp.bfloat16
    parts = lax.axis_size("ctx")
    steps = parts.bit_length() - 1
    device_index = lax.axis_index("ctx")
    row_count = inputs.shape[1]
    head_group = row_count * parts
    half_width = row_count // 2
    own_lengths = lengths[0]
    offsets_half = jnp.arange(half_width, dtype=jnp.int32)
    arrived = mirror_out(jnp.stack([inputs[0][half_width:], cotangent[0][half_width:]]), steps)
    x_rows = jnp.concatenate([inputs[0][:half_width], arrived[0]], axis=0)
    dy_rows = jnp.concatenate([cotangent[0][:half_width], arrived[1]], axis=0)
    query_place = jnp.concatenate(
        [
            device_index * row_count + offsets_half,
            (parts - 1 - device_index) * row_count + half_width + offsets_half,
        ]
    )
    key_place = jnp.arange(head_group, dtype=jnp.int32)
    query_segment, query_offset = places(own_lengths, query_place)
    key_segment, key_offset = places(own_lengths, key_place)
    weight_query, weight_key, weight_value, weight_out = (
        lax.all_gather(w_query.astype(brain_float), "fsdp", axis=1, tiled=True),
        lax.all_gather(key_projection.astype(brain_float), "fsdp", axis=1, tiled=True),
        lax.all_gather(value_projection.astype(brain_float), "fsdp", axis=1, tiled=True),
        lax.all_gather(w_out.astype(brain_float), "fsdp", axis=1, tiled=True),
    )
    x_float = x_rows.astype(jnp.float32)
    normed_f, norm_one_back = jax.vjp(root_mean_norm, x_float, gain_one)
    normed_input = normed_f.astype(brain_float)
    query_raw = matmul(normed_input, weight_query)
    unrotated_key = matmul(normed_input, weight_key)
    value_b = matmul(normed_input, weight_value).astype(brain_float)
    freq = jnp.exp(
        jnp.arange(HEAD_SIZE // 2, dtype=jnp.float32) * (-2.0 * math.log(THETA) / HEAD_SIZE)
    )
    angle = query_offset.astype(jnp.float32)[:, None] * freq[None, :]
    cosine_table = jnp.concatenate([jnp.cos(angle), jnp.cos(angle)], axis=-1)[:, None, :]
    sine_table = jnp.concatenate([jnp.sin(angle), jnp.sin(angle)], axis=-1)[:, None, :]

    def post_local(query_in, key_in, gain_q, gain_k):
        return head_post(query_in, key_in, gain_q, gain_k, cosine_table, sine_table)

    (query_rot, rotated_key), post_back = jax.vjp(
        post_local, query_raw, unrotated_key, query_gain, key_norm_gain
    )
    query_batch = query_rot.astype(brain_float)
    key_batch = rotated_key.astype(brain_float).reshape(row_count, KEY_VALUE_HEADS * HEAD_SIZE)
    gathered_keys, gathered_values = (
        lax.all_gather(key_batch, "ctx", axis=0, tiled=True),
        lax.all_gather(value_b, "ctx", axis=0, tiled=True),
    )
    gathered_keys = halves_order(gathered_keys, parts)
    gathered_values = halves_order(gathered_values, parts)
    shared_heads = QUERY_HEADS // KEY_VALUE_HEADS
    score_scale = 1.0 / math.sqrt(HEAD_SIZE)
    keys_per_block = min(1024, head_group)
    block_count = head_group // keys_per_block
    query_quad = query_batch.reshape(row_count, KEY_VALUE_HEADS, shared_heads, HEAD_SIZE)
    blocked_keys = gathered_keys.reshape(block_count, keys_per_block, KEY_VALUE_HEADS, HEAD_SIZE)
    blocked_values = gathered_values.reshape(
        block_count, keys_per_block, KEY_VALUE_HEADS, HEAD_SIZE
    )
    segment_blocks = key_segment.reshape(block_count, keys_per_block)
    place_blocks = key_place.reshape(block_count, keys_per_block)

    def tile_backward(query_tile, tile_segment, tile_place, tile_log, grad_tile, tile_delta):

        def allowed_of(segment_block, place_block):
            return (tile_segment[:, None] == segment_block[None, :]) & (
                tile_place[:, None] >= place_block[None, :]
            )

        def back_step(carry, block):
            key_block, value_block, segment_block, place_block = block
            allowed = allowed_of(segment_block, place_block)

            def back_active(grad_query):
                raw_scores = (
                    jnp.einsum(
                        "qhgd,khd->hgqk", query_tile, key_block, preferred_element_type=jnp.float32
                    )
                    * score_scale
                )
                probs = jnp.exp(
                    jnp.where(allowed[None, None], raw_scores, MASKED_FILL) - tile_log[..., None]
                )
                grad_probs = jnp.einsum(
                    "qhgd,khd->hgqk", grad_tile, value_block, preferred_element_type=jnp.float32
                )
                grad_scores = (probs * (grad_probs - tile_delta[..., None])).astype(brain_float)
                grad_query = grad_query + jnp.einsum(
                    "hgqk,khd->qhgd", grad_scores, key_block, preferred_element_type=jnp.float32
                )
                grad_key_block = jnp.einsum(
                    "hgqk,qhgd->khd", grad_scores, query_tile, preferred_element_type=jnp.float32
                )
                grad_value_block = jnp.einsum(
                    "hgqk,qhgd->khd",
                    probs.astype(brain_float),
                    grad_tile,
                    preferred_element_type=jnp.float32,
                )
                return (grad_query, (grad_key_block, grad_value_block))

            def skipped(grad_query):
                empty_result = jnp.zeros((keys_per_block, KEY_VALUE_HEADS, HEAD_SIZE), jnp.float32)
                return (grad_query, (empty_result, empty_result))

            return lax.cond(jnp.any(allowed), back_active, skipped, carry)

        initial_gradient = jnp.zeros(
            (half_width, KEY_VALUE_HEADS, shared_heads, HEAD_SIZE), jnp.float32
        )
        return lax.scan(
            back_step,
            initial_gradient,
            (blocked_keys, blocked_values, segment_blocks, place_blocks),
        )

    heads_list = []
    extra_list = []
    log_list = []
    for tile in range(2):
        rows_tile = slice(tile * half_width, (tile + 1) * half_width)
        tile_query_tile = query_quad[rows_tile]
        tile_tile_segment = query_segment[rows_tile]
        tile_tile_place = query_place[rows_tile]

        def tile_allowed_of(segment_block, place_block):
            return (tile_tile_segment[:, None] == segment_block[None, :]) & (
                tile_tile_place[:, None] >= place_block[None, :]
            )

        def scores_of(key_block, allowed):
            raw_scores = (
                jnp.einsum(
                    "qhgd,khd->hgqk", tile_query_tile, key_block, preferred_element_type=jnp.float32
                )
                * score_scale
            )
            return jnp.where(allowed[None, None], raw_scores, MASKED_FILL)

        def stats_step(carry, block):
            key_block, segment_block, place_block = block
            allowed = tile_allowed_of(segment_block, place_block)

            def stats_active(state):
                peak, total = state
                scores = scores_of(key_block, allowed)
                newest = jnp.maximum(peak, jnp.max(scores, axis=-1))
                total = total * jnp.exp(peak - newest) + jnp.sum(
                    jnp.exp(scores - newest[..., None]), axis=-1
                )
                return (newest, total)

            return (lax.cond(jnp.any(allowed), stats_active, lambda state: state, carry), None)

        initial_peak = jnp.full(
            (KEY_VALUE_HEADS, shared_heads, half_width), MASKED_FILL, jnp.float32
        )
        initial_total = jnp.zeros((KEY_VALUE_HEADS, shared_heads, half_width), jnp.float32)
        (peak, total), unused = lax.scan(
            stats_step, (initial_peak, initial_total), (blocked_keys, segment_blocks, place_blocks)
        )
        tile_tile_log = peak + jnp.log(total)

        def output_step(carry, block):
            key_block, value_block, segment_block, place_block = block
            allowed = tile_allowed_of(segment_block, place_block)

            def output_active(state):
                upper, lower = state
                probs = jnp.exp(scores_of(key_block, allowed) - tile_tile_log[..., None])
                probs_high = probs.astype(brain_float)
                probs_low = (probs - probs_high.astype(jnp.float32)).astype(brain_float)
                upper = upper + jnp.einsum(
                    "hgqk,khd->qhgd", probs_high, value_block, preferred_element_type=jnp.float32
                )
                lower = lower + jnp.einsum(
                    "hgqk,khd->qhgd", probs_low, value_block, preferred_element_type=jnp.float32
                )
                return (upper, lower)

            return (lax.cond(jnp.any(allowed), output_active, lambda state: state, carry), None)

        initial_accumulator = jnp.zeros(
            (half_width, KEY_VALUE_HEADS, shared_heads, HEAD_SIZE), jnp.float32
        )
        (tile_heads, tile_extra), unused = lax.scan(
            output_step,
            (initial_accumulator, initial_accumulator),
            (blocked_keys, blocked_values, segment_blocks, place_blocks),
        )
        tile_heads, tile_extra, tile_log = (tile_heads, tile_extra, tile_tile_log)
        heads_list.append(tile_heads)
        extra_list.append(tile_extra)
        log_list.append(tile_log)
    heads_four = jnp.concatenate(heads_list, axis=0)
    heads_extra = jnp.concatenate(extra_list, axis=0)
    mixed = heads_four.reshape(row_count, QUERY_HEADS * HEAD_SIZE).astype(brain_float)
    middle = x_float + project_back(mixed, weight_out)
    normed_two_f, norm_two_back = jax.vjp(root_mean_norm, middle, gain_two)
    normed_two = normed_two_f.astype(brain_float)
    weight_gate, weight_up, weight_down = (
        lax.all_gather(w_gate.astype(brain_float), "fsdp", axis=1, tiled=True),
        lax.all_gather(w_up.astype(brain_float), "fsdp", axis=1, tiled=True),
        lax.all_gather(w_down.astype(brain_float), "fsdp", axis=1, tiled=True),
    )
    gate = matmul(normed_two, weight_gate)
    upward = matmul(normed_two, weight_up)
    hidden_f, swiglu_back = jax.vjp(swiglu, gate, upward)
    hidden = hidden_f.astype(brain_float)
    ffn_out = project_back(hidden, weight_down)
    grad_gate_f, grad_up_f = swiglu_back(matmul(dy_rows, weight_down))
    grad_gate = grad_gate_f.astype(brain_float)
    grad_up = grad_up_f.astype(brain_float)
    grad_normed_two = project_back(grad_gate, weight_gate) + project_back(grad_up, weight_up)
    grad_gate_weight = outer_sum(normed_two, grad_gate)
    grad_up_weight = outer_sum(normed_two, grad_up)
    grad_down_weight = outer_sum(dy_rows, hidden)
    grad_middle_norm, grad_gain_two = norm_two_back(grad_normed_two)
    grad_middle = dy_rows.astype(jnp.float32) + grad_middle_norm
    grad_branch = grad_middle.astype(brain_float)
    grad_out_weight = outer_sum(grad_branch, mixed)
    mixed_gradient = matmul(grad_branch, weight_out).astype(brain_float)
    mixed_gradient_quad = mixed_gradient.reshape(
        row_count, KEY_VALUE_HEADS, shared_heads, HEAD_SIZE
    )
    exact_heads = heads_four + heads_extra
    delta = jnp.sum(mixed_gradient_quad.astype(jnp.float32) * exact_heads, axis=-1).transpose(
        1, 2, 0
    )
    grad_query_list = []
    all_key_gradients = jnp.zeros((head_group, KEY_VALUE_HEADS * HEAD_SIZE), jnp.float32)
    all_value_gradients = jnp.zeros((head_group, KEY_VALUE_HEADS * HEAD_SIZE), jnp.float32)
    for tile in range(2):
        rows_tile = slice(tile * half_width, (tile + 1) * half_width)
        tile_grad_query, (key_block_gradients, value_block_gradients) = tile_backward(
            query_quad[rows_tile],
            query_segment[rows_tile],
            query_place[rows_tile],
            log_list[tile],
            mixed_gradient_quad[rows_tile],
            delta[:, :, rows_tile],
        )
        grad_query_list.append(tile_grad_query)
        all_key_gradients = all_key_gradients + key_block_gradients.reshape(
            head_group, KEY_VALUE_HEADS * HEAD_SIZE
        )
        all_value_gradients = all_value_gradients + value_block_gradients.reshape(
            head_group, KEY_VALUE_HEADS * HEAD_SIZE
        )
    grad_query_four = jnp.concatenate(grad_query_list, axis=0)
    all_key_gradients = all_key_gradients * score_scale
    all_key_gradients = halves_order(all_key_gradients, parts)
    all_value_gradients = halves_order(all_value_gradients, parts)
    own_key_gradient, grad_value_own = (
        lax.psum_scatter(
            all_key_gradients.astype(jnp.bfloat16), "ctx", scatter_dimension=0, tiled=True
        ).astype(jnp.float32),
        lax.psum_scatter(
            all_value_gradients.astype(jnp.bfloat16), "ctx", scatter_dimension=0, tiled=True
        ).astype(jnp.float32),
    )
    rotated_key_gradient = (
        own_key_gradient.astype(brain_float)
        .astype(jnp.float32)
        .reshape(row_count, KEY_VALUE_HEADS, HEAD_SIZE)
    )
    grad_value = grad_value_own.astype(brain_float)
    grad_query_rot = (
        (grad_query_four * score_scale)
        .astype(brain_float)
        .astype(jnp.float32)
        .reshape(row_count, QUERY_HEADS, HEAD_SIZE)
    )
    grad_query_raw_f, grad_key_raw_f, grad_query_gain, grad_key_gain = post_back(
        (grad_query_rot, rotated_key_gradient)
    )
    grad_query_raw = grad_query_raw_f.astype(brain_float)
    grad_key_raw = grad_key_raw_f.astype(brain_float)
    grad_normed = (
        project_back(grad_query_raw, weight_query)
        + project_back(grad_key_raw, weight_key)
        + project_back(grad_value, weight_value)
    )
    grad_query_weight = outer_sum(normed_input, grad_query_raw)
    grad_key_weight = outer_sum(normed_input, grad_key_raw)
    grad_value_weight = outer_sum(normed_input, grad_value)
    grad_x_norm, grad_gain_one = norm_one_back(grad_normed)
    out_rows = (middle + ffn_out).astype(brain_float)
    grad_rows = (grad_middle + grad_x_norm).astype(brain_float)
    returned = mirror_back(jnp.stack([out_rows[half_width:], grad_rows[half_width:]]), steps)
    out_rows = jnp.concatenate([out_rows[:half_width], returned[0]], axis=0)
    grad_rows = jnp.concatenate([grad_rows[:half_width], returned[1]], axis=0)
    summed = (
        lax.psum_scatter(
            grad_query_weight.astype(jnp.bfloat16), "fsdp", scatter_dimension=1, tiled=True
        ).astype(jnp.float32),
        lax.psum_scatter(
            grad_key_weight.astype(jnp.bfloat16), "fsdp", scatter_dimension=1, tiled=True
        ).astype(jnp.float32),
        lax.psum_scatter(
            grad_value_weight.astype(jnp.bfloat16), "fsdp", scatter_dimension=1, tiled=True
        ).astype(jnp.float32),
        lax.psum_scatter(
            grad_out_weight.astype(jnp.bfloat16), "fsdp", scatter_dimension=1, tiled=True
        ).astype(jnp.float32),
        lax.psum_scatter(
            grad_gate_weight.astype(jnp.bfloat16), "fsdp", scatter_dimension=1, tiled=True
        ).astype(jnp.float32),
        lax.psum_scatter(
            grad_up_weight.astype(jnp.bfloat16), "fsdp", scatter_dimension=1, tiled=True
        ).astype(jnp.float32),
        lax.psum_scatter(
            grad_down_weight.astype(jnp.bfloat16), "fsdp", scatter_dimension=1, tiled=True
        ).astype(jnp.float32),
    )
    final_grads = (
        lax.psum_scatter(
            summed[0].astype(jnp.bfloat16), "ctx", scatter_dimension=0, tiled=True
        ).astype(jnp.float32),
        lax.psum_scatter(
            summed[1].astype(jnp.bfloat16), "ctx", scatter_dimension=0, tiled=True
        ).astype(jnp.float32),
        lax.psum_scatter(
            summed[2].astype(jnp.bfloat16), "ctx", scatter_dimension=0, tiled=True
        ).astype(jnp.float32),
        lax.psum_scatter(
            summed[3].astype(jnp.bfloat16), "ctx", scatter_dimension=0, tiled=True
        ).astype(jnp.float32),
        lax.psum_scatter(
            summed[4].astype(jnp.bfloat16), "ctx", scatter_dimension=0, tiled=True
        ).astype(jnp.float32),
        lax.psum_scatter(
            summed[5].astype(jnp.bfloat16), "ctx", scatter_dimension=0, tiled=True
        ).astype(jnp.float32),
        lax.psum_scatter(
            summed[6].astype(jnp.bfloat16), "ctx", scatter_dimension=0, tiled=True
        ).astype(jnp.float32),
    )
    gains_total = lax.psum(
        (grad_gain_one, grad_gain_two, grad_query_gain, grad_key_gain), ("ctx", "fsdp")
    )
    return (
        out_rows[None],
        grad_rows[None],
        gains_total[0],
        gains_total[1],
        gains_total[2],
        gains_total[3],
        final_grads[0],
        final_grads[1],
        final_grads[2],
        final_grads[3],
        final_grads[4],
        final_grads[5],
        final_grads[6],
    )


def solution(mesh):
    row, whole, split = P("fsdp", "ctx", None), P(), P(None, "fsdp")
    out_split = P("ctx", "fsdp")

    def step(x, dy, lengths, *rest):
        p = Plan(mesh.shape["ctx"], mesh.shape["fsdp"], x.shape[1], x.shape[2], rest[5].shape[1] // HEAD, rest[8].shape[1])
        p.nseq = lengths.shape[1]
        if not p.fits():
            return general(x, dy, lengths, *rest)
        return tuple(local(p, x, dy, lengths, *rest))

    return jax.shard_map(
        step, mesh=mesh,
        in_specs=(row, row, P("fsdp", None), whole, whole, whole, whole) + (split,) * 7,
        out_specs=(row, row, whole, whole, whole, whole) + (out_split,) * 7,
        check_vma=False,
    )
```

```python
import functools
import math
import types

import jax
import jax.numpy as jnp
import numpy as np
from jax import lax
from jax.experimental import pallas as pl
from jax.experimental.pallas import tpu as pltpu
from jax.sharding import PartitionSpec as P

MESH = pl.DeviceIdType.MESH
BF16, F32 = jnp.bfloat16, jnp.float32
HEAD = 64
TILE = 256
EPS = 1e-05
THETA = 1000000.0
PLANES = 4
WINDOW = 3
SPLIT_STEPS = 2
OUT_SLOTS = 4
FF_SLOTS = 12
EXP2_SCALE = math.log2(math.e) / math.sqrt(HEAD)


def nt_dot(left, right):
    return lax.dot_general(left, right, (((1,), (1,)), ((), ())), preferred_element_type=F32)


def dot(left, right):
    return jnp.dot(left, right, preferred_element_type=F32)


(
    BZ,
    HID,
    DOWN,
    DW,
    BN,
    F,
    S1,
    S2,
    S3,
    S4,
    GM,
    BS,
    BP,
    GB,
    KA,
    KX,
    KZ,
    BF,
    DWO,
    DWQ,
    IG,
    GS,
    GF,
    BO,
    GX,
) = range(25)
PAIR_FIRST = (1, 3, 5, 6)
ORDER = (
    (DOWN, 0), (DW, 0), (HID, 1), (F, 0), (DOWN, 1), (DW, 1), (S1, 0), (HID, 2), (F, 1), (DOWN, 2), (DW, 2), (S1, 1),
    (BN, 0), (BN, 1), (BZ,), (F, 2), (DW, 3), (S1, 2), (DW, 4), (DW, 5), (F, 3), (DW, 6), (S1, 3), (F, 4), (F, 5),
    (S1, 4), (DW, 7), (S1, 5), (S2, 1), (DW, 8), (GM,), (F, 6), (BS, 0), (BP, 0, 0), (BP, 0, 2), (S2, 0), (S2, 3),
    (S1, 6), (KA, 0, 0), (KA, 0, 2), (GB, 1), (BS, 1), (S2, 4), (S2, 5), (F, 7), (BP, 1, 0), (S3, 1), (BP, 1, 2),
    (S1, 7), (S3, 3), (KA, 1, 0), (S3, 0), (S2, 2), (DWO,), (KX, 0, 2), (BP, 0, 1), (KA, 1, 2), (S3, 5), (BP, 1, 1),
    (KA, 0, 1), (KX, 0, 0), (KA, 1, 1), (F, 8), (KX, 1, 2), (KX, 0, 1), (BF, 1), (KZ, 0, 2), (F, 9), (S1, 8),
    (KX, 1, 1), (KZ, 1, 2), (S2, 8), (S2, 6), (S1, 9), (BF, 0), (S3, 2), (BO,), (KZ, 0, 1), (S4, 3), (IG, 0), (S3, 4),
    (KX, 1, 0), (S2, 7), (KZ, 1, 1), (IG, 1), (DWQ, 10), (F, 10), (GS, 0), (S1, 10), (S3, 6), (GF, 0), (DWQ, 11),
    (GS, 1), (F, 11), (S2, 9), (S3, 8), (S1, 11), (GF, 1), (S2, 10), (GX,), (GS, 2), (S3, 7), (S3, 9), (S4, 4),
    (S2, 11), (GF, 2), (S4, 1), (S4, 7), (GS, 3), (S4, 2), (S4, 5), (S3, 10), (S3, 11), (S4, 10), (S4, 6), (GF, 3),
    (S4, 9), (S4, 0), (S4, 8), (S4, 11),
)


class Plan:
    def __init__(self, ctx, groups, rows, width, kv_heads, ff):
        self.A, self.B, self.G = PLANES, ctx // (2 * PLANES), groups
        self.R, self.D, self.KV, self.FL = rows, width, kv_heads, ff
        self.S = width // ctx
        self.nt = ff // TILE
        self.HQ = 128 * kv_heads
        self.no = self.HQ // TILE
        self.tiles = 3 * self.nt + self.no + kv_heads
        self.down, self.gate, self.up, self.out = 0, self.nt, 2 * self.nt, 3 * self.nt
        self.qkv = self.out + self.no
        self.batches = []
        for first, count, step in ((0, 3 * self.nt, 3), (self.out, self.no, 2), (self.qkv, kv_heads, 2)):
            self.batches += [(t, min(step, first + count - t)) for t in range(first, first + count, step)]
        self.ff_batches = -(-3 * self.nt // 3)
        self.pair_first = PAIR_FIRST
        split = ORDER.index((GM,))
        self.order_forward, self.order_backward = ORDER[:split], ORDER[split:]

    def fits(self):
        rows = self.G * self.R
        weights = 2 * self.tiles * self.D * TILE
        keys = 2 * WINDOW * 2 * self.B * self.G * self.KV * self.R * 128
        activations = 2 * rows * (13 * self.D + 3 * self.FL)
        even = self.nt == 9 and self.G == 2 and self.B == 2 and self.no == 2 and self.FL % TILE == 0 and self.HQ % TILE == 0 and self.R % 128 == 0
        return even and weights + keys + activations < 45 << 20


def rotate(u, cos, sin):
    low, high = u[:, :32], u[:, 32:]
    return jnp.concatenate([low * cos - high * sin, high * cos + low * sin], axis=1)


def rotate_back(u, cos, sin):
    low, high = u[:, :32], u[:, 32:]
    return jnp.concatenate([low * cos + high * sin, high * cos - low * sin], axis=1)


AG_AUX, AG_DY, AG_GB, RS_FO, RS_GN2, RS_GN, HEADS, WO = range(8)


def kernel(p, names, *refs):
    r = types.SimpleNamespace(**dict(zip(names, refs)))
    A, B, G, R, D, KV, S = p.A, p.B, p.G, p.R, p.D, p.KV, p.S
    i, f = lax.axis_index("ctx"), lax.axis_index("fsdp")
    c = lax.rem(i, 2)
    b = lax.rem(i // 2, B)
    a = i // (2 * B)
    place = 2 * b + c
    others = range(1, G)

    def at(aa, bb, cc):
        return ((aa * B + bb) * 2 + cc, f)

    def group_device(k):
        return (i, lax.rem(f + k, G))

    def remote(src, dst, send, recv, device):
        return pltpu.make_async_remote_copy(
            src_ref=src, dst_ref=dst, send_sem=send, recv_sem=recv, device_id=device, device_id_type=MESH
        )

    sibling = at(a, b, 1 - c)

    peers = [sibling]
    peers += [at(a, lax.rem(b + k, B), c) for k in range(1, B)]
    peers += [at(lax.rem(a + k, A), b, c) for k in range(1, A)]
    peers += [group_device(k) for k in others]
    barrier = pltpu.get_barrier_semaphore()
    for peer in peers:
        pl.semaphore_signal(barrier, inc=1, device_id=peer, device_id_type=MESH)

    y_sems = r.y_sems

    def gather(kind, buffer, k):
        return remote(buffer.at[0], buffer.at[G - k], y_sems.at[kind, 0, k], y_sems.at[kind, 1, G - k], group_device(k))

    def gathered(kind, buffer, k):
        return remote(buffer.at[k], buffer.at[k], y_sems.at[kind, 0, k], y_sems.at[kind, 1, k], group_device(k))

    def scatter(kind, send, recv, k):
        return remote(send.at[k - 1], recv.at[G - k - 1], y_sems.at[kind, 0, k], y_sems.at[kind, 1, G - k], group_device(k))

    def scattered(kind, send, recv, k):
        return remote(send.at[k - 1], recv.at[k - 1], y_sems.at[kind, 0, k], y_sems.at[kind, 1, k], group_device(k))

    x_all, aux, dy_all = r.x_all, r.aux, r.dy_all
    x_sems_y = r.x_sems_y

    def gather_x(k, q):
        rows = pl.ds(q * (R // 2), R // 2)
        return remote(x_all.at[0, rows], x_all.at[G - k, rows], x_sems_y.at[0, k, q], x_sems_y.at[1, G - k, q], group_device(k))

    def gathered_x(k, q):
        rows = pl.ds(q * (R // 2), R // 2)
        return remote(x_all.at[k, rows], x_all.at[k, rows], x_sems_y.at[0, k, q], x_sems_y.at[1, k, q], group_device(k))

    local_sems = r.local_sems

    def tables():
        where = i * R + lax.broadcasted_iota(jnp.int32, (8, R), 1)
        start = jnp.zeros((8, R), jnp.int32)
        end = jnp.int32(0)
        for j in range(p.nseq):
            end = end + r.lengths[0, j]
            start = jnp.where(where >= end, end, start)
        offset = (where - start).astype(F32)
        steps = lax.broadcasted_iota(jnp.int32, (32, R), 0).astype(F32)
        angle = offset[0:1] * jnp.exp(steps * (-2.0 * math.log(THETA) / HEAD))
        aux[0, 0:32] = jnp.cos(angle)
        aux[0, 32:64] = jnp.sin(angle)
        aux[0, 64:72] = start.astype(F32)
        for j, gain in enumerate((r.query_gain, r.key_gain)):
            wide = jnp.concatenate([jnp.broadcast_to(gain[...], (128, HEAD))] * 2, axis=1)
            r.gain_columns[j * HEAD:(j + 1) * HEAD] = jnp.transpose(wide)[0:HEAD]

    kvw = r.kvw
    z_sems, x_sems, c_sems = r.z_sems, r.x_sems, r.c_sems
    wall = r.wall

    def weight(t):
        return wall[t].reshape(D, TILE)

    def weight_rows(t, aa):
        return wall[t, aa // 2, aa % 2].reshape(D // A, TILE)

    n_t = r.n_t
    raws, q_t, o_acc = r.raws, r.q_t, r.o_acc

    half = R // 2

    def block_half(d, slot, k, q):
        return kvw.at[d, slot, k, :, pl.ds(q * half, half)]

    def z_copy(d, k, q):
        source, target = block_half(d - 1, place, k, q), block_half(d, place, k, q)
        return remote(source, target, z_sems.at[0, d - 1, k, q], z_sems.at[1, d - 1, k, q], at(lax.rem(a + 1, A), b, c))

    def z_arrival(d, k, q):
        slot = block_half(d, place, k, q)
        return remote(slot, slot, z_sems.at[0, d - 1, k, q], z_sems.at[1, d - 1, k, q], at(lax.rem(a + A - 1, A), b, c))

    def x_copy(d, shift, k, q):
        slot = block_half(d, place, k, q)
        return remote(slot, slot, x_sems.at[0, d, shift, k, q], x_sems.at[1, d, shift, k, q], at(a, lax.rem(b + shift, B), c))

    def x_arrival(d, shift, k, q):
        other = lax.rem(b + B - shift, B)
        slot = block_half(d, 2 * other + c, k, q)
        return remote(slot, slot, x_sems.at[0, d, shift, k, q], x_sems.at[1, d, shift, k, q], at(a, other, c))

    def c_copy(d, column, k, q):
        slot = block_half(d, 2 * column + c, k, q)
        return remote(slot, slot, c_sems.at[0, d, column, k, q], c_sems.at[1, d, column, k, q], sibling)

    def c_arrival(d, column, k, q):
        slot = block_half(d, 2 * column + 1 - c, k, q)
        return remote(slot, slot, c_sems.at[0, d, column, k, q], c_sems.at[1, d, column, k, q], sibling)

    def x_needed(d, source, target):
        if d == 0:
            return target > source
        if d == 1:
            return target >= 0
        return target < source

    def c_needed(d, column, core):
        if d == 0:
            return jnp.logical_or(column < b, jnp.logical_and(column == b, core == 0))
        if d == 1:
            return column >= 0
        return jnp.logical_or(column > b, jnp.logical_and(column == b, core == 1))

    def when_all(*conditions):
        whole = conditions[0]
        for condition in conditions[1:]:
            whole = jnp.logical_and(whole, condition)
        return pl.when(whole)

    def onward(d, k, q):
        @when_all(a + 1 < A, a >= d)
        def _():
            z_copy(d + 1, k, q).start()

    def spread(d, k, q):
        for shift in range(1, B):
            @when_all(a >= d, x_needed(d, b, lax.rem(b + shift, B)))
            def _():
                x_copy(d, shift, k, q).start()
        @when_all(a >= d, c_needed(d, b, c))
        def _():
            c_copy(d, b, k, q).start()

    def from_plane(d, k, q):
        @pl.when(a >= d)
        def _():
            z_arrival(d, k, q).wait_recv()

    def from_columns(d, k, q):
        for shift in range(1, B):
            other = lax.rem(b + B - shift, B)
            @when_all(a >= d, x_needed(d, other, b))
            def _():
                x_arrival(d, shift, k, q).wait_recv()
                c_copy(d, other, k, q).start()

    def from_sibling(d, k):
        def step(column, _):
            @when_all(a >= d, c_needed(d, column, 1 - c))
            def _():
                for q in range(2):
                    c_arrival(d, column, k, q).wait_recv()
            return 0
        lax.fori_loop(0, B, step, 0)

    def all_sent(k):
        for q in range(2):
            for d in range(WINDOW):
                if d + 1 < WINDOW:
                    @when_all(a + 1 < A, a >= d)
                    def _():
                        z_copy(d + 1, k, q).wait_send()
                for shift in range(1, B):
                    @when_all(a >= d, x_needed(d, b, lax.rem(b + shift, B)))
                    def _():
                        x_copy(d, shift, k, q).wait_send()
                def step(column, _):
                    @when_all(a >= d, c_needed(d, column, c))
                    def _():
                        c_copy(d, column, k, q).wait_send()
                    return 0
                lax.fori_loop(0, B, step, 0)

    def project(k, first, count):
        rows, lanes = pl.ds(first, count), slice(first, first + count)
        x = x_all[k, rows].astype(F32)
        n = x * lax.rsqrt(jnp.mean(x * x, axis=1, keepdims=True) + EPS) * r.gain_one[...]
        n_rows = n.astype(BF16)
        n_t[:, k * R + first:k * R + first + count] = jnp.transpose(n).astype(BF16)
        cos, sin = aux[k, 0:32, lanes], aux[k, 32:64, lanes]
        q_gain, k_gain = r.gain_columns[0:64, 0:1], r.gain_columns[64:128, 0:1]
        for h in range(KV):
            raw = jnp.transpose(dot(n_rows, weight(p.qkv + h)))
            raws[k, h, :, lanes] = raw[0:192]
            query = raw[0:128].reshape(2, HEAD, count)
            query = query * lax.rsqrt(jnp.mean(query * query, axis=1, keepdims=True) + EPS) * q_gain
            query = rotate(query, cos, sin).astype(BF16)
            for j in range(2):
                q_t[k, h, 0:64, j * R + first:j * R + first + count] = query[j]
                q_t[k, h, 64:128, j * R + first:j * R + first + count] = jnp.zeros((64, count), BF16)
            key = raw[128:192].reshape(1, HEAD, count)
            key = key * lax.rsqrt(jnp.mean(key * key, axis=1, keepdims=True) + EPS) * k_gain
            key = rotate(key, cos, sin).reshape(HEAD, count)
            kv = jnp.concatenate([key, raw[192:256]], axis=0)
            kvw[0, place, k, h, rows] = jnp.transpose(kv).astype(BF16)

    def mask_of(k, key_start, diagonal):
        keys = lax.broadcasted_iota(jnp.int32, (R, 2 * R), 0)
        start = jnp.concatenate([aux[k, 64:65], aux[k, 64:65]], axis=1)
        allowed = (keys + key_start).astype(F32) >= start
        if diagonal:
            query = lax.broadcasted_iota(jnp.int32, (R, 2 * R), 1)
            query = jnp.where(query >= R, query - R, query)
            allowed = jnp.logical_and(allowed, keys <= query)
        return allowed

    def attend(d, other, k, diagonal=False):
        key_start = ((a - d) * 2 * B + other) * R
        allowed = mask_of(k, key_start, diagonal)
        for h in range(KV):
            kv = kvw[d, other, k, h]
            scores = dot(kv, q_t[k, h])
            weights = jnp.where(allowed, jnp.exp2(scores * EXP2_SCALE), 0.0).astype(BF16)
            values = jnp.concatenate([jnp.transpose(kv)[64:128], jnp.ones((16, R), BF16)], axis=0)
            added = dot(values, weights)
            if diagonal:
                o_acc[k, h] = added
            else:
                o_acc[k, h] += added

    def attended(d):
        if d == 0:
            return 0, place
        if d == 1:
            return 0, jnp.where(a >= 1, 2 * B, 0)
        return place, jnp.where(a >= 2, 2 * B, 0)

    def attend_plane(d, k):
        low, high = attended(d)
        def step(other, _):
            attend(d, other, k)
            return 0
        lax.fori_loop(low, high, step, 0)

    mixed = r.mixed
    n2_all = gb_all = r.n2_all
    y_send, y_recv, fo_send, fo_recv = r.y_send, r.y_recv, r.fo_send, r.fo_recv
    part, out_acc, middle = r.part, r.out_acc, r.middle
    gains = r.gains

    def store_part(k, send, own, aa, value):
        columns = slice(aa * (D // A), (aa + 1) * (D // A))
        if k == 0:
            own[:, columns] = value
        else:
            send[k - 1, :, columns] = value.astype(BF16)

    def finish_heads(k):
        for h in range(KV):
            o = o_acc[k, h]
            o_n = o[0:64] / o[64:65]
            o_acc[k, h, 0:64] = o_n
            both = jnp.concatenate([o_n[:, 0:R], o_n[:, R:2 * R]], axis=0)
            mixed[k, :, 128 * h:128 * h + 128] = jnp.transpose(both).astype(BF16)

    mixed_in, wo_other = r.mixed_in, r.wo_other

    def heads_out(k):
        return remote(mixed.at[k], mixed_in.at[1 - k], y_sems.at[HEADS, 0, k], y_sems.at[HEADS, 1, 1 - k], group_device(1))

    def heads_in(k):
        return remote(mixed.at[k], mixed_in.at[k], y_sems.at[HEADS, 0, k], y_sems.at[HEADS, 1, k], group_device(1))

    def out_tile():
        return remote(wall.at[p.out + c], wo_other.at[c], y_sems.at[WO, 0, 0], y_sems.at[WO, 1, 0], group_device(1))

    def out_tile_on():
        return remote(wo_other.at[c], wo_other.at[c], y_sems.at[WO, 0, 1], y_sems.at[WO, 1, 1], sibling)

    def out_tile_in():
        return remote(wo_other.at[1 - c], wo_other.at[1 - c], y_sems.at[WO, 0, 1], y_sems.at[WO, 1, 1], sibling)

    def project_out(k, target):
        for aa in range(A):
            total = jnp.zeros((R, D // A), F32)
            for t in range(p.no):
                lanes = slice(t * TILE, (t + 1) * TILE)
                total += nt_dot(mixed[k, :, lanes], weight_rows(p.out + t, aa))
                other = wo_other[t, aa // 2, aa % 2].reshape(D // A, TILE)
                total += nt_dot(mixed_in[k, :, lanes], other)
            target[:, aa * (D // A):(aa + 1) * (D // A)] = total

    def normed_middle(k, branch, keep):
        for piece in range(R // 128):
            rows = pl.ds(piece * 128, 128)
            v = x_all[k, rows].astype(F32) + branch[rows]
            if keep:
                middle[rows] = v
            n2_all[k, rows] = (v * lax.rsqrt(jnp.mean(v * v, axis=1, keepdims=True) + EPS) * r.gain_two[...]).astype(BF16)

    def load_scope(s_q, s_k, s_v, s_o):
        own_x = pltpu.make_async_copy(r.x.at[0], x_all.at[0], local_sems.at[0])
        loads = [
            pltpu.make_async_copy(source, s, local_sems.at[2 + j])
            for j, (source, s) in enumerate(((r.w_query, s_q), (r.w_key, s_k), (r.w_value, s_v), (r.w_out, s_o)))
        ]
        own_x.start()
        for load in loads:
            load.start()

        def cast_qkv(aa, _):
            rows = pl.ds(aa * (D // A), D // A)
            for h in range(KV):
                whole = jnp.concatenate(
                    [s_q[rows, 128 * h:128 * h + 128], s_k[rows, 64 * h:64 * h + 64], s_v[rows, 64 * h:64 * h + 64]], axis=1
                ).astype(BF16)
                wall[p.qkv + h, aa // 2, lax.rem(aa, 2)] = whole.reshape(B, 2, S, TILE)
            return 0

        def cast_out(aa, _):
            rows = pl.ds(aa * (D // A), D // A)
            for t in range(p.no):
                wall[p.out + t, aa // 2, lax.rem(aa, 2)] = s_o[rows, TILE * t:TILE * (t + 1)].astype(BF16).reshape(B, 2, S, TILE)
            return 0

        tables()
        own_x.wait()
        pl.semaphore_wait(barrier, len(peers))
        for k in others:
            gather(AG_AUX, aux, k).start()
            for q in range(2):
                gather_x(k, q).start()
        for load in loads[:3]:
            load.wait()
        lax.fori_loop(0, A, cast_qkv, 0)
        loads[3].wait()
        lax.fori_loop(0, A, cast_out, 0)

    def forward_scope(stage, stage_sems):
        own_dy = pltpu.make_async_copy(r.dy.at[0], dy_all.at[0], local_sems.at[1])
        ff = ((r.w_gate, p.gate), (r.w_up, p.up), (r.w_down, p.down))
        slots = FF_SLOTS
        chunks = A * B * 2

        def ff_load(source, n):
            rows = pl.ds(n * S, S)
            return pltpu.make_async_copy(source.at[rows], stage.at[lax.rem(n, slots)], stage_sems.at[lax.rem(n, slots)])

        def prime(which):
            for n in range(slots - 1):
                ff_load(ff[which][0], n).start()

        def cast_ff(which):
            source, first = ff[which]
            def step(n, _):
                @pl.when(n + slots - 1 < chunks)
                def _():
                    ff_load(source, n + slots - 1).start()
                ff_load(source, n).wait()
                aa, bb, cc = n // (2 * B), lax.rem(n // 2, B), lax.rem(n, 2)
                for t in range(p.nt):
                    part_of = stage[lax.rem(n, slots), :, t * TILE:(t + 1) * TILE]
                    wall[first + t, aa // 2, lax.rem(aa, 2), bb, cc] = part_of.astype(BF16)
                return 0
            lax.fori_loop(0, chunks, step, 0)
            if which + 1 < len(ff):
                prime(which + 1)

        prime(0)
        own_dy.start()
        halves = range(2)
        project(0, 0, R)
        for q in halves:
            onward(0, 0, q)
            spread(0, 0, q)
        attend(0, place, 0, True)
        own_dy.wait()
        cast_ff(0)
        from_plane(1, 0, 0)
        onward(1, 0, 0)
        spread(1, 0, 0)
        from_columns(0, 0, 0)
        for k in others:
            gathered(AG_AUX, aux, k).wait_recv()
            gathered_x(k, 0).wait_recv()
            project(k, 0, half)
            onward(0, k, 0)
            spread(0, k, 0)
        from_plane(1, 0, 1)
        onward(1, 0, 1)
        spread(1, 0, 1)
        from_columns(0, 0, 1)
        cast_ff(1)
        for k in others:
            gathered_x(k, 1).wait_recv()
            project(k, half, half)
            onward(0, k, 1)
            spread(0, k, 1)
        for k in others:
            gather(AG_DY, dy_all, k).start()
        out_tile().start()
        from_columns(1, 0, 0)
        from_plane(2, 0, 0)
        spread(2, 0, 0)
        for k in others:
            from_plane(1, k, 0)
            onward(1, k, 0)
            spread(1, k, 0)
        cast_ff(2)
        from_columns(1, 0, 1)
        from_sibling(0, 0)
        attend_plane(0, 0)
        for k in others:
            attend(0, place, k, True)
        from_plane(2, 0, 1)
        spread(2, 0, 1)
        for k in others:
            from_plane(1, k, 1)
            onward(1, k, 1)
            spread(1, k, 1)
            for q in halves:
                from_columns(0, k, q)
        from_sibling(1, 0)
        attend_plane(1, 0)
        for k in others:
            @pl.when(b > 0)
            def _():
                for q in halves:
                    from_plane(2, k, q)
                    spread(2, k, q)
        for q in halves:
            from_columns(2, 0, q)
        from_sibling(2, 0)
        attend_plane(2, 0)
        finish_heads(0)
        heads_out(0).start()
        for k in others:
            for q in halves:
                from_columns(1, k, q)
            from_sibling(0, k)
            attend_plane(0, k)
        for k in others:
            from_sibling(1, k)
            attend_plane(1, k)

            @pl.when(b == 0)
            def _():
                for q in halves:
                    from_plane(2, k, q)
                    spread(2, k, q)
            for q in halves:
                from_columns(2, k, q)
            from_sibling(2, k)
            attend_plane(2, k)
            finish_heads(k)
            heads_out(k).start()
        out_tile().wait_recv()
        out_tile_on().start()
        out_tile_in().wait_recv()
        for k in others:
            heads_in(k).wait_recv()
            project_out(k, out_acc)
            normed_middle(k, out_acc, False)
        for k in range(G):
            all_sent(k)
        out_tile().wait_send()
        out_tile_on().wait_send()

    pl.run_scoped(
        load_scope,
        pltpu.VMEM((D, 128 * KV), F32),
        pltpu.VMEM((D, 64 * KV), F32),
        pltpu.VMEM((D, 64 * KV), F32),
        pltpu.VMEM((D, 128 * KV), F32),
    )
    pl.run_scoped(
        forward_scope,
        pltpu.VMEM((FF_SLOTS, S, p.FL), F32),
        pltpu.SemaphoreType.DMA((FF_SLOTS,)),
    )
    for k in others:
        for q in range(2):
            gather_x(k, q).wait_send()
        gather(AG_AUX, aux, k).wait_send()

    rc, r1, r2, r3 = r.rc, r.r1, r.r2, r.r3
    w_sems = r.w_sems
    stage_c, fetch_sems = r.stage_c, r.fetch_sems
    high, low = a // 2, lax.rem(a, 2)
    column_device = at(a, 1 - b, c)
    pair_device = at(2 * high + 1 - low, b, c)

    def sum_core(n):
        t, m = p.batches[n]
        source = wall.at[pl.ds(t, m), :, :, :, 1 - c]
        return remote(source, rc.at[pl.ds(t, m)], w_sems.at[0, 0, n], w_sems.at[1, 0, n], sibling)

    def sum_first(n):
        t, m = p.batches[n]
        if n in p.pair_first:
            source, device = wall.at[pl.ds(t, m), :, 1 - low, :, c], pair_device
        else:
            source, device = wall.at[pl.ds(t, m), :, :, 1 - b, c], column_device
        return remote(source, r1.at[pl.ds(t, m)], w_sems.at[0, 1, n], w_sems.at[1, 1, n], device)

    def sum_second(n):
        t, m = p.batches[n]
        if n in p.pair_first:
            source, device = wall.at[pl.ds(t, m), :, low, 1 - b, c], column_device
        else:
            source, device = wall.at[pl.ds(t, m), :, 1 - low, b, c], pair_device
        return remote(source, r2.at[pl.ds(t, m)], w_sems.at[0, 2, n], w_sems.at[1, 2, n], device)

    def sum_third(n):
        t, m = p.batches[n]
        source = wall.at[pl.ds(t, m), 1 - high, low, b, c]
        return remote(source, r3.at[pl.ds(t, m)], w_sems.at[0, 3, n], w_sems.at[1, 3, n], at(2 * (1 - high) + low, b, c))

    def fetch_core(n):
        t, m = p.batches[n]
        return pltpu.make_async_copy(rc.at[pl.ds(t, m)], stage_c.at[n % 2, pl.ds(0, m)], fetch_sems.at[n % 2])

    def step_core(n):
        sum_core(n).start()

    def step_fetch(n):
        sum_core(n).wait_recv()
        fetch_core(n).start()

    def step_first(n):
        t, m = p.batches[n]
        fetch_core(n).wait()
        def add(j, _):
            tile, hi, lo = j // A, lax.rem(j // 2, 2), lax.rem(j, 2)
            mine = wall[t + tile, hi, lo, :, c].astype(F32) + stage_c[n % 2, tile, hi, lo].astype(F32)
            wall[t + tile, hi, lo, :, c] = mine.astype(BF16)
            return 0
        lax.fori_loop(0, m * A, add, 0)
        sum_first(n).start()

    def step_second(n):
        t, m = p.batches[n]
        sum_first(n).wait_recv()
        def add(tile, _):
            if n in p.pair_first:
                mine = wall[t + tile, :, low, :, c].astype(F32) + r1[t + tile].astype(F32)
                wall[t + tile, :, low, :, c] = mine.astype(BF16)
            else:
                mine = wall[t + tile, :, :, b, c].astype(F32) + r1[t + tile].astype(F32)
                wall[t + tile, :, :, b, c] = mine.astype(BF16)
            return 0
        lax.fori_loop(0, m, add, 0)
        sum_second(n).start()

    def step_third(n):
        t, m = p.batches[n]
        sum_second(n).wait_recv()
        def add(tile, _):
            mine = wall[t + tile, :, low, b, c].astype(F32) + r2[t + tile].astype(F32)
            wall[t + tile, :, low, b, c] = mine.astype(BF16)
            return 0
        lax.fori_loop(0, m, add, 0)
        sum_third(n).start()

    out_stage, out_sems = r.out_stage, r.out_sems

    def out_copy(n):
        t, m = p.batches[n]
        return pltpu.make_async_copy(out_stage.at[n % OUT_SLOTS, pl.ds(0, m)], r.d_weights.at[pl.ds(t, m)], out_sems.at[n % OUT_SLOTS])

    out_order = []

    def step_out(n):
        t, m = p.batches[n]
        for earlier in (sum_core, sum_first, sum_second):
            earlier(n).wait_send()
        sum_third(n).wait_recv()
        for earlier in out_order:
            if earlier % OUT_SLOTS == n % OUT_SLOTS:
                out_copy(earlier).wait()
        out_order[:] = [e for e in out_order if e % OUT_SLOTS != n % OUT_SLOTS] + [n]
        def add(tile, _):
            out_stage[n % OUT_SLOTS, tile] = wall[t + tile, high, low, b, c].astype(F32) + r3[t + tile].astype(F32)
            return 0
        lax.fori_loop(0, m, add, 0)
        out_copy(n).start()

    def run(order, steps):
        steps = {**steps, F: step_fetch, S1: step_first, S2: step_second, S3: step_third, S4: step_out}
        for step, *numbers in order:
            steps[step](*numbers)

    def feed_forward(hs, n2_t, dy_t):
        def turned(source, k, target):
            for piece in range(R // 128):
                rows = pl.ds(piece * 128, 128)
                target[:, k * R + piece * 128:k * R + (piece + 1) * 128] = jnp.transpose(source[k, rows].astype(F32)).astype(BF16)

        def hidden(k, first, count):
            rows = slice(k * R, (k + 1) * R)
            def step(t, _):
                gate = dot(n2_all[k], weight(p.gate + t))
                up = dot(n2_all[k], weight(p.up + t))
                grad = dot(dy_all[k], weight(p.down + t))
                sig = 1.0 / (1.0 + jnp.exp(-gate))
                silu = gate * sig
                hs[2, t, rows] = (silu * up).astype(BF16)
                hs[0, t, rows] = (grad * up * (sig * (1.0 + gate * (1.0 - sig)))).astype(BF16)
                hs[1, t, rows] = (grad * silu).astype(BF16)
                return 0
            lax.fori_loop(first, first + count, step, 0)

        def back_normed(k, parts):
            rows = slice(k * R, (k + 1) * R)
            for aa in parts:
                total = jnp.zeros((R, D // A), F32)
                for t in range(p.nt):
                    total += nt_dot(hs[0, t, rows], weight_rows(p.gate + t, aa))
                    total += nt_dot(hs[1, t, rows], weight_rows(p.up + t, aa))
                store_part(k, y_send, part, aa, total)

        def down(k, first, count):
            rows = slice(k * R, (k + 1) * R)
            for aa in range(A):
                columns = slice(aa * (D // A), (aa + 1) * (D // A))
                total = jnp.zeros((R, D // A), F32)
                for t in range(first, first + count):
                    total += nt_dot(hs[2, t, rows], weight_rows(p.down + t, aa))
                if k:
                    store_part(k, fo_send, None, aa, total)
                else:
                    out_acc[:, columns] = (out_acc if first else middle)[:, columns] + total

        def weight_gradients(n):
            t, m = p.batches[n]
            for tile in range(t, t + m):
                kind, u = (2, 0, 1)[tile // p.nt], tile % p.nt
                left = dy_t if kind == 2 else n2_t
                for aa in range(A):
                    rows = slice(aa * (D // A), (aa + 1) * (D // A))
                    wall[tile, aa // 2, aa % 2] = dot(left[rows], hs[kind, u]).astype(BF16).reshape(B, 2, S, TILE)

        third = p.batches[0][1]
        for k in others:
            gathered(AG_DY, dy_all, k).wait_recv()
            hidden(k, 0, p.nt)
            turned(dy_all, k, dy_t)
            turned(n2_all, k, n2_t)
            down(k, 0, p.nt)
        turned(dy_all, 0, dy_t)
        heads_in(0).wait_recv()
        project_out(0, part)
        normed_middle(0, part, True)
        turned(n2_all, 0, n2_t)
        hidden(0, 0, third)

        def hidden_part(j):
            hidden(0, j * third, third)

        def down_part(j):
            down(0, j * third, third)

        def gradients_and_core(n):
            weight_gradients(n)
            step_core(n)

        def back_normed_half(half):
            for k in others:
                back_normed(k, range(half * A // 2, (half + 1) * A // 2))
                if half:
                    scatter(RS_GN2, y_send, y_recv, k).start()

        run(p.order_forward, {
            HID: hidden_part, DOWN: down_part, DW: gradients_and_core, BN: back_normed_half,
            BZ: lambda: back_normed(0, range(A)),
        })

    pl.run_scoped(
        feed_forward,
        pltpu.VMEM((3, p.nt, G * R, TILE), BF16),
        pltpu.VMEM((D, G * R), BF16),
        pltpu.VMEM((D, G * R), BF16),
    )
    last = p.ff_batches


    def middle_gradient():
        for k in others:
            scattered(RS_GN2, y_send, y_recv, k).wait_recv()
        gain_grad = jnp.zeros((1, D), F32)
        for piece in range(R // 128):
            rows = pl.ds(piece * 128, 128)
            e = part[rows]
            for k in others:
                e += y_recv[k - 1, rows].astype(F32)
            v = middle[rows]
            rr = lax.rsqrt(jnp.mean(v * v, axis=1, keepdims=True) + EPS)
            vh = v * rr
            gain_grad += jnp.sum(e * vh, axis=0, keepdims=True)
            ge = e * r.gain_two[...]
            gm = dy_all[0, rows].astype(F32) + rr * (ge - vh * jnp.mean(vh * ge, axis=1, keepdims=True))
            middle[rows] = gm
            r.gb_t[:, piece * 128:(piece + 1) * 128] = jnp.transpose(gm).astype(BF16)
        gains[...] = jnp.zeros((8, D), F32)
        gains[0:1] = gain_grad
        gb_all[0] = middle[...].astype(BF16)
        for k in others:
            gather(AG_GB, gb_all, k).start()

    dm = r.dm
    graw = r.graw
    kvr, xr, zr = r.kvr, r.xr, r.zr
    kc_sems, kx_sems, kz_sems = r.kc_sems, r.kx_sems, r.kz_sems
    head_sums = r.head_sums
    head_sums[...] = jnp.zeros((128, R), F32)

    def k_core(d, column, k):
        return remote(kvw.at[d, 2 * column + 1 - c, k], kvr.at[d, column, k], kc_sems.at[0, d, column, k], kc_sems.at[1, d, column, k], sibling)

    def k_column(d, shift, k):
        target = lax.rem(b + shift, B)
        return remote(kvw.at[d, 2 * target + c, k], xr.at[d, shift - 1, k], kx_sems.at[0, d, shift, k], kx_sems.at[1, d, shift, k], at(a, target, c))

    def k_plane(d, k):
        return remote(kvw.at[d, place, k], zr.at[d - 1, k], kz_sems.at[0, d - 1, k], kz_sems.at[1, d - 1, k], at(lax.rem(a + A - 1, A), b, c))

    def in_window(d, column, core, from_core):
        if d == 0:
            return jnp.logical_or(column < b, jnp.logical_and(column == b, core <= from_core))
        if d == 1:
            return column >= 0
        return jnp.logical_or(column > b, jnp.logical_and(column == b, core >= from_core))

    def column_reached(d, target, source):
        if d == 0:
            return target < source
        if d == 1:
            return target >= 0
        return target > source

    def keys_core(d, k):
        for column in range(B):
            @when_all(a >= d, in_window(d, column, 1 - c, c))
            def _():
                k_core(d, column, k).start()

    def keys_add(d, k, kv_stage, kv_sems):
        def fetch(column):
            return pltpu.make_async_copy(kvr.at[d, column, k], kv_stage.at[column], kv_sems.at[column])

        for column in range(B):
            @when_all(a >= d, in_window(d, column, c, 1 - c))
            def _():
                k_core(d, column, k).wait_recv()
                fetch(column).start()
        for column in range(B):
            @when_all(a >= d, in_window(d, column, c, 1 - c))
            def _():
                fetch(column).wait()
                for h in range(KV):
                    slot = 2 * column + c
                    kvw[d, slot, k, h] = (kvw[d, slot, k, h].astype(F32) + kv_stage[column, h].astype(F32)).astype(BF16)
        for shift in range(1, B):
            @when_all(a >= d, column_reached(d, lax.rem(b + shift, B), b))
            def _():
                k_column(d, shift, k).start()

    def keys_columns(d, k):
        for shift in range(1, B):
            @when_all(a >= d, column_reached(d, b, lax.rem(b + B - shift, B)))
            def _():
                k_column(d, shift, k).wait_recv()
                for h in range(KV):
                    kvw[d, place, k, h] = (kvw[d, place, k, h].astype(F32) + xr[d, shift - 1, k, h].astype(F32)).astype(BF16)

    def keys_plane(d, k):
        @pl.when(a >= d)
        def _():
            k_plane(d, k).start()

    def keys_from_plane(d, k):
        @when_all(a + 1 < A, a + 1 >= d)
        def _():
            k_plane(d, k).wait_recv()
            for h in range(KV):
                kvw[d - 1, place, k, h] = (kvw[d - 1, place, k, h].astype(F32) + zr[d - 1, k, h].astype(F32)).astype(BF16)

    def keys_sent(k):
        for d in range(WINDOW):
            for column in range(B):
                @when_all(a >= d, in_window(d, column, 1 - c, c))
                def _():
                    k_core(d, column, k).wait_send()
            for shift in range(1, B):
                @when_all(a >= d, column_reached(d, lax.rem(b + shift, B), b))
                def _():
                    k_column(d, shift, k).wait_send()
            if d:
                @pl.when(a >= d)
                def _():
                    k_plane(d, k).wait_send()

    def rms_back(raw, e, gain):
        rr = lax.rsqrt(jnp.mean(raw * raw, axis=1, keepdims=True) + EPS)
        vh = raw * rr
        ge = e * gain
        return jnp.sum(e * vh, axis=0), rr * (ge - vh * jnp.mean(vh * ge, axis=1, keepdims=True))

    def back_start(k, do_t, do_rows, q_rows, dq, rows_of):
        for t in range(p.no):
            dm[:, t * TILE:(t + 1) * TILE] = dot(gb_all[k], weight(p.out + t)).astype(BF16)
        for h in range(KV):
            turned = jnp.transpose(dm[:, 128 * h:128 * h + 128].astype(F32))
            grad = jnp.concatenate([turned[0:64], turned[64:128]], axis=1)
            rows_of[k, h, 0:1] = jnp.log2(o_acc[k, h, 64:65])
            rows_of[k, h, 1:2] = jnp.sum(grad * o_acc[k, h, 0:64], axis=0, keepdims=True)
            padded = jnp.concatenate([jnp.zeros((64, 2 * R), F32), grad], axis=0)
            do_t[k, h] = padded.astype(BF16)
            do_rows[k, h] = jnp.transpose(padded).astype(BF16)
            q_rows[k, h] = (jnp.transpose(q_t[k, h].astype(F32)) * (1.0 / math.sqrt(HEAD))).astype(BF16)
            dq[k, h] = jnp.zeros((64, 2 * R), F32)

    def back_block(k, d, other, do_t, do_rows, q_rows, dq, rows_of, diagonal=False):
        key_start = ((a - d) * 2 * B + other) * R
        allowed = mask_of(k, key_start, diagonal)
        for h in range(KV):
            kv = kvw[d, other, k, h]
            scores = dot(kv, q_t[k, h])
            probs = jnp.where(allowed, jnp.exp2(scores * EXP2_SCALE - rows_of[k, h, 0:1]), 0.0)
            grad = dot(kv, do_t[k, h])
            grad_scores = (probs * (grad - rows_of[k, h, 1:2])).astype(BF16)
            kvw[d, other, k, h] = (dot(grad_scores, q_rows[k, h]) + dot(probs.astype(BF16), do_rows[k, h])).astype(BF16)
            dq[k, h] += dot(jnp.transpose(kv)[0:64], grad_scores)

    def back_plane(k, d, *scratch):
        if d == 0:
            back_block(k, 0, place, *scratch, diagonal=True)
        low, high = attended(d)
        def step(other, _):
            back_block(k, d, other, *scratch)
            return 0
        lax.fori_loop(low, high, step, 0)
        keys_core(d, k)

    def back_finish(k, dq):
        cos, sin = aux[k, 0:32], aux[k, 32:64]
        for h in range(KV):
            e = (dq[k, h] * (1.0 / math.sqrt(HEAD))).astype(BF16).astype(F32)
            e = rotate_back(jnp.stack([e[:, 0:R], e[:, R:2 * R]]), cos, sin)
            gain_part, grad = rms_back(raws[k, h, 0:128].reshape(2, HEAD, R), e, r.gain_columns[0:64, 0:1])
            head_sums[0:64] += gain_part
            graw[h, k * R:(k + 1) * R, 0:128] = jnp.transpose(grad.reshape(128, R)).astype(BF16)

    def keys_back(k):
        cos, sin = aux[k, 0:32], aux[k, 32:64]
        for h in range(KV):
            final = jnp.transpose(kvw[0, place, k, h].astype(F32))
            e = rotate_back(final[0:64].reshape(1, HEAD, R), cos, sin)
            gain_part, grad = rms_back(raws[k, h, 128:192].reshape(1, HEAD, R), e, r.gain_columns[64:128, 0:1])
            head_sums[64:128] += gain_part
            both = jnp.concatenate([grad.reshape(HEAD, R), final[64:128]], axis=0)
            graw[h, k * R:(k + 1) * R, 128:256] = jnp.transpose(both).astype(BF16)

    xg = r.xg

    def input_gradient(k):
        for aa in range(A):
            columns = slice(aa * (D // A), (aa + 1) * (D // A))
            total = jnp.zeros((R, D // A), F32)
            for h in range(KV):
                total += nt_dot(graw[h, k * R:(k + 1) * R], weight_rows(p.qkv + h, aa))
            store_part(k, y_send, part, aa, total)
            x = x_all[k, :, columns].astype(F32)
            xg[:, columns] += jnp.sum(total * x * x_scale(k), axis=0, keepdims=True)

    def x_scale(k):
        return r.x_scale[k, :, 0:1]

    def out_gradient():
        for t in range(p.no):
            for aa in range(A):
                rows = slice(aa * (D // A), (aa + 1) * (D // A))
                total = jnp.zeros((D // A, TILE), F32)
                for k in range(G):
                    total += dot(r.gb_t[rows, k * R:(k + 1) * R], mixed[k, :, t * TILE:(t + 1) * TILE])
                wall[p.out + t, aa // 2, aa % 2] = total.astype(BF16).reshape(B, 2, S, TILE)
        step_core(p.ff_batches)

    def qkv_gradient(n):
        t, m = p.batches[n]
        for tile in range(t, t + m):
            for aa in range(A):
                rows = slice(aa * (D // A), (aa + 1) * (D // A))
                wall[tile, aa // 2, aa % 2] = dot(n_t[rows], graw[tile - p.qkv]).astype(BF16).reshape(B, 2, S, TILE)
        step_core(n)

    def branch_arrives(k):
        gathered(AG_GB, gb_all, k).wait_recv()
        scatter(RS_FO, fo_send, fo_recv, k).start()
        for piece in range(R // 128):
            rows = pl.ds(piece * 128, 128)
            r.gb_t[:, k * R + piece * 128:k * R + (piece + 1) * 128] = jnp.transpose(gb_all[k, rows].astype(F32)).astype(BF16)

    def keys_over_columns(k, d):
        keys_columns(d, k)
        if d == 2:
            keys_plane(2, k)

    def keys_over_planes(k, d):
        keys_from_plane(d, k)
        if d == 2:
            keys_plane(1, k)
        else:
            keys_back(k)

    def input_step(k):
        if k:
            scatter(RS_GN2, y_send, y_recv, k).wait_send()
        input_gradient(k)
        if k:
            scatter(RS_GN, y_send, y_recv, k).start()

    g_land, g_sems = r.g_land, r.g_sems
    stages = [
        (2, c, 0, lambda j: at(a, b, j)),
        (G, f, 2, lambda j: (i, j)),
        (B, b, 2 + G, lambda j: at(a, j, c)),
        (A, a, 2 + G + B, lambda j: at(j, b, c)),
    ]

    def gains_out():
        return pltpu.make_async_copy(gains, r.d_gains, local_sems.at[2])

    def gain_send(s, shift):
        size, mine, base, device = stages[s]
        return remote(gains, g_land.at[base + mine], g_sems.at[0, s, shift], g_sems.at[1, s, shift], device(lax.rem(mine + shift, size)))

    def gain_arrival(s, shift):
        size, mine, base, device = stages[s]
        slot = lax.rem(mine + size - shift, size)
        return remote(gains, g_land.at[base + slot], g_sems.at[0, s, shift], g_sems.at[1, s, shift], device(slot))

    def gain_start(s):
        size, mine, base, _ = stages[s]
        for shift in range(1, size):
            gain_send(s, shift).start()
        g_land[base + mine] = gains[...]

    def gain_finish(s):
        size, _, base, _ = stages[s]
        for shift in range(1, size):
            gain_arrival(s, shift).wait_recv()
            gain_send(s, shift).wait_send()
        total = g_land[base]
        for j in range(1, size):
            total += g_land[base + j]
        gains[...] = total
        if s == len(stages) - 1:
            gains_out().start()

    def gain_first(s):
        if s == 0:
            gains[1:2] = xg[...]
            gains[2:3, 0:128] = jnp.sum(jnp.transpose(head_sums[...]), axis=0, keepdims=True)
        gain_start(s)

    def rows_out(j):
        source, target = ((r.block_rows, r.block_out), (r.grad_rows, r.grad_inputs))[j]
        return pltpu.make_async_copy(source, target.at[0], local_sems.at[6 + j])

    def block_rows():
        for k in others:
            scattered(RS_FO, fo_send, fo_recv, k).wait_recv()
        for piece in range(R // 128):
            rows = pl.ds(piece * 128, 128)
            v = out_acc[rows]
            for k in others:
                v += fo_recv[k - 1, rows].astype(F32)
            r.block_rows[rows] = v.astype(BF16)

        rows_out(0).start()

    def input_rows():
        for k in range(G):
            keys_sent(k)
            heads_out(k).wait_send()
        for k in others:
            gather(AG_DY, dy_all, k).wait_send()
            gather(AG_GB, gb_all, k).wait_send()
            scatter(RS_FO, fo_send, fo_recv, k).wait_send()
            scatter(RS_GN, y_send, y_recv, k).wait_send()
        for k in others:
            scattered(RS_GN, y_send, y_recv, k).wait_recv()
        for piece in range(R // 128):
            rows = pl.ds(piece * 128, 128)
            e = part[rows]
            for k in others:
                e += y_recv[k - 1, rows].astype(F32)
            v = x_all[0, rows].astype(F32)
            rr = r.x_scale[0, rows, 0:1]
            vh = v * rr
            ge = e * r.gain_one[...]
            back = rr * (ge - vh * jnp.mean(vh * ge, axis=1, keepdims=True))
            r.grad_rows[rows] = (middle[rows] + back).astype(BF16)

        rows_out(1).start()

    def backward_scope(do_t, do_rows, q_rows, dq, rows_of, kv_stage, kv_sems, gb_t):
        r.gb_t = gb_t
        scratch = (do_t, do_rows, q_rows, dq, rows_of)
        steps = {
            GM: middle_gradient, BS: lambda k: back_start(k, *scratch), BP: lambda k, d: back_plane(k, d, *scratch),
            GB: branch_arrives, KA: lambda k, d: keys_add(d, k, kv_stage, kv_sems), KX: keys_over_columns, KZ: keys_over_planes,
            BF: lambda k: back_finish(k, dq), DWO: out_gradient, DWQ: qkv_gradient, IG: input_step, GS: gain_first,
            GF: gain_finish, BO: block_rows, GX: input_rows,
        }
        run(p.order_backward, steps)

    xg[...] = jnp.zeros((1, D), F32)
    for k in range(G):
        x = x_all[k].astype(F32)
        r.x_scale[k] = jnp.broadcast_to(lax.rsqrt(jnp.mean(x * x, axis=1, keepdims=True) + EPS), (R, 128))
    pl.run_scoped(
        backward_scope,
        pltpu.VMEM((G, KV, 128, 2 * R), BF16),
        pltpu.VMEM((G, KV, 2 * R, 128), BF16),
        pltpu.VMEM((G, KV, 2 * R, 128), BF16),
        pltpu.VMEM((G, KV, 64, 2 * R), F32),
        pltpu.VMEM((G, KV, 8, 2 * R), F32),
        pltpu.VMEM((B, KV, R, 128), BF16),
        pltpu.SemaphoreType.DMA((B,)),
        pltpu.VMEM((D, G * R), BF16),
    )
    for n in out_order:
        out_copy(n).wait()
    for j in range(2):
        rows_out(j).wait()
    gains_out().wait()

    for n in range(len(p.batches)):
        sum_third(n).wait_send()


def local(p, x, dy, lengths, gain_one, gain_two, query_gain, key_gain, wq, wk, wv, wo, wg, wu, wd):
    A, B, G, R, D, KV, S = p.A, p.B, p.G, p.R, p.D, p.KV, p.S
    any_spec, vmem, smem = (pl.BlockSpec(memory_space=m) for m in (pl.ANY, pltpu.VMEM, pltpu.SMEM))
    ins = dict(
        x=(x, any_spec), dy=(dy, any_spec), lengths=(lengths, smem), gain_one=(gain_one[None], vmem),
        gain_two=(gain_two[None], vmem), query_gain=(query_gain[None], vmem), key_gain=(key_gain[None], vmem),
        w_query=(wq, any_spec), w_key=(wk, any_spec), w_value=(wv, any_spec), w_out=(wo, any_spec),
        w_gate=(wg, any_spec), w_up=(wu, any_spec), w_down=(wd, any_spec),
    )
    rows_out = ((1, R, D), BF16)
    landing = dict(
        block_out=rows_out, grad_inputs=rows_out, d_gains=((8, D), F32),
        d_weights=((p.tiles, S, TILE), F32), rc=((p.tiles, 2, 2, B, S, TILE), BF16), kvr=((WINDOW, B, G, KV, R, 128), BF16),
    )
    DMA = pltpu.SemaphoreType.DMA
    n_batches, widest = len(p.batches), max(m for _, m in p.batches)
    scratch = dict(
        x_all=pltpu.VMEM((G, R, D), BF16), aux=pltpu.VMEM((G, 72, R), F32), dy_all=pltpu.VMEM((G, R, D), BF16),
        y_sems=DMA((8, 2, G)), x_sems_y=DMA((2, G, 2)), local_sems=DMA((8,)),
        gain_columns=pltpu.VMEM((128, 128), F32),
        kvw=pltpu.VMEM((WINDOW, 2 * B, G, KV, R, 128), BF16),
        z_sems=DMA((2, 2, G, 2)), x_sems=DMA((2, WINDOW, B, G, 2)), c_sems=DMA((2, WINDOW, B, G, 2)),
        wall=pltpu.VMEM((p.tiles, 2, 2, B, 2, S, TILE), BF16),
        n_t=pltpu.VMEM((D, G * R), BF16),
        raws=pltpu.VMEM((G, KV, 192, R), F32), q_t=pltpu.VMEM((G, KV, 128, 2 * R), BF16),
        o_acc=pltpu.VMEM((G, KV, 80, 2 * R), F32), mixed=pltpu.VMEM((G, R, p.HQ), BF16),
        y_send=pltpu.VMEM((G - 1, R, D), BF16), y_recv=pltpu.VMEM((G - 1, R, D), BF16),
        fo_send=pltpu.VMEM((G - 1, R, D), BF16), fo_recv=pltpu.VMEM((G - 1, R, D), BF16),
        part=pltpu.VMEM((R, D), F32), out_acc=pltpu.VMEM((R, D), F32), middle=pltpu.VMEM((R, D), F32),
        n2_all=pltpu.VMEM((G, R, D), BF16), mixed_in=pltpu.VMEM((G, R, p.HQ), BF16), wo_other=pltpu.VMEM((p.no, 2, 2, B, 2, S, TILE), BF16),
        block_rows=pltpu.VMEM((R, D), BF16), grad_rows=pltpu.VMEM((R, D), BF16), gains=pltpu.VMEM((8, D), F32), xg=pltpu.VMEM((1, D), F32), x_scale=pltpu.VMEM((G, R, 128), F32),
        w_sems=DMA((2, 4, n_batches)), fetch_sems=DMA((2,)), stage_c=pltpu.VMEM((2, widest, 2, 2, B, S, TILE), BF16),
        r1=pltpu.VMEM((p.tiles, 2, 2, S, TILE), BF16), r2=pltpu.VMEM((p.tiles, 2, S, TILE), BF16),
        r3=pltpu.VMEM((p.tiles, S, TILE), BF16), out_stage=pltpu.VMEM((OUT_SLOTS, widest, S, TILE), F32), out_sems=DMA((OUT_SLOTS,)),
        dm=pltpu.VMEM((R, p.HQ), BF16), graw=pltpu.VMEM((KV, G * R, TILE), BF16),
        xr=pltpu.VMEM((WINDOW, B - 1, G, KV, R, 128), BF16), zr=pltpu.VMEM((2, G, KV, R, 128), BF16),
        kc_sems=DMA((2, WINDOW, B, G)), kx_sems=DMA((2, WINDOW, B, G)), kz_sems=DMA((2, 2, G)),
        head_sums=pltpu.VMEM((128, R), F32),
        g_land=pltpu.VMEM((2 + B + A + G, 8, D), F32), g_sems=DMA((2, 4, max(A, B, G, 2))),
    )
    out_specs = [any_spec for _ in landing]
    names = list(ins) + list(landing) + list(scratch)
    results = pl.pallas_call(
        functools.partial(kernel, p, names),
        out_shape=[jax.ShapeDtypeStruct(*o) for o in landing.values()],
        in_specs=[s for _, s in ins.values()],
        out_specs=out_specs,
        scratch_shapes=list(scratch.values()),
        compiler_params=pltpu.CompilerParams(collective_id=0, has_side_effects=True, vmem_limit_bytes=64 << 20),
        name="block",
    )(*[v for v, _ in ins.values()])
    o = dict(zip(landing, results))
    o = types.SimpleNamespace(**o)
    packed = [o.block_out, o.grad_inputs, o.d_gains, o.d_weights]
    shapes = [(packed[0].shape, BF16), (packed[0].shape, BF16), ((D,), F32), ((D,), F32), ((HEAD,), F32), ((HEAD,), F32)]
    shapes += [((S, n), F32) for n in (128 * KV, 64 * KV, 64 * KV, 128 * KV, p.FL, p.FL, p.FL)]
    rows = pl.BlockSpec((1, R // SPLIT_STEPS, D), lambda i: (0, i, 0))
    whole = [pl.BlockSpec(shape, lambda i: (0,)) for shape, _ in shapes[2:6]]
    return pl.pallas_call(
        functools.partial(split_kernel, p),
        grid=(SPLIT_STEPS,),
        out_shape=[jax.ShapeDtypeStruct(*shape) for shape in shapes],
        in_specs=[
            rows, rows, pl.BlockSpec((8, D), lambda i: (0, 0)),
            pl.BlockSpec((p.tiles, S // SPLIT_STEPS, TILE), lambda i: (0, i, 0)),
        ],
        out_specs=[rows, rows] + whole + [
            pl.BlockSpec((S // SPLIT_STEPS, shape[1]), lambda i: (i, 0)) for shape, _ in shapes[6:]
        ],
        name="split",
    )(*packed)


def split_kernel(p, out_in, grad_in, gains, tiles, block_out, grad_inputs, g_one, g_two, g_query, g_key, d_query, d_key, d_value, d_out, d_gate, d_up, d_down):
    block_out[...] = out_in[...]
    grad_inputs[...] = grad_in[...]
    g_one[...] = gains[1]
    g_two[...] = gains[0]
    g_query[...] = gains[2, 0:HEAD]
    g_key[...] = gains[2, HEAD:2 * HEAD]
    for ref, first, count in ((d_gate, p.gate, p.nt), (d_up, p.up, p.nt), (d_down, p.down, p.nt), (d_out, p.out, p.no)):
        for t in range(count):
            ref[:, t * TILE:(t + 1) * TILE] = tiles[first + t]
    for h in range(p.KV):
        tile = tiles[p.qkv + h]
        d_query[:, 128 * h:128 * h + 128] = tile[:, 0:128]
        d_key[:, 64 * h:64 * h + 64] = tile[:, 128:192]
        d_value[:, 64 * h:64 * h + 64] = tile[:, 192:256]


QUERY_HEADS = 16
KEY_VALUE_HEADS = 8
HEAD_SIZE = HEAD


MASKED_FILL = -1e30


def swapped(value, axis, bit):
    mask = 2**bit
    pairs = [(source, source ^ mask) for source in range(lax.axis_size(axis))]
    return lax.ppermute(value, axis, pairs)


def root_mean_norm(values, gain):
    return values * lax.rsqrt(jnp.mean(values * values, axis=-1, keepdims=True) + EPS) * gain


def apply_rotary(values, cosine_table, sine_table):
    half_width = values.shape[-1] // 2
    turned = jnp.concatenate([-values[..., half_width:], values[..., :half_width]], axis=-1)
    return values * cosine_table + turned * sine_table


def places(lengths, where):
    ends = jnp.cumsum(lengths)
    before = (ends[None, :] <= where[:, None]).astype(jnp.int32)
    segment = jnp.sum(before, axis=1)
    offset = where - jnp.sum(before * lengths[None, :], axis=1)
    return (segment, offset)


def head_post(query_raw, unrotated_key, query_gain, key_norm_gain, cosine_table, sine_table):
    token_count = query_raw.shape[0]
    query_rot = apply_rotary(
        root_mean_norm(query_raw.reshape(token_count, QUERY_HEADS, HEAD_SIZE), query_gain),
        cosine_table,
        sine_table,
    )
    rotated_key = apply_rotary(
        root_mean_norm(
            unrotated_key.reshape(token_count, KEY_VALUE_HEADS, HEAD_SIZE), key_norm_gain
        ),
        cosine_table,
        sine_table,
    )
    return (query_rot, rotated_key)


def swiglu(gate, upward):
    return jax.nn.silu(gate) * upward


def matmul(left, right):
    return jnp.dot(left, right, preferred_element_type=jnp.float32)


def project_back(left, right):
    return lax.dot_general(
        left, right, (((1,), (1,)), ((), ())), preferred_element_type=jnp.float32
    )


def outer_sum(left, right):
    return lax.dot_general(
        left, right, (((0,), (0,)), ((), ())), preferred_element_type=jnp.float32
    )


def mirror_out(payload, steps):
    for bit in range(steps):
        payload = swapped(payload, "ctx", bit)
    return payload


def mirror_back(payload, steps):
    for bit in range(steps):
        payload = swapped(payload, "ctx", bit)
    return payload


def halves_order(array, parts):
    shaped = array.reshape((parts, 2, array.shape[0] // (2 * parts)) + array.shape[1:])
    return jnp.stack([shaped[:, 0], shaped[::-1, 1]], axis=1).reshape(array.shape)


def general(
    inputs,
    cotangent,
    lengths,
    gain_one,
    gain_two,
    query_gain,
    key_norm_gain,
    w_query,
    key_projection,
    value_projection,
    w_out,
    w_gate,
    w_up,
    w_down,
):
    brain_float = jnp.bfloat16
    parts = lax.axis_size("ctx")
    steps = parts.bit_length() - 1
    device_index = lax.axis_index("ctx")
    row_count = inputs.shape[1]
    head_group = row_count * parts
    half_width = row_count // 2
    own_lengths = lengths[0]
    offsets_half = jnp.arange(half_width, dtype=jnp.int32)
    arrived = mirror_out(jnp.stack([inputs[0][half_width:], cotangent[0][half_width:]]), steps)
    x_rows = jnp.concatenate([inputs[0][:half_width], arrived[0]], axis=0)
    dy_rows = jnp.concatenate([cotangent[0][:half_width], arrived[1]], axis=0)
    query_place = jnp.concatenate(
        [
            device_index * row_count + offsets_half,
            (parts - 1 - device_index) * row_count + half_width + offsets_half,
        ]
    )
    key_place = jnp.arange(head_group, dtype=jnp.int32)
    query_segment, query_offset = places(own_lengths, query_place)
    key_segment, key_offset = places(own_lengths, key_place)
    weight_query, weight_key, weight_value, weight_out = (
        lax.all_gather(w_query.astype(brain_float), "fsdp", axis=1, tiled=True),
        lax.all_gather(key_projection.astype(brain_float), "fsdp", axis=1, tiled=True),
        lax.all_gather(value_projection.astype(brain_float), "fsdp", axis=1, tiled=True),
        lax.all_gather(w_out.astype(brain_float), "fsdp", axis=1, tiled=True),
    )
    x_float = x_rows.astype(jnp.float32)
    normed_f, norm_one_back = jax.vjp(root_mean_norm, x_float, gain_one)
    normed_input = normed_f.astype(brain_float)
    query_raw = matmul(normed_input, weight_query)
    unrotated_key = matmul(normed_input, weight_key)
    value_b = matmul(normed_input, weight_value).astype(brain_float)
    freq = jnp.exp(
        jnp.arange(HEAD_SIZE // 2, dtype=jnp.float32) * (-2.0 * math.log(THETA) / HEAD_SIZE)
    )
    angle = query_offset.astype(jnp.float32)[:, None] * freq[None, :]
    cosine_table = jnp.concatenate([jnp.cos(angle), jnp.cos(angle)], axis=-1)[:, None, :]
    sine_table = jnp.concatenate([jnp.sin(angle), jnp.sin(angle)], axis=-1)[:, None, :]

    def post_local(query_in, key_in, gain_q, gain_k):
        return head_post(query_in, key_in, gain_q, gain_k, cosine_table, sine_table)

    (query_rot, rotated_key), post_back = jax.vjp(
        post_local, query_raw, unrotated_key, query_gain, key_norm_gain
    )
    query_batch = query_rot.astype(brain_float)
    key_batch = rotated_key.astype(brain_float).reshape(row_count, KEY_VALUE_HEADS * HEAD_SIZE)
    gathered_keys, gathered_values = (
        lax.all_gather(key_batch, "ctx", axis=0, tiled=True),
        lax.all_gather(value_b, "ctx", axis=0, tiled=True),
    )
    gathered_keys = halves_order(gathered_keys, parts)
    gathered_values = halves_order(gathered_values, parts)
    shared_heads = QUERY_HEADS // KEY_VALUE_HEADS
    score_scale = 1.0 / math.sqrt(HEAD_SIZE)
    keys_per_block = min(1024, head_group)
    block_count = head_group // keys_per_block
    query_quad = query_batch.reshape(row_count, KEY_VALUE_HEADS, shared_heads, HEAD_SIZE)
    blocked_keys = gathered_keys.reshape(block_count, keys_per_block, KEY_VALUE_HEADS, HEAD_SIZE)
    blocked_values = gathered_values.reshape(
        block_count, keys_per_block, KEY_VALUE_HEADS, HEAD_SIZE
    )
    segment_blocks = key_segment.reshape(block_count, keys_per_block)
    place_blocks = key_place.reshape(block_count, keys_per_block)

    def tile_backward(query_tile, tile_segment, tile_place, tile_log, grad_tile, tile_delta):

        def allowed_of(segment_block, place_block):
            return (tile_segment[:, None] == segment_block[None, :]) & (
                tile_place[:, None] >= place_block[None, :]
            )

        def back_step(carry, block):
            key_block, value_block, segment_block, place_block = block
            allowed = allowed_of(segment_block, place_block)

            def back_active(grad_query):
                raw_scores = (
                    jnp.einsum(
                        "qhgd,khd->hgqk", query_tile, key_block, preferred_element_type=jnp.float32
                    )
                    * score_scale
                )
                probs = jnp.exp(
                    jnp.where(allowed[None, None], raw_scores, MASKED_FILL) - tile_log[..., None]
                )
                grad_probs = jnp.einsum(
                    "qhgd,khd->hgqk", grad_tile, value_block, preferred_element_type=jnp.float32
                )
                grad_scores = (probs * (grad_probs - tile_delta[..., None])).astype(brain_float)
                grad_query = grad_query + jnp.einsum(
                    "hgqk,khd->qhgd", grad_scores, key_block, preferred_element_type=jnp.float32
                )
                grad_key_block = jnp.einsum(
                    "hgqk,qhgd->khd", grad_scores, query_tile, preferred_element_type=jnp.float32
                )
                grad_value_block = jnp.einsum(
                    "hgqk,qhgd->khd",
                    probs.astype(brain_float),
                    grad_tile,
                    preferred_element_type=jnp.float32,
                )
                return (grad_query, (grad_key_block, grad_value_block))

            def skipped(grad_query):
                empty_result = jnp.zeros((keys_per_block, KEY_VALUE_HEADS, HEAD_SIZE), jnp.float32)
                return (grad_query, (empty_result, empty_result))

            return lax.cond(jnp.any(allowed), back_active, skipped, carry)

        initial_gradient = jnp.zeros(
            (half_width, KEY_VALUE_HEADS, shared_heads, HEAD_SIZE), jnp.float32
        )
        return lax.scan(
            back_step,
            initial_gradient,
            (blocked_keys, blocked_values, segment_blocks, place_blocks),
        )

    heads_list = []
    extra_list = []
    log_list = []
    for tile in range(2):
        rows_tile = slice(tile * half_width, (tile + 1) * half_width)
        tile_query_tile = query_quad[rows_tile]
        tile_tile_segment = query_segment[rows_tile]
        tile_tile_place = query_place[rows_tile]

        def tile_allowed_of(segment_block, place_block):
            return (tile_tile_segment[:, None] == segment_block[None, :]) & (
                tile_tile_place[:, None] >= place_block[None, :]
            )

        def scores_of(key_block, allowed):
            raw_scores = (
                jnp.einsum(
                    "qhgd,khd->hgqk", tile_query_tile, key_block, preferred_element_type=jnp.float32
                )
                * score_scale
            )
            return jnp.where(allowed[None, None], raw_scores, MASKED_FILL)

        def stats_step(carry, block):
            key_block, segment_block, place_block = block
            allowed = tile_allowed_of(segment_block, place_block)

            def stats_active(state):
                peak, total = state
                scores = scores_of(key_block, allowed)
                newest = jnp.maximum(peak, jnp.max(scores, axis=-1))
                total = total * jnp.exp(peak - newest) + jnp.sum(
                    jnp.exp(scores - newest[..., None]), axis=-1
                )
                return (newest, total)

            return (lax.cond(jnp.any(allowed), stats_active, lambda state: state, carry), None)

        initial_peak = jnp.full(
            (KEY_VALUE_HEADS, shared_heads, half_width), MASKED_FILL, jnp.float32
        )
        initial_total = jnp.zeros((KEY_VALUE_HEADS, shared_heads, half_width), jnp.float32)
        (peak, total), unused = lax.scan(
            stats_step, (initial_peak, initial_total), (blocked_keys, segment_blocks, place_blocks)
        )
        tile_tile_log = peak + jnp.log(total)

        def output_step(carry, block):
            key_block, value_block, segment_block, place_block = block
            allowed = tile_allowed_of(segment_block, place_block)

            def output_active(state):
                upper, lower = state
                probs = jnp.exp(scores_of(key_block, allowed) - tile_tile_log[..., None])
                probs_high = probs.astype(brain_float)
                probs_low = (probs - probs_high.astype(jnp.float32)).astype(brain_float)
                upper = upper + jnp.einsum(
                    "hgqk,khd->qhgd", probs_high, value_block, preferred_element_type=jnp.float32
                )
                lower = lower + jnp.einsum(
                    "hgqk,khd->qhgd", probs_low, value_block, preferred_element_type=jnp.float32
                )
                return (upper, lower)

            return (lax.cond(jnp.any(allowed), output_active, lambda state: state, carry), None)

        initial_accumulator = jnp.zeros(
            (half_width, KEY_VALUE_HEADS, shared_heads, HEAD_SIZE), jnp.float32
        )
        (tile_heads, tile_extra), unused = lax.scan(
            output_step,
            (initial_accumulator, initial_accumulator),
            (blocked_keys, blocked_values, segment_blocks, place_blocks),
        )
        tile_heads, tile_extra, tile_log = (tile_heads, tile_extra, tile_tile_log)
        heads_list.append(tile_heads)
        extra_list.append(tile_extra)
        log_list.append(tile_log)
    heads_four = jnp.concatenate(heads_list, axis=0)
    heads_extra = jnp.concatenate(extra_list, axis=0)
    mixed = heads_four.reshape(row_count, QUERY_HEADS * HEAD_SIZE).astype(brain_float)
    middle = x_float + project_back(mixed, weight_out)
    normed_two_f, norm_two_back = jax.vjp(root_mean_norm, middle, gain_two)
    normed_two = normed_two_f.astype(brain_float)
    weight_gate, weight_up, weight_down = (
        lax.all_gather(w_gate.astype(brain_float), "fsdp", axis=1, tiled=True),
        lax.all_gather(w_up.astype(brain_float), "fsdp", axis=1, tiled=True),
        lax.all_gather(w_down.astype(brain_float), "fsdp", axis=1, tiled=True),
    )
    gate = matmul(normed_two, weight_gate)
    upward = matmul(normed_two, weight_up)
    hidden_f, swiglu_back = jax.vjp(swiglu, gate, upward)
    hidden = hidden_f.astype(brain_float)
    ffn_out = project_back(hidden, weight_down)
    grad_gate_f, grad_up_f = swiglu_back(matmul(dy_rows, weight_down))
    grad_gate = grad_gate_f.astype(brain_float)
    grad_up = grad_up_f.astype(brain_float)
    grad_normed_two = project_back(grad_gate, weight_gate) + project_back(grad_up, weight_up)
    grad_gate_weight = outer_sum(normed_two, grad_gate)
    grad_up_weight = outer_sum(normed_two, grad_up)
    grad_down_weight = outer_sum(dy_rows, hidden)
    grad_middle_norm, grad_gain_two = norm_two_back(grad_normed_two)
    grad_middle = dy_rows.astype(jnp.float32) + grad_middle_norm
    grad_branch = grad_middle.astype(brain_float)
    grad_out_weight = outer_sum(grad_branch, mixed)
    mixed_gradient = matmul(grad_branch, weight_out).astype(brain_float)
    mixed_gradient_quad = mixed_gradient.reshape(
        row_count, KEY_VALUE_HEADS, shared_heads, HEAD_SIZE
    )
    exact_heads = heads_four + heads_extra
    delta = jnp.sum(mixed_gradient_quad.astype(jnp.float32) * exact_heads, axis=-1).transpose(
        1, 2, 0
    )
    grad_query_list = []
    all_key_gradients = jnp.zeros((head_group, KEY_VALUE_HEADS * HEAD_SIZE), jnp.float32)
    all_value_gradients = jnp.zeros((head_group, KEY_VALUE_HEADS * HEAD_SIZE), jnp.float32)
    for tile in range(2):
        rows_tile = slice(tile * half_width, (tile + 1) * half_width)
        tile_grad_query, (key_block_gradients, value_block_gradients) = tile_backward(
            query_quad[rows_tile],
            query_segment[rows_tile],
            query_place[rows_tile],
            log_list[tile],
            mixed_gradient_quad[rows_tile],
            delta[:, :, rows_tile],
        )
        grad_query_list.append(tile_grad_query)
        all_key_gradients = all_key_gradients + key_block_gradients.reshape(
            head_group, KEY_VALUE_HEADS * HEAD_SIZE
        )
        all_value_gradients = all_value_gradients + value_block_gradients.reshape(
            head_group, KEY_VALUE_HEADS * HEAD_SIZE
        )
    grad_query_four = jnp.concatenate(grad_query_list, axis=0)
    all_key_gradients = all_key_gradients * score_scale
    all_key_gradients = halves_order(all_key_gradients, parts)
    all_value_gradients = halves_order(all_value_gradients, parts)
    own_key_gradient, grad_value_own = (
        lax.psum_scatter(
            all_key_gradients.astype(jnp.bfloat16), "ctx", scatter_dimension=0, tiled=True
        ).astype(jnp.float32),
        lax.psum_scatter(
            all_value_gradients.astype(jnp.bfloat16), "ctx", scatter_dimension=0, tiled=True
        ).astype(jnp.float32),
    )
    rotated_key_gradient = (
        own_key_gradient.astype(brain_float)
        .astype(jnp.float32)
        .reshape(row_count, KEY_VALUE_HEADS, HEAD_SIZE)
    )
    grad_value = grad_value_own.astype(brain_float)
    grad_query_rot = (
        (grad_query_four * score_scale)
        .astype(brain_float)
        .astype(jnp.float32)
        .reshape(row_count, QUERY_HEADS, HEAD_SIZE)
    )
    grad_query_raw_f, grad_key_raw_f, grad_query_gain, grad_key_gain = post_back(
        (grad_query_rot, rotated_key_gradient)
    )
    grad_query_raw = grad_query_raw_f.astype(brain_float)
    grad_key_raw = grad_key_raw_f.astype(brain_float)
    grad_normed = (
        project_back(grad_query_raw, weight_query)
        + project_back(grad_key_raw, weight_key)
        + project_back(grad_value, weight_value)
    )
    grad_query_weight = outer_sum(normed_input, grad_query_raw)
    grad_key_weight = outer_sum(normed_input, grad_key_raw)
    grad_value_weight = outer_sum(normed_input, grad_value)
    grad_x_norm, grad_gain_one = norm_one_back(grad_normed)
    out_rows = (middle + ffn_out).astype(brain_float)
    grad_rows = (grad_middle + grad_x_norm).astype(brain_float)
    returned = mirror_back(jnp.stack([out_rows[half_width:], grad_rows[half_width:]]), steps)
    out_rows = jnp.concatenate([out_rows[:half_width], returned[0]], axis=0)
    grad_rows = jnp.concatenate([grad_rows[:half_width], returned[1]], axis=0)
    summed = (
        lax.psum_scatter(
            grad_query_weight.astype(jnp.bfloat16), "fsdp", scatter_dimension=1, tiled=True
        ).astype(jnp.float32),
        lax.psum_scatter(
            grad_key_weight.astype(jnp.bfloat16), "fsdp", scatter_dimension=1, tiled=True
        ).astype(jnp.float32),
        lax.psum_scatter(
            grad_value_weight.astype(jnp.bfloat16), "fsdp", scatter_dimension=1, tiled=True
        ).astype(jnp.float32),
        lax.psum_scatter(
            grad_out_weight.astype(jnp.bfloat16), "fsdp", scatter_dimension=1, tiled=True
        ).astype(jnp.float32),
        lax.psum_scatter(
            grad_gate_weight.astype(jnp.bfloat16), "fsdp", scatter_dimension=1, tiled=True
        ).astype(jnp.float32),
        lax.psum_scatter(
            grad_up_weight.astype(jnp.bfloat16), "fsdp", scatter_dimension=1, tiled=True
        ).astype(jnp.float32),
        lax.psum_scatter(
            grad_down_weight.astype(jnp.bfloat16), "fsdp", scatter_dimension=1, tiled=True
        ).astype(jnp.float32),
    )
    final_grads = (
        lax.psum_scatter(
            summed[0].astype(jnp.bfloat16), "ctx", scatter_dimension=0, tiled=True
        ).astype(jnp.float32),
        lax.psum_scatter(
            summed[1].astype(jnp.bfloat16), "ctx", scatter_dimension=0, tiled=True
        ).astype(jnp.float32),
        lax.psum_scatter(
            summed[2].astype(jnp.bfloat16), "ctx", scatter_dimension=0, tiled=True
        ).astype(jnp.float32),
        lax.psum_scatter(
            summed[3].astype(jnp.bfloat16), "ctx", scatter_dimension=0, tiled=True
        ).astype(jnp.float32),
        lax.psum_scatter(
            summed[4].astype(jnp.bfloat16), "ctx", scatter_dimension=0, tiled=True
        ).astype(jnp.float32),
        lax.psum_scatter(
            summed[5].astype(jnp.bfloat16), "ctx", scatter_dimension=0, tiled=True
        ).astype(jnp.float32),
        lax.psum_scatter(
            summed[6].astype(jnp.bfloat16), "ctx", scatter_dimension=0, tiled=True
        ).astype(jnp.float32),
    )
    gains_total = lax.psum(
        (grad_gain_one, grad_gain_two, grad_query_gain, grad_key_gain), ("ctx", "fsdp")
    )
    return (
        out_rows[None],
        grad_rows[None],
        gains_total[0],
        gains_total[1],
        gains_total[2],
        gains_total[3],
        final_grads[0],
        final_grads[1],
        final_grads[2],
        final_grads[3],
        final_grads[4],
        final_grads[5],
        final_grads[6],
    )


def solution(mesh):
    row, whole, split = P("fsdp", "ctx", None), P(), P(None, "fsdp")
    out_split = P("ctx", "fsdp")

    def step(x, dy, lengths, *rest):
        p = Plan(mesh.shape["ctx"], mesh.shape["fsdp"], x.shape[1], x.shape[2], rest[5].shape[1] // HEAD, rest[8].shape[1])
        p.nseq = lengths.shape[1]
        if not p.fits():
            return general(x, dy, lengths, *rest)
        return tuple(local(p, x, dy, lengths, *rest))

    return jax.shard_map(
        step, mesh=mesh,
        in_specs=(row, row, P("fsdp", None), whole, whole, whole, whole) + (split,) * 7,
        out_specs=(row, row, whole, whole, whole, whole) + (out_split,) * 7,
        check_vma=False,
    )
```
